32 devices in a mesh: dp: 16 (over z, y, x), tensor: 2 (over core).
Axes of the slice: x: 2, y: 2, z: 4, core: 2. Of those that a mesh axis runs over, the one named last changes fastest.
Arguments:
- queries: bfloat16 [4096, 4096], P('dp', 'tensor'), may hold values from -8 to 8
- neighbour_keys: bfloat16 [128, 128, 4096], P('dp', None, 'tensor'), may hold values from -8 to 8
- neighbour_values: bfloat16 [128, 128, 4096], P('dp', None, 'tensor'), may hold values from -6 to 6
- residual: bfloat16 [4096, 4096], P(('dp', 'tensor')), may hold values from -1.5 to 1.5
- out_weight: bfloat16 [4096, 4096], P('tensor', 'dp'), may hold values from -0.09375 to 0.09375
- drop_mask: int32 [4096, 4096], P(('dp', 'tensor')), may hold values 0 or 1
- norm_gain: float32 [4096], replicated, may hold values from 0.5 to 1.5
- norm_bias: float32 [4096], replicated, may hold values from -0.5 to 0.5
- neighbour_owner: int32 [64, 2], P('dp'), may hold values from 0 to 15, as said below
- neighbour_slot: int32 [64, 2], P('dp'), may hold values from 0 to 7, as said below
Outputs:
- residual_next: bfloat16 [4096, 4096], P(('dp', 'tensor'))
- layer_normed: bfloat16 [4096, 4096], P(('dp', 'tensor'))
The draws below stay inside these ranges and needn't reach their ends.
Inputs may be any that keep to these rules, and one draw needn't show every extreme that they name: `neighbour_owner`: the 8 neighbours of the blocks of one dp index are stored on 8 different devices. A device receives at most 12 of all blocks' neighbour requests, and some device exactly that many. `neighbour_slot`: several blocks may use the same stored row.
All inputs are finite; a program needn't handle non-finite values. No bound on the sum of `drop_mask` on one device may be relied on, other than what follows from the above.
Results may differ from the reference program's by a relative error of at most 0.017.
Values may be sent and summed in bfloat16 or wider, within the bound.
No kernel may reach another device: no remote copies, remote signals or barrier semaphores. Data moves between devices by JAX's collectives and lax.ppermute only.
A program may use at most 128 MiB of HBM per device.

```python
import jax
import jax.numpy as jnp
from jax import lax

D = 4096
HEADS = 32
HEAD = 128
SPAN = 64
NBR_LEN = 128
NBRS = 2
C_DEV = 4
OWN_CAP = 8
TOKENS = 4096
NCH = 64
NBR_SLOTS = 128
QK_WIDTH = 4096


def owner_layout(key):
    devices = NCH // C_DEV
    per_device = NBRS * C_DEV
    most = min(devices, per_device + per_device // 2)
    pair_count = devices // 2
    paired = jax.random.permutation(jax.random.fold_in(key, 11), devices)
    transfer = jax.random.randint(jax.random.fold_in(key, 12), (pair_count,), 0, most - per_device + 1)
    transfer = transfer.at[0].set(most - per_device)
    counts = jnp.full((devices,), per_device, jnp.int32)
    counts = counts.at[paired[0::2]].add(transfer).at[paired[1::2]].add(-transfer)
    ordering = jax.random.permutation(jax.random.fold_in(key, 13), devices)
    ordered = counts[ordering]
    run_ends = jnp.cumsum(ordered)
    run_starts = run_ends - ordered
    position = jnp.arange(devices * per_device, dtype=jnp.int32)
    run_index = jnp.sum((run_ends[None, :] <= position[:, None]).astype(jnp.int32), axis=1)
    owners = ordering[run_index]
    slots_at = (position - run_starts[run_index]) % OWN_CAP
    owners = owners.reshape(per_device, devices).T.reshape(NCH, NBRS)
    slots_at = slots_at.reshape(per_device, devices).T.reshape(NCH, NBRS)
    return (owners.astype(jnp.int32), slots_at.astype(jnp.int32))


def draw_neighbour_owner(key, part):
    layout = owner_layout(key)
    return layout[0]


def draw_neighbour_slot(key, part):
    layout = owner_layout(key)
    return layout[1]


def draw_queries(key, part):
    key = jax.random.fold_in(key, 4)
    drawn = jnp.clip(1.5 * jax.random.normal(jax.random.fold_in(key, 1), (TOKENS, HEADS * HEAD), jnp.float32), -7.0, 7.0)
    return drawn.astype(jnp.bfloat16)


def draw_neighbour_keys(key, part):
    key = jax.random.fold_in(key, 5)
    drawn = jnp.clip(jax.random.normal(jax.random.fold_in(key, 1), (NBR_SLOTS, NBR_LEN, HEADS * HEAD), jnp.float32), -7.0, 7.0)
    return drawn.astype(jnp.bfloat16)


def set_ends(values, stream_key, smallest, largest):
    spot = [jax.random.randint(jax.random.fold_in(stream_key, axis), (), 0, length) for axis, length in enumerate(values.shape)]
    longest = values.shape.index(max(values.shape))
    beside = spot[:longest] + [(spot[longest] + 1) % values.shape[longest]] + spot[longest + 1:]
    return values.at[tuple(spot)].set(smallest).at[tuple(beside)].set(largest)


def levels(own_key, dims, pieces, smallest, top_value):
    level = 1.0
    for axis_at, shards_of in pieces:
        heights = jax.random.uniform(jax.random.fold_in(jax.random.fold_in(own_key, 6), axis_at), (shards_of,), jnp.float32, smallest / len(pieces), top_value / len(pieces))
        level = level * jnp.repeat(jnp.exp(heights), dims[axis_at] // shards_of).reshape((-1,) + (1,) * (len(dims) - 1 - axis_at))
    return level


def normal_values(stream_key, shape, deviation, limit, cuts=(), kind=jnp.bfloat16):
    gain = levels(stream_key, shape, cuts, -0.22, 0.18) if cuts else 1.0
    result = jax.random.normal(stream_key, shape, jnp.float32) * deviation * gain
    return jnp.minimum(jnp.maximum(result, -limit), limit).astype(kind)


def setup_inputs(seed: int = 0) -> dict:
    splits = jax.random.split(jax.random.key(seed), 11)
    queries = draw_queries(jax.random.fold_in(splits[10], 71), 0)
    neighbour_keys = draw_neighbour_keys(jax.random.fold_in(splits[10], 71), 0)
    neighbour_values = normal_values(splits[2], (NBR_SLOTS, NBR_LEN, QK_WIDTH), 1.0, 6.0, ((0, 16), (2, 2)))
    residual = normal_values(splits[3], (TOKENS, D), 0.25, 1.5, ((0, 32),))
    out_weight = normal_values(splits[4], (QK_WIDTH, D), QK_WIDTH ** -0.5, 0.09375, ((0, 2), (1, 16)))
    drop_mask = set_ends((jax.random.randint(splits[5], (TOKENS, D), 0, 10) < 9).astype(jnp.int32), jax.random.fold_in(splits[5], 1), 0, 1)
    norm_gain = jnp.clip(1.0 + 0.1 * jax.random.normal(splits[6], (D,), jnp.float32), 0.5, 1.5)
    norm_bias = jnp.clip(jax.random.uniform(splits[7], (D,), jnp.float32, -0.5, 0.5), -0.5, 0.5)
    neighbour_owner = draw_neighbour_owner(jax.random.fold_in(splits[10], 71), 0)
    neighbour_slot = draw_neighbour_slot(jax.random.fold_in(splits[10], 71), 0)
    return {"queries": queries, "neighbour_keys": neighbour_keys, "neighbour_values": neighbour_values, "residual": residual, "out_weight": out_weight, "drop_mask": drop_mask, "norm_gain": norm_gain, "norm_bias": norm_bias, "neighbour_owner": neighbour_owner, "neighbour_slot": neighbour_slot}


keep_rate = 0.9
norm_eps = 1e-05

def attend_block(query_rows, key_rows, value_rows):
    count_b, count_r, row_width = query_rows.shape
    length = key_rows.shape[1]
    heads_here = row_width // HEAD
    query_heads = query_rows.reshape(count_b, count_r, heads_here, HEAD).astype(jnp.float32)
    key_heads = key_rows.reshape(count_b, length, heads_here, HEAD).astype(jnp.float32)
    value_heads = value_rows.reshape(count_b, length, heads_here, HEAD).astype(jnp.float32)
    scores = jnp.einsum('brhe,blhe->bhrl', query_heads, key_heads) * HEAD ** (-0.5)
    peak_rows = lax.optimization_barrier(jnp.max(scores, axis=-1))
    raised = jnp.exp(scores - peak_rows[..., None])
    totals = lax.optimization_barrier(jnp.sum(raised, axis=-1))
    weights = (raised / totals[..., None]).astype(jnp.bfloat16).astype(jnp.float32)
    partial_value = jnp.einsum('bhrl,blhe->brhe', weights, value_heads)
    partial_value = partial_value.astype(jnp.bfloat16).reshape(count_b, count_r, row_width)
    return (partial_value, jnp.transpose(peak_rows, (0, 2, 1)), jnp.transpose(totals, (0, 2, 1)))

def merge_pair(partials, peak_rows, totals):
    highest = lax.optimization_barrier(jnp.max(peak_rows, axis=1, keepdims=True))
    merge_weight = totals * jnp.exp(peak_rows - highest)
    weight_sum = lax.optimization_barrier(jnp.sum(merge_weight, axis=1))
    part_shape = partials.shape
    part_heads = partials.reshape(part_shape[0], part_shape[1], part_shape[2], -1, HEAD).astype(jnp.float32)
    combined = lax.optimization_barrier(jnp.sum(part_heads * merge_weight[..., None], axis=1)) / weight_sum[..., None]
    return combined.reshape(part_shape[0], part_shape[2], part_shape[3]).astype(jnp.bfloat16)

def reference(queries, neighbour_keys, neighbour_values, residual, out_weight, drop_mask, norm_gain, norm_bias, neighbour_owner, neighbour_slot):
    row_width = HEADS * HEAD
    shifted = jnp.concatenate([jnp.zeros((1, row_width), queries.dtype), queries[:-1]], axis=0)
    shifted = shifted.reshape(NCH, SPAN, row_width)
    store_index = (neighbour_owner * OWN_CAP + neighbour_slot).astype(jnp.int32)

    def one_block(block_items):
        block_rows, block_index = block_items
        gathered_keys = jnp.take(neighbour_keys, block_index, axis=0)
        gathered_values = jnp.take(neighbour_values, block_index, axis=0)
        repeated = jnp.broadcast_to(block_rows[None], (NBRS, SPAN, row_width))
        partial_value, peak_rows, totals = attend_block(repeated, gathered_keys, gathered_values)
        return merge_pair(partial_value[None], peak_rows[None], totals[None])[0]
    merged = lax.map(one_block, (shifted, store_index))
    flat_rows = merged.reshape(TOKENS, row_width)
    cross_rows = jnp.concatenate([flat_rows[1:], jnp.zeros((1, row_width), flat_rows.dtype)], axis=0)
    branch = jnp.dot(cross_rows, out_weight, preferred_element_type=jnp.float32)
    keep_scale = drop_mask.astype(jnp.float32) * (1.0 / keep_rate)
    stream = residual.astype(jnp.float32) + keep_scale * branch
    centre = lax.optimization_barrier(jnp.mean(stream, axis=1, keepdims=True))
    spread = lax.optimization_barrier(jnp.mean(jnp.square(stream - centre), axis=1, keepdims=True))
    normed = (stream - centre) * lax.rsqrt(spread + norm_eps) * norm_gain + norm_bias
    return (stream.astype(jnp.bfloat16), normed.astype(jnp.bfloat16))
```

```python
import functools

import jax
import jax.numpy as jnp
from jax import lax
from jax.experimental import pallas as pl
from jax.experimental.pallas import tpu as pltpu
from jax.sharding import PartitionSpec as P

HEAD = 128
LANES = 128
MIB = 1024 * 1024
ROW_TILE = 16
PLANE = 4

keep_rate = 0.9
norm_eps = 1e-05


def shifted(x, axis, by):
    count = lax.axis_size(axis)
    pairs = [(i, i + by) for i in range(count) if 0 <= i + by < count]
    return lax.ppermute(x, axis, pairs)


def spread_kernel(tagged, block_ref, slot_ref, carried_ref, *refs):
    *pieces, out_ref, moved, tags, sems = refs
    peers, span_len, _ = out_ref.shape
    rows, piece_width = pieces[0].shape
    row_width = moved.shape[1]
    at = 0
    for piece in pieces:
        for start in range(0, piece_width, 512):
            size = min(512, piece_width - start)
            held = piece[:, start : start + size].astype(jnp.float32)
            rolled = pltpu.roll(held, 1, 0)
            first = lax.broadcasted_iota(jnp.int32, (rows, size), 0) == 0
            above = carried_ref[0:1, at : at + size].astype(jnp.float32)
            moved[:, at : at + size] = jnp.where(first, above, rolled).astype(moved.dtype)
            at += size

    def copies(peer):
        start = pl.multiple_of(block_ref[peer] * span_len, span_len)
        yield pltpu.make_async_copy(
            moved.at[pl.ds(start, span_len)],
            out_ref.at[peer, :, pl.ds(0, row_width)],
            sems.at[0, peer],
        )
        if tagged:
            yield pltpu.make_async_copy(
                tags.at[peer], out_ref.at[peer, :, pl.ds(row_width, LANES)], sems.at[1, peer]
            )

    for peer in range(peers):
        if tagged:
            slot = slot_ref[peer].astype(jnp.float32)
            tags[peer] = jnp.full((span_len, LANES), slot, jnp.float32).astype(tags.dtype)
        for copy in copies(peer):
            copy.start()
    for peer in range(peers):
        for copy in copies(peer):
            copy.wait()


def spread(pieces, carried, block_of_peer, slot_of_peer, span_len, chunk, tagged):
    peers = block_of_peer.shape[0]
    rows, piece_width = pieces[0].shape
    row_width = piece_width * len(pieces)
    wide = row_width + (LANES if tagged else 0)
    return pl.pallas_call(
        functools.partial(spread_kernel, tagged),
        grid_spec=pltpu.PrefetchScalarGridSpec(
            num_scalar_prefetch=2,
            grid=(1,),
            in_specs=[pl.BlockSpec((1, row_width), lambda i, *_: (0, chunk))]
            + [pl.BlockSpec((rows, piece_width), lambda i, *_: (0, 0))] * len(pieces),
            out_specs=pl.BlockSpec(memory_space=pl.ANY),
            scratch_shapes=[
                pltpu.VMEM((rows, row_width), carried.dtype),
                pltpu.VMEM((peers, span_len, LANES), carried.dtype),
                pltpu.SemaphoreType.DMA((2, peers)),
            ],
        ),
        out_shape=jax.ShapeDtypeStruct((peers, span_len, wide), carried.dtype),
        compiler_params=pltpu.CompilerParams(vmem_limit_bytes=32 * MIB),
        name="spread_queries",
    )(block_of_peer, slot_of_peer, carried, *pieces)


def pack_levels(stats, heads):
    part = lax.broadcasted_iota(jnp.int32, stats.shape, 1) // heads
    high = stats.astype(jnp.bfloat16).astype(jnp.float32)
    rest = stats - high
    middle = rest.astype(jnp.bfloat16).astype(jnp.float32)
    low = rest - middle
    return jnp.where(part == 0, high, jnp.where(part == 1, middle, jnp.where(part == 2, low, 0.0)))


def unpack_levels(packed, heads):
    packed = packed.astype(jnp.float32)
    return (
        packed
        + pltpu.roll(packed, LANES - heads, 1)
        + pltpu.roll(packed, LANES - 2 * heads, 1)
    )


def attend_kernel(valid_ref, slot_ref, query_ref, key_ref, value_ref, out_ref):
    row_width = query_ref.shape[2]
    span_len = query_ref.shape[1]
    length = key_ref.shape[1]
    heads = row_width // HEAD
    group = min(heads, 4)
    peer = pl.program_id(0)

    @pl.when(valid_ref[peer] > 0)
    def _():
        lane = lax.broadcasted_iota(jnp.int32, (span_len, LANES), 1)
        stats = jnp.zeros((span_len, LANES), jnp.float32)
        ones = jnp.ones((length, HEAD), jnp.bfloat16)
        for first in range(0, heads, group):
            chosen = range(first, first + group)
            cuts = [slice(head * HEAD, (head + 1) * HEAD) for head in chosen]
            scores = [
                lax.dot_general(
                    query_ref[0, :, cut],
                    key_ref[0, :, cut],
                    (((1,), (1,)), ((), ())),
                    preferred_element_type=jnp.float32,
                )
                * HEAD ** (-0.5)
                for cut in cuts
            ]
            peaks = [jnp.max(score, axis=1, keepdims=True) for score in scores]
            raised = [
                jnp.exp(score - peak).astype(jnp.bfloat16) for score, peak in zip(scores, peaks)
            ]
            sums = [
                jnp.dot(
                    weight,
                    jnp.concatenate([value_ref[0, :, cut], ones], axis=1),
                    preferred_element_type=jnp.float32,
                )
                for weight, cut in zip(raised, cuts)
            ]
            for head, cut, peak, both in zip(chosen, cuts, peaks, sums):
                total = both[:, HEAD:]
                out_ref[0, :, cut] = (both[:, :HEAD] / total).astype(out_ref.dtype)
                stats = jnp.where(lane % heads == head, peak + jnp.log(total), stats)
        out_ref[0, :, row_width:] = pack_levels(stats, heads).astype(out_ref.dtype)


def attend(asked, keys, values, valid, slots, width, chunk, part):
    peers, span_len, _ = asked.shape
    length = keys.shape[1]
    heads = width // HEAD
    wide = width + LANES
    return pl.pallas_call(
        attend_kernel,
        grid_spec=pltpu.PrefetchScalarGridSpec(
            num_scalar_prefetch=2,
            grid=(peers,),
            in_specs=[
                pl.BlockSpec((1, span_len, width), lambda i, v, s: (i, 0, part)),
                pl.BlockSpec((1, length, width), lambda i, v, s: (s[i], 0, chunk)),
                pl.BlockSpec((1, length, width), lambda i, v, s: (s[i], 0, chunk)),
            ],
            out_specs=pl.BlockSpec((1, span_len, wide), lambda i, v, s: (i, 0, 0)),
        ),
        out_shape=jax.ShapeDtypeStruct((peers, span_len, wide), asked.dtype),
        compiler_params=pltpu.CompilerParams(vmem_limit_bytes=56 * MIB),
        cost_estimate=pl.CostEstimate(
            flops=4 * peers * heads * span_len * length * HEAD,
            bytes_accessed=2 * peers * width * (2 * span_len + 2 * length),
            transcendentals=peers * heads * span_len * length,
        ),
        name="attend_blocks",
    )(valid, slots, asked, keys, values)


def merge_block(uses, parts):
    row_width = parts[0].shape[2] - LANES
    heads = row_width // HEAD

    def masked(use, held, other):
        return held if use is None else jnp.where(use, held, other)

    levels = [
        masked(use, unpack_levels(ref[0, :, row_width:], heads), -1e30)
        for use, ref in zip(uses, parts)
    ]
    highest = functools.reduce(jnp.maximum, levels)
    weights = [jnp.exp(level - highest) for level in levels]
    total = functools.reduce(jnp.add, weights)
    weights = [weight / total for weight in weights]
    for head in range(heads):
        cut = slice(head * HEAD, (head + 1) * HEAD)
        merged = functools.reduce(
            jnp.add,
            [
                weight[:, head : head + 1]
                * masked(use, ref[0, :, cut].astype(jnp.float32), 0.0)
                for use, weight, ref in zip(uses, weights, parts)
            ],
        )
        yield cut, merged
    lane = lax.broadcasted_iota(jnp.int32, highest.shape, 1)
    level = jnp.where(lane < heads, highest + jnp.log(total), 0.0)
    level = level + pltpu.roll(level, heads, 1) + pltpu.roll(level, 2 * heads, 1)
    yield slice(row_width, row_width + LANES), pack_levels(level, heads)


def merge_far_kernel(picked, index_ref, use_ref, *refs):
    block = pl.program_id(0)
    uses = [use_ref[block * picked + r] > 0 for r in range(picked)]
    out_ref = refs[-1]
    for cut, merged in merge_block(uses, refs[:-1]):
        out_ref[0, :, cut] = merged.astype(out_ref.dtype)


def merge_all_kernel(picked, index_ref, use_ref, *refs):
    out_ref, kept = refs[-2:]
    parts = refs[:-2]
    span_len = parts[0].shape[1]
    rows, row_width = out_ref.shape
    rows -= ROW_TILE
    step = pl.program_id(0)
    block = rows // span_len - 1 - step
    uses = [use_ref[block * picked + r] > 0 for r in range(picked)] + [None]
    start = pl.multiple_of(block * span_len, span_len)
    last = lax.broadcasted_iota(jnp.int32, (span_len, HEAD), 0) == span_len - 1

    @pl.when(step == 0)
    def _():
        kept[...] = jnp.zeros_like(kept)

    for cut, merged in merge_block(uses, parts):
        if cut.start < row_width:
            moved = pltpu.roll(merged, span_len - 1, 0)
            moved = jnp.where(last, kept[0:1, cut], moved)
            out_ref[pl.ds(start, span_len), cut] = moved.astype(out_ref.dtype)
            kept[:, cut] = merged[:8]
            out_ref[rows:, cut] = merged[:ROW_TILE].astype(out_ref.dtype)


def merge_far(parts, index, use, blocks):
    _, span_len, wide = parts.shape
    picked = index.shape[0] // blocks
    specs = [
        pl.BlockSpec(
            (1, span_len, wide),
            functools.partial(lambda r, i, index, use: (index[i * picked + r], 0, 0), r),
        )
        for r in range(picked)
    ]
    return pl.pallas_call(
        functools.partial(merge_far_kernel, picked),
        grid_spec=pltpu.PrefetchScalarGridSpec(
            num_scalar_prefetch=2,
            grid=(blocks,),
            in_specs=specs,
            out_specs=pl.BlockSpec((1, span_len, wide), lambda i, *_: (i, 0, 0)),
        ),
        out_shape=jax.ShapeDtypeStruct((blocks, span_len, wide), parts.dtype),
        compiler_params=pltpu.CompilerParams(vmem_limit_bytes=32 * MIB),
        name="merge_far",
    )(index, use, *([parts] * picked))


def merge_all(parts, index, use, blocks, far):
    _, span_len, wide = parts.shape
    row_width = wide - LANES
    picked = index.shape[0] // blocks
    rows = blocks * span_len
    specs = [
        pl.BlockSpec(
            (1, span_len, wide),
            functools.partial(
                lambda r, i, index, use: (index[(blocks - 1 - i) * picked + r], 0, 0), r
            ),
        )
        for r in range(picked)
    ]
    specs.append(pl.BlockSpec((1, span_len, wide), lambda i, *_: (blocks - 1 - i, 0, 0)))
    return pl.pallas_call(
        functools.partial(merge_all_kernel, picked),
        grid_spec=pltpu.PrefetchScalarGridSpec(
            num_scalar_prefetch=2,
            grid=(blocks,),
            in_specs=specs,
            out_specs=pl.BlockSpec((rows + ROW_TILE, row_width), lambda i, *_: (0, 0)),
            scratch_shapes=[pltpu.VMEM((8, row_width), jnp.float32)],
        ),
        out_shape=jax.ShapeDtypeStruct((rows + ROW_TILE, row_width), parts.dtype),
        compiler_params=pltpu.CompilerParams(vmem_limit_bytes=32 * MIB),
        name="merge_all",
    )(index, use, *([parts] * picked), far)


def project_kernel(place_ref, stay_ref, *refs):
    *rest, keep_ref, send_ref, rows_ref, first_ref = refs
    sources, below_ref, weights = rest[: -PLANE - 1], rest[-PLANE - 1], rest[-PLANE:]
    half = keep_ref.shape[0]
    part = half // PLANE
    step = pl.program_id(0)

    @pl.when(step == 0)
    def _():
        for at, ref in enumerate(sources):
            member = place_ref[0] ^ (at % PLANE)
            width = ref.shape[1]
            cut = slice(at // PLANE * width, (at // PLANE + 1) * width)
            for side in range(2):
                to = pl.multiple_of(side * half + member * part, part)
                rows_ref[pl.ds(to, part), cut] = ref[side * part : (side + 1) * part]
            to = pl.multiple_of(member * ROW_TILE, ROW_TILE)
            first_ref[pl.ds(to, ROW_TILE), cut] = ref[2 * part :]
        shape = (ROW_TILE, rows_ref.shape[1])
        last = lax.broadcasted_iota(jnp.int32, shape, 0) == ROW_TILE - 1
        for member in range(PLANE):
            if member < PLANE - 1:
                at = (member + 1) * ROW_TILE
                below = first_ref[at : at + ROW_TILE].astype(jnp.float32)[0:1]
            else:
                below = below_ref[...].astype(jnp.float32)[0:1]
            end = half + (member + 1) * part
            held = rows_ref[end - ROW_TILE : end].astype(jnp.float32)
            rows_ref[end - ROW_TILE : end] = jnp.where(last, below, held).astype(rows_ref.dtype)

    stay = pl.multiple_of(stay_ref[0] * half, half)
    go = pl.multiple_of((1 - stay_ref[0]) * half, half)
    for at, weight_ref in enumerate(weights):

        @pl.when(step == at)
        def _():
            for start, ref in ((go, send_ref), (stay, keep_ref)):
                ref[...] = jnp.dot(
                    rows_ref[pl.ds(start, half)],
                    weight_ref[...],
                    preferred_element_type=jnp.float32,
                ).astype(ref.dtype)


def project(sources, below, weights, place, stay):
    height, width = sources[0].shape
    row_width = below.shape[1]
    rows = PLANE * (height - ROW_TILE)
    shards = len(weights)
    tile = weights[0].shape[1]
    columns = shards * tile
    half = rows // 2
    return pl.pallas_call(
        project_kernel,
        grid_spec=pltpu.PrefetchScalarGridSpec(
            num_scalar_prefetch=2,
            grid=(shards,),
            in_specs=[pl.BlockSpec((height, width), lambda i, *_: (0, 0))] * len(sources)
            + [pl.BlockSpec((1, row_width), lambda i, *_: (0, 0))]
            + [pl.BlockSpec((row_width, tile), lambda i, *_: (0, 0))] * shards,
            out_specs=[
                pl.BlockSpec((half, tile), lambda i, *_: (0, i)),
                pl.BlockSpec((half, tile), lambda i, *_: (0, i)),
            ],
            scratch_shapes=[
                pltpu.VMEM((rows, row_width), sources[0].dtype),
                pltpu.VMEM((PLANE * ROW_TILE, row_width), sources[0].dtype),
            ],
        ),
        out_shape=[jax.ShapeDtypeStruct((half, columns), sources[0].dtype)] * 2,
        compiler_params=pltpu.CompilerParams(vmem_limit_bytes=30 * MIB),
        name="project_rows",
    )(place, stay, *sources, below, *weights)


def add_kernel(place_ref, keep_ref, other_ref, *outs):
    for at, ref in enumerate(outs):
        member = place_ref[0] ^ at
        ref[...] = (
            keep_ref[member].astype(jnp.float32) + other_ref[member].astype(jnp.float32)
        ).astype(ref.dtype)


def add_cores(keep, other, place):
    half, columns = keep.shape
    part = half // PLANE
    tile = min(columns, 512)
    folded = (PLANE, part, columns)
    return pl.pallas_call(
        add_kernel,
        grid_spec=pltpu.PrefetchScalarGridSpec(
            num_scalar_prefetch=1,
            grid=(columns // tile,),
            in_specs=[pl.BlockSpec((PLANE, part, tile), lambda i, *_: (0, 0, i))] * 2,
            out_specs=[pl.BlockSpec((part, tile), lambda i, *_: (0, i))] * PLANE,
        ),
        out_shape=[jax.ShapeDtypeStruct((part, columns), keep.dtype)] * PLANE,
        compiler_params=pltpu.CompilerParams(vmem_limit_bytes=32 * MIB),
        name="add_cores",
    )(place, keep.reshape(folded), other.reshape(folded))


def norm_kernel(strip, place_ref, line_ref, *refs):
    branches = refs[:-7]
    residual_ref, mask_ref, gain_ref, bias_ref, next_ref, normed_ref, branch_ref = refs[-7:]
    if len(branches) == 1:
        branch_ref[...] = branches[0][...].astype(jnp.float32)
    else:
        for at, ref in enumerate(branches):
            member = place_ref[0] ^ at
            for shard in range(ref.shape[1] // strip):
                to = pl.multiple_of((line_ref[shard] * PLANE + member) * strip, strip)
                branch_ref[:, pl.ds(to, strip)] = ref[
                    :, shard * strip : (shard + 1) * strip
                ].astype(jnp.float32)
    keep_scale = mask_ref[...].astype(jnp.float32) * (1.0 / keep_rate)
    stream = residual_ref[...].astype(jnp.float32) + keep_scale * branch_ref[...]
    centre = jnp.mean(stream, axis=1, keepdims=True)
    moved = stream - centre
    spread_of = jnp.mean(jnp.square(moved), axis=1, keepdims=True)
    normed = moved * lax.rsqrt(spread_of + norm_eps) * gain_ref[...] + bias_ref[...]
    next_ref[...] = stream.astype(next_ref.dtype)
    normed_ref[...] = normed.astype(normed_ref.dtype)


def add_norm(place, line, branches, strip, residual, drop_mask, gain, bias):
    rows, columns = residual.shape
    tile = min(32, rows)
    row_spec = pl.BlockSpec((tile, columns), lambda i, *_: (i, 0))
    branch_spec = pl.BlockSpec((tile, branches[0].shape[1]), lambda i, *_: (i, 0))
    flat_spec = pl.BlockSpec((1, columns), lambda i, *_: (0, 0))
    return pl.pallas_call(
        functools.partial(norm_kernel, strip),
        grid_spec=pltpu.PrefetchScalarGridSpec(
            num_scalar_prefetch=2,
            grid=(rows // tile,),
            in_specs=[branch_spec] * len(branches) + [row_spec, row_spec, flat_spec, flat_spec],
            out_specs=[row_spec, row_spec],
            scratch_shapes=[pltpu.VMEM((tile, columns), jnp.float32)],
        ),
        out_shape=[jax.ShapeDtypeStruct((rows, columns), residual.dtype)] * 2,
        compiler_params=pltpu.CompilerParams(vmem_limit_bytes=32 * MIB),
        name="add_norm",
    )(place, line, *branches, residual, drop_mask, gain[None], bias[None])


def pick_requests(owners, slots, peers, per_block):
    selector = owners[None, :] == peers[:, None]
    pair_block = jnp.arange(owners.shape[0], dtype=jnp.int32) // per_block
    return (
        jnp.sum(jnp.where(selector, pair_block[None, :], 0), axis=1),
        jnp.sum(jnp.where(selector, slots[None, :] + 1, 0), axis=1),
    )


def within(owners, base, half):
    index = owners - base
    use = (index >= 0) & (index < half)
    return jnp.where(use, index, 0), use.astype(jnp.int32)


def local(
    queries,
    neighbour_keys,
    neighbour_values,
    residual,
    out_weight,
    drop_mask,
    norm_gain,
    norm_bias,
    neighbour_owner,
    neighbour_slot,
):
    peer_count = lax.axis_size("dp")
    side_count = lax.axis_size("tensor")
    half = peer_count // 2
    halves = [list(range(half)), list(range(half, peer_count))]
    across = [(i, (i + half) % peer_count) for i in range(peer_count)]
    by_plane = side_count == 2 and peer_count == 4 * PLANE
    blocks, per_block = neighbour_owner.shape
    rows, row_width = queries.shape
    span_len = rows // blocks
    here = lax.axis_index("dp").astype(jnp.int32)
    upper = here // half
    base = upper * half
    partner = lax.rem(here + half, peer_count)

    def exchange(x):
        return lax.all_to_all(
            x, "dp", split_axis=0, concat_axis=0, tiled=True, axis_index_groups=halves
        )

    def pinned(*values):
        return lax.optimization_barrier(values)

    def to_partner(x):
        return lax.ppermute(x, "dp", across)

    chunks = 2
    width = row_width // chunks
    far_first = to_partner(queries[:, :width])
    carried = shifted(queries[-1:], "dp", 1)
    owners = neighbour_owner.reshape(-1)
    slot_rows = neighbour_slot.reshape(-1)
    near_peers = base + jnp.arange(half, dtype=jnp.int32)
    near_out = spread(
        [queries], carried, *pick_requests(owners, slot_rows, near_peers, per_block),
        span_len, 0, True,
    )
    near_asked = exchange(near_out)
    far_carried = lax.ppermute(
        queries[-1:], "dp", [(i - 1, (i + half) % peer_count) for i in range(1, peer_count)]
    )
    requests = owners.shape[0]
    far_table = to_partner(
        jnp.pad(jnp.concatenate([owners, slot_rows]), (0, LANES - 2 * requests))[None, :]
    )
    far_first, far_carried, far_table, held_queries, _ = pinned(
        far_first, far_carried, far_table, queries, near_out
    )
    far_owners = far_table[0, :requests]
    far_picked = pick_requests(
        far_owners, far_table[0, requests : 2 * requests], near_peers, per_block
    )

    def slots_of(asked):
        return asked[:, 0, -LANES].astype(jnp.int32)

    def answer(asked, tags, chunk, part):
        valid = (tags > 0).astype(jnp.int32)
        slots = jnp.maximum(tags - 1, 0)
        return attend(
            asked, neighbour_keys, neighbour_values, valid, slots, width, chunk, part
        )

    far_second = to_partner(held_queries[:, width:])
    near_index, near_use = within(owners, base, half)
    far_index, far_use = within(far_owners, base, half)
    far_out = spread([far_first], far_carried, *far_picked, span_len, 0, True)
    far_asked = exchange(far_out)
    near_asked, _ = pinned(near_asked, far_out)
    near_tags = slots_of(near_asked)
    near_parts = [answer(near_asked, near_tags, chunk, chunk) for chunk in range(chunks)]
    far_asked, far_second, weight, *near_parts = pinned(
        far_asked, far_second, out_weight, *near_parts
    )

    middle = row_width // 2
    far_out = spread([far_second], far_carried, *far_picked, span_len, 1, False)
    next_asked = exchange(far_out)
    near_part, far_asked, _ = pinned(near_parts[0], far_asked, far_out)
    near_back = exchange(near_part)
    far_weight = [to_partner(weight[:middle])] if by_plane else []
    far_tags = slots_of(far_asked)
    far_parts = answer(far_asked, far_tags, 0, 0)
    far_parts, next_asked, near_back, near_part, weight, *far_weight = pinned(
        far_parts, next_asked, near_back, near_parts[1], weight, *far_weight
    )

    far_back = exchange(far_parts)
    next_back = exchange(near_part)
    if by_plane:
        far_weight.append(to_partner(weight[middle:]))
    far_parts = answer(next_asked, far_tags, 1, 0)
    far_back, far_parts, next_back, weight, *far_weight = pinned(
        far_back, far_parts, next_back, weight, *far_weight
    )

    far_merged = merge_far(far_back, far_index, far_use, blocks)
    far_home = to_partner(far_merged)
    far_back = exchange(far_parts)
    far_home, far_back, weight = pinned(far_home, far_back, weight)

    def swap(x, by):
        return lax.ppermute(x, "dp", [(i, i ^ by) for i in range(peer_count)])

    def plane_rows(moved):
        return [moved] + [swap(moved, by) for by in range(1, PLANE)] if by_plane else [moved]

    far_merged = merge_far(far_back, far_index, far_use, blocks)
    far_home, near_back, weight, _ = pinned(far_home, near_back, weight, far_merged)
    next_home = to_partner(far_merged)
    sources = plane_rows(merge_all(near_back, near_index, near_use, blocks, far_home))
    near_swap = [swap(weight, PLANE)] if by_plane else []
    count = len(sources)
    next_home, next_back = pinned(next_home, next_back)
    next_home, next_back, *held = pinned(next_home, next_back, *sources, *near_swap)
    sources, near_swap = held[:count], held[count:]
    moved = merge_all(next_back, near_index, near_use, blocks, next_home)
    if by_plane:
        place = lax.rem(here, PLANE).reshape(1)
        stay = lax.axis_index("tensor").astype(jnp.int32).reshape(1)
        far_weight = jnp.concatenate(far_weight, axis=0)
        far_weight, moved = pinned(far_weight, moved)
        shards = [weight, *near_swap, far_weight, swap(far_weight, PLANE)]
        line = jnp.stack(
            [here // PLANE, (here ^ PLANE) // PLANE, partner // PLANE, (partner ^ PLANE) // PLANE]
        )
        first_rows = [moved_part[rows : rows + 1] for moved_part in (sources[0], moved)]
        sources += plane_rows(moved)
        first_row = jnp.concatenate(first_rows, axis=1)
        below = functools.reduce(
            jnp.add,
            [
                lax.ppermute(
                    first_row,
                    "dp",
                    [(i + PLANE, i + at) for i in range(0, peer_count - PLANE, PLANE)],
                )
                for at in range(PLANE)
            ],
        )
        keep, send = project(sources, below, shards, place, stay)
        summed = add_cores(keep, lax.ppermute(send, "tensor", [(0, 1), (1, 0)]), place)
        branches = [summed[0]] + [swap(summed[by], by) for by in range(1, PLANE)]
    else:
        whole_weight = lax.all_gather(out_weight, "dp", axis=1, tiled=True)
        moved = jnp.concatenate([sources[0], moved], axis=1)
        below = shifted(moved[rows : rows + 1], "dp", -1)
        cross_rows = jnp.concatenate([moved[: rows - 1], below], axis=0)
        branch = jnp.dot(cross_rows, whole_weight, preferred_element_type=jnp.float32)
        branches = [
            lax.psum_scatter(
                branch.astype(jnp.bfloat16), "tensor", scatter_dimension=0, tiled=True
            )
        ]
        place = line = jnp.zeros((1,), jnp.int32)
    return tuple(
        add_norm(
            place, line, branches, out_weight.shape[1], residual, drop_mask, norm_gain, norm_bias
        )
    )


def solution(mesh):
    placed = (
        P("dp", "tensor"),
        P("dp", None, "tensor"),
        P("dp", None, "tensor"),
        P(("dp", "tensor"), None),
        P("tensor", "dp"),
        P(("dp", "tensor"), None),
        P(),
        P(),
        P("dp", None),
        P("dp", None),
    )
    return jax.shard_map(
        local,
        mesh=mesh,
        in_specs=placed,
        out_specs=(P(("dp", "tensor"), None), P(("dp", "tensor"), None)),
        check_vma=False,
    )
```

```python
import functools

import jax
import jax.numpy as jnp
from jax import lax
from jax.experimental import pallas as pl
from jax.experimental.pallas import tpu as pltpu
from jax.sharding import PartitionSpec as P

HEAD = 128
LANES = 128
MIB = 1024 * 1024
ROW_TILE = 16
PLANE = 4

keep_rate = 0.9
norm_eps = 1e-05


def shifted(x, axis, by):
    count = lax.axis_size(axis)
    pairs = [(i, i + by) for i in range(count) if 0 <= i + by < count]
    return lax.ppermute(x, axis, pairs)


def spread_kernel(count, column, block_ref, slot_ref, carried_ref, *refs):
    pieces = refs[:count]
    out_ref, moved, tags, sems = refs[-4:]
    peers, span_len, _ = out_ref.shape
    rows, piece_width = pieces[0].shape
    row_width = moved.shape[1]
    at = 0
    for piece in pieces:
        for start in range(0, piece_width, 512):
            size = min(512, piece_width - start)
            held = piece[:, start : start + size].astype(jnp.float32)
            rolled = pltpu.roll(held, 1, 0)
            first = lax.broadcasted_iota(jnp.int32, (rows, size), 0) == 0
            above = carried_ref[0:1, at : at + size].astype(jnp.float32)
            moved[:, at : at + size] = jnp.where(first, above, rolled).astype(moved.dtype)
            at += size

    def copies(peer):
        start = pl.multiple_of(block_ref[peer] * span_len, span_len)
        yield pltpu.make_async_copy(
            moved.at[pl.ds(start, span_len)],
            out_ref.at[peer, :, pl.ds(column, row_width)],
            sems.at[0, peer],
        )
        yield pltpu.make_async_copy(
            tags.at[peer],
            out_ref.at[peer, :, pl.ds(column + row_width, LANES)],
            sems.at[1, peer],
        )

    for peer in range(peers):
        slot = slot_ref[peer].astype(jnp.float32)
        tags[peer] = jnp.full((span_len, LANES), slot, jnp.float32).astype(tags.dtype)
        for copy in copies(peer):
            copy.start()
    for peer in range(peers):
        for copy in copies(peer):
            copy.wait()


def spread(pieces, carried, block_of_peer, slot_of_peer, span_len, chunk, shared=None):
    peers = block_of_peer.shape[0]
    rows, piece_width = pieces[0].shape
    row_width = piece_width * len(pieces)
    wide = row_width + LANES
    whole = wide if shared is None else shared.shape[2]
    extra = [] if shared is None else [shared]
    return pl.pallas_call(
        functools.partial(spread_kernel, len(pieces), whole - wide),
        grid_spec=pltpu.PrefetchScalarGridSpec(
            num_scalar_prefetch=2,
            grid=(1,),
            in_specs=[pl.BlockSpec((1, row_width), lambda i, *_: (0, chunk))]
            + [pl.BlockSpec((rows, piece_width), lambda i, *_: (0, 0))] * len(pieces)
            + [pl.BlockSpec(memory_space=pl.ANY)] * len(extra),
            out_specs=pl.BlockSpec(memory_space=pl.ANY),
            scratch_shapes=[
                pltpu.VMEM((rows, row_width), carried.dtype),
                pltpu.VMEM((peers, span_len, LANES), carried.dtype),
                pltpu.SemaphoreType.DMA((2, peers)),
            ],
        ),
        out_shape=jax.ShapeDtypeStruct((peers, span_len, whole), carried.dtype),
        input_output_aliases={3 + len(pieces): 0} if extra else {},
        compiler_params=pltpu.CompilerParams(vmem_limit_bytes=32 * MIB),
        name="spread_queries",
    )(block_of_peer, slot_of_peer, carried, *pieces, *extra)


def pack_levels(stats, heads):
    part = lax.broadcasted_iota(jnp.int32, stats.shape, 1) // heads
    high = stats.astype(jnp.bfloat16).astype(jnp.float32)
    rest = stats - high
    middle = rest.astype(jnp.bfloat16).astype(jnp.float32)
    low = rest - middle
    return jnp.where(part == 0, high, jnp.where(part == 1, middle, jnp.where(part == 2, low, 0.0)))


def unpack_levels(packed, heads):
    packed = packed.astype(jnp.float32)
    return (
        packed
        + pltpu.roll(packed, LANES - heads, 1)
        + pltpu.roll(packed, LANES - 2 * heads, 1)
    )


def attend_kernel(valid_ref, slot_ref, query_ref, key_ref, value_ref, *refs):
    out_ref = refs[-1]
    row_width = key_ref.shape[2]
    span_len = query_ref.shape[1]
    length = key_ref.shape[1]
    heads = row_width // HEAD
    group = min(heads, 4)
    peer = pl.program_id(0)

    @pl.when(valid_ref[peer] > 0)
    def _():
        lane = lax.broadcasted_iota(jnp.int32, (span_len, LANES), 1)
        stats = jnp.zeros((span_len, LANES), jnp.float32)
        ones = jnp.ones((length, HEAD), jnp.bfloat16)
        for first in range(0, heads, group):
            chosen = range(first, first + group)
            cuts = [slice(head * HEAD, (head + 1) * HEAD) for head in chosen]
            scores = [
                lax.dot_general(
                    query_ref[0, :, cut],
                    key_ref[0, :, cut],
                    (((1,), (1,)), ((), ())),
                    preferred_element_type=jnp.float32,
                )
                * HEAD ** (-0.5)
                for cut in cuts
            ]
            peaks = [jnp.max(score, axis=1, keepdims=True) for score in scores]
            raised = [
                jnp.exp(score - peak).astype(jnp.bfloat16) for score, peak in zip(scores, peaks)
            ]
            sums = [
                jnp.dot(
                    weight,
                    jnp.concatenate([value_ref[0, :, cut], ones], axis=1),
                    preferred_element_type=jnp.float32,
                )
                for weight, cut in zip(raised, cuts)
            ]
            for head, cut, peak, both in zip(chosen, cuts, peaks, sums):
                total = both[:, HEAD:]
                out_ref[0, :, cut] = (both[:, :HEAD] / total).astype(out_ref.dtype)
                stats = jnp.where(lane % heads == head, peak + jnp.log(total), stats)
        out_ref[0, :, row_width:] = pack_levels(stats, heads).astype(out_ref.dtype)


def attend(asked, keys, values, valid, slots, width, chunk, part, size, place, places, shared):
    peers, span_len, _ = asked.shape
    length = keys.shape[1]
    heads = width // HEAD
    wide = width + LANES
    extra = [] if shared is None else [shared]
    return pl.pallas_call(
        attend_kernel,
        grid_spec=pltpu.PrefetchScalarGridSpec(
            num_scalar_prefetch=2,
            grid=(peers,),
            in_specs=[
                pl.BlockSpec((1, span_len, size), lambda i, v, s: (i, 0, part)),
                pl.BlockSpec((1, length, width), lambda i, v, s: (s[i], 0, chunk)),
                pl.BlockSpec((1, length, width), lambda i, v, s: (s[i], 0, chunk)),
            ]
            + [pl.BlockSpec(memory_space=pl.ANY)] * len(extra),
            out_specs=pl.BlockSpec((1, span_len, wide), lambda i, v, s: (i, 0, place)),
        ),
        out_shape=jax.ShapeDtypeStruct((peers, span_len, places * wide), asked.dtype),
        input_output_aliases={5: 0} if extra else {},
        compiler_params=pltpu.CompilerParams(vmem_limit_bytes=56 * MIB),
        cost_estimate=pl.CostEstimate(
            flops=4 * peers * heads * span_len * length * HEAD,
            bytes_accessed=2 * peers * width * (2 * span_len + 2 * length),
            transcendentals=peers * heads * span_len * length,
        ),
        name="attend_blocks",
    )(valid, slots, asked, keys, values, *extra)


def merge_block(uses, parts):
    row_width = parts[0].shape[2] - LANES
    heads = row_width // HEAD

    def masked(use, held, other):
        return held if use is None else jnp.where(use, held, other)

    levels = [
        masked(use, unpack_levels(ref[0, :, row_width:], heads), -1e30)
        for use, ref in zip(uses, parts)
    ]
    highest = functools.reduce(jnp.maximum, levels)
    weights = [jnp.exp(level - highest) for level in levels]
    total = functools.reduce(jnp.add, weights)
    weights = [weight / total for weight in weights]
    for head in range(heads):
        cut = slice(head * HEAD, (head + 1) * HEAD)
        merged = functools.reduce(
            jnp.add,
            [
                weight[:, head : head + 1]
                * masked(use, ref[0, :, cut].astype(jnp.float32), 0.0)
                for use, weight, ref in zip(uses, weights, parts)
            ],
        )
        yield cut, merged
    lane = lax.broadcasted_iota(jnp.int32, highest.shape, 1)
    level = jnp.where(lane < heads, highest + jnp.log(total), 0.0)
    level = level + pltpu.roll(level, heads, 1) + pltpu.roll(level, 2 * heads, 1)
    yield slice(row_width, row_width + LANES), pack_levels(level, heads)


def merge_far_kernel(picked, index_ref, use_ref, *refs):
    block = pl.program_id(0)
    uses = [use_ref[block * picked + r] > 0 for r in range(picked)]
    out_ref = refs[-1]
    for cut, merged in merge_block(uses, refs[:-1]):
        out_ref[0, :, cut] = merged.astype(out_ref.dtype)


def merge_all_kernel(picked, index_ref, use_ref, *refs):
    out_ref, kept = refs[-2:]
    parts = refs[:-2]
    span_len = parts[0].shape[1]
    rows, row_width = out_ref.shape
    rows -= ROW_TILE
    step = pl.program_id(0)
    block = rows // span_len - 1 - step
    uses = [use_ref[block * picked + r] > 0 for r in range(picked)] + [None]
    start = pl.multiple_of(block * span_len, span_len)
    last = lax.broadcasted_iota(jnp.int32, (span_len, HEAD), 0) == span_len - 1

    @pl.when(step == 0)
    def _():
        kept[...] = jnp.zeros_like(kept)

    for cut, merged in merge_block(uses, parts):
        if cut.start < row_width:
            moved = pltpu.roll(merged, span_len - 1, 0)
            moved = jnp.where(last, kept[0:1, cut], moved)
            out_ref[pl.ds(start, span_len), cut] = moved.astype(out_ref.dtype)
            kept[:, cut] = merged[:8]
            out_ref[rows:, cut] = merged[:ROW_TILE].astype(out_ref.dtype)


def merge_far(parts, column, wide, index, use, blocks):
    span_len = parts.shape[1]
    picked = index.shape[0] // blocks
    specs = [
        pl.BlockSpec(
            (1, span_len, wide),
            functools.partial(lambda r, i, index, use: (index[i * picked + r], 0, column), r),
        )
        for r in range(picked)
    ]
    return pl.pallas_call(
        functools.partial(merge_far_kernel, picked),
        grid_spec=pltpu.PrefetchScalarGridSpec(
            num_scalar_prefetch=2,
            grid=(blocks,),
            in_specs=specs,
            out_specs=pl.BlockSpec((1, span_len, wide), lambda i, *_: (i, 0, 0)),
        ),
        out_shape=jax.ShapeDtypeStruct((blocks, span_len, wide), parts.dtype),
        compiler_params=pltpu.CompilerParams(vmem_limit_bytes=32 * MIB),
        name="merge_far",
    )(index, use, *([parts] * picked))


def merge_all(parts, column, wide, index, use, blocks, far):
    span_len = parts.shape[1]
    row_width = wide - LANES
    picked = index.shape[0] // blocks
    rows = blocks * span_len
    specs = [
        pl.BlockSpec(
            (1, span_len, wide),
            functools.partial(
                lambda r, i, index, use: (index[(blocks - 1 - i) * picked + r], 0, column), r
            ),
        )
        for r in range(picked)
    ]
    specs.append(pl.BlockSpec((1, span_len, wide), lambda i, *_: (blocks - 1 - i, 0, 0)))
    return pl.pallas_call(
        functools.partial(merge_all_kernel, picked),
        grid_spec=pltpu.PrefetchScalarGridSpec(
            num_scalar_prefetch=2,
            grid=(blocks,),
            in_specs=specs,
            out_specs=pl.BlockSpec((rows + ROW_TILE, row_width), lambda i, *_: (0, 0)),
            scratch_shapes=[pltpu.VMEM((8, row_width), jnp.float32)],
        ),
        out_shape=jax.ShapeDtypeStruct((rows + ROW_TILE, row_width), parts.dtype),
        compiler_params=pltpu.CompilerParams(vmem_limit_bytes=32 * MIB),
        name="merge_all",
    )(index, use, *([parts] * picked), far)


def project_kernel(count, place_ref, stay_ref, *refs):
    sources, below_ref, weights = refs[:count], refs[count], refs[count + 1 : -7]
    keep_ref, send_ref, rows_ref, first_ref, held_ref, row_sems, weight_sems = refs[-7:]
    half = keep_ref.shape[0]
    part = half // PLANE
    tile = held_ref.shape[2]

    def source_copies():
        for at, ref in enumerate(sources):
            member = place_ref[0] ^ (at % PLANE)
            width = ref.shape[1]
            cut = pl.ds(at // PLANE * width, width)
            for side in range(2):
                to = pl.multiple_of(side * half + member * part, part)
                yield pltpu.make_async_copy(
                    ref.at[pl.ds(side * part, part)],
                    rows_ref.at[pl.ds(to, part), cut],
                    row_sems.at[at, side],
                )
            to = pl.multiple_of(member * ROW_TILE, ROW_TILE)
            yield pltpu.make_async_copy(
                ref.at[pl.ds(2 * part, ROW_TILE)],
                first_ref.at[pl.ds(to, ROW_TILE), cut],
                row_sems.at[at, 2],
            )

    def weight_copy(shard):
        return pltpu.make_async_copy(weights[shard], held_ref.at[shard], weight_sems.at[shard])

    for copy in source_copies():
        copy.start()
    for shard in range(len(weights)):
        weight_copy(shard).start()
    for copy in source_copies():
        copy.wait()
    shape = (ROW_TILE, rows_ref.shape[1])
    last = lax.broadcasted_iota(jnp.int32, shape, 0) == ROW_TILE - 1
    for member in range(PLANE):
        if member < PLANE - 1:
            at = (member + 1) * ROW_TILE
            below = first_ref[at : at + ROW_TILE].astype(jnp.float32)[0:1]
        else:
            below = below_ref[...].astype(jnp.float32)[0:1]
        end = half + (member + 1) * part
        held = rows_ref[end - ROW_TILE : end].astype(jnp.float32)
        rows_ref[end - ROW_TILE : end] = jnp.where(last, below, held).astype(rows_ref.dtype)
    stay = pl.multiple_of(stay_ref[0] * half, half)
    go = pl.multiple_of((1 - stay_ref[0]) * half, half)
    for shard in range(len(weights)):
        weight_copy(shard).wait()
        for start, ref in ((go, send_ref), (stay, keep_ref)):
            ref[:, shard * tile : (shard + 1) * tile] = jnp.dot(
                rows_ref[pl.ds(start, half)],
                held_ref[shard],
                preferred_element_type=jnp.float32,
            ).astype(ref.dtype)


def project(sources, below, weights, place, stay):
    height = sources[0].shape[0]
    row_width = below.shape[1]
    rows = PLANE * (height - ROW_TILE)
    shards = len(weights)
    tile = weights[0].shape[1]
    columns = shards * tile
    half = rows // 2
    kind = sources[0].dtype
    return pl.pallas_call(
        functools.partial(project_kernel, len(sources)),
        grid_spec=pltpu.PrefetchScalarGridSpec(
            num_scalar_prefetch=2,
            grid=(1,),
            in_specs=[pl.BlockSpec(memory_space=pl.ANY)] * len(sources)
            + [pl.BlockSpec((1, row_width), lambda i, *_: (0, 0))]
            + [pl.BlockSpec(memory_space=pl.ANY)] * shards,
            out_specs=[pl.BlockSpec((half, columns), lambda i, *_: (0, 0))] * 2,
            scratch_shapes=[
                pltpu.VMEM((rows, row_width), kind),
                pltpu.VMEM((PLANE * ROW_TILE, row_width), kind),
                pltpu.VMEM((shards, row_width, tile), kind),
                pltpu.SemaphoreType.DMA((len(sources), 3)),
                pltpu.SemaphoreType.DMA((shards,)),
            ],
        ),
        out_shape=[jax.ShapeDtypeStruct((half, columns), kind)] * 2,
        compiler_params=pltpu.CompilerParams(vmem_limit_bytes=30 * MIB),
        name="project_rows",
    )(place, stay, *sources, below, *weights)


def add_kernel(place_ref, keep_ref, other_ref, *outs):
    for at, ref in enumerate(outs):
        member = place_ref[0] ^ at
        ref[...] = (
            keep_ref[member].astype(jnp.float32) + other_ref[member].astype(jnp.float32)
        ).astype(ref.dtype)


def add_cores(keep, other, place):
    half, columns = keep.shape
    part = half // PLANE
    tile = min(columns, 512)
    folded = (PLANE, part, columns)
    return pl.pallas_call(
        add_kernel,
        grid_spec=pltpu.PrefetchScalarGridSpec(
            num_scalar_prefetch=1,
            grid=(columns // tile,),
            in_specs=[pl.BlockSpec((PLANE, part, tile), lambda i, *_: (0, 0, i))] * 2,
            out_specs=[pl.BlockSpec((part, tile), lambda i, *_: (0, i))] * PLANE,
        ),
        out_shape=[jax.ShapeDtypeStruct((part, columns), keep.dtype)] * PLANE,
        compiler_params=pltpu.CompilerParams(vmem_limit_bytes=32 * MIB),
        name="add_cores",
    )(place, keep.reshape(folded), other.reshape(folded))


def norm_kernel(strip, place_ref, line_ref, *refs):
    branches = refs[:-7]
    residual_ref, mask_ref, gain_ref, bias_ref, next_ref, normed_ref, branch_ref = refs[-7:]
    if len(branches) == 1:
        branch_ref[...] = branches[0][...].astype(jnp.float32)
    else:
        for at, ref in enumerate(branches):
            member = place_ref[0] ^ at
            for shard in range(ref.shape[1] // strip):
                to = pl.multiple_of((line_ref[shard] * PLANE + member) * strip, strip)
                branch_ref[:, pl.ds(to, strip)] = ref[
                    :, shard * strip : (shard + 1) * strip
                ].astype(jnp.float32)
    keep_scale = mask_ref[...].astype(jnp.float32) * (1.0 / keep_rate)
    stream = residual_ref[...].astype(jnp.float32) + keep_scale * branch_ref[...]
    centre = jnp.mean(stream, axis=1, keepdims=True)
    moved = stream - centre
    spread_of = jnp.mean(jnp.square(moved), axis=1, keepdims=True)
    normed = moved * lax.rsqrt(spread_of + norm_eps) * gain_ref[...] + bias_ref[...]
    next_ref[...] = stream.astype(next_ref.dtype)
    normed_ref[...] = normed.astype(normed_ref.dtype)


def add_norm(place, line, branches, strip, residual, drop_mask, gain, bias):
    rows, columns = residual.shape
    tile = min(32, rows)
    row_spec = pl.BlockSpec((tile, columns), lambda i, *_: (i, 0))
    branch_spec = pl.BlockSpec((tile, branches[0].shape[1]), lambda i, *_: (i, 0))
    flat_spec = pl.BlockSpec((1, columns), lambda i, *_: (0, 0))
    return pl.pallas_call(
        functools.partial(norm_kernel, strip),
        grid_spec=pltpu.PrefetchScalarGridSpec(
            num_scalar_prefetch=2,
            grid=(rows // tile,),
            in_specs=[branch_spec] * len(branches) + [row_spec, row_spec, flat_spec, flat_spec],
            out_specs=[row_spec, row_spec],
            scratch_shapes=[pltpu.VMEM((tile, columns), jnp.float32)],
        ),
        out_shape=[jax.ShapeDtypeStruct((rows, columns), residual.dtype)] * 2,
        compiler_params=pltpu.CompilerParams(vmem_limit_bytes=32 * MIB),
        name="add_norm",
    )(place, line, *branches, residual, drop_mask, gain[None], bias[None])


def pick_requests(owners, slots, peers, per_block):
    selector = owners[None, :] == peers[:, None]
    pair_block = jnp.arange(owners.shape[0], dtype=jnp.int32) // per_block
    return (
        jnp.sum(jnp.where(selector, pair_block[None, :], 0), axis=1),
        jnp.sum(jnp.where(selector, slots[None, :] + 1, 0), axis=1),
    )


def within(owners, base, half):
    index = owners - base
    use = (index >= 0) & (index < half)
    return jnp.where(use, index, 0), use.astype(jnp.int32)


def local(
    queries,
    neighbour_keys,
    neighbour_values,
    residual,
    out_weight,
    drop_mask,
    norm_gain,
    norm_bias,
    neighbour_owner,
    neighbour_slot,
):
    peer_count = lax.axis_size("dp")
    side_count = lax.axis_size("tensor")
    half = peer_count // 2
    halves = [list(range(half)), list(range(half, peer_count))]
    across = [(i, (i + half) % peer_count) for i in range(peer_count)]
    by_plane = side_count == 2 and peer_count == 4 * PLANE
    blocks, per_block = neighbour_owner.shape
    rows, row_width = queries.shape
    span_len = rows // blocks
    here = lax.axis_index("dp").astype(jnp.int32)
    upper = here // half
    base = upper * half
    partner = lax.rem(here + half, peer_count)

    def exchange(x):
        return lax.all_to_all(
            x, "dp", split_axis=0, concat_axis=0, tiled=True, axis_index_groups=halves
        )

    def pinned(*values):
        return lax.optimization_barrier(values)

    def to_partner(x):
        return lax.ppermute(x, "dp", across)

    chunks = 2
    width = row_width // chunks
    far_first = to_partner(queries[:, :width])
    carried = shifted(queries[-1:], "dp", 1)
    owners = neighbour_owner.reshape(-1)
    slot_rows = neighbour_slot.reshape(-1)
    near_peers = base + jnp.arange(half, dtype=jnp.int32)
    near_out = spread(
        [queries], carried, *pick_requests(owners, slot_rows, near_peers, per_block),
        span_len, 0,
    )
    near_asked = exchange(near_out)
    far_carried = lax.ppermute(
        queries[-1:], "dp", [(i - 1, (i + half) % peer_count) for i in range(1, peer_count)]
    )
    requests = owners.shape[0]
    far_table = to_partner(
        jnp.pad(jnp.concatenate([owners, slot_rows]), (0, LANES - 2 * requests))[None, :]
    )
    far_first, far_carried, far_table, held_queries, _ = pinned(
        far_first, far_carried, far_table, queries, near_out
    )
    far_owners = far_table[0, :requests]
    far_picked = pick_requests(
        far_owners, far_table[0, requests : 2 * requests], near_peers, per_block
    )

    def slots_of(asked):
        return asked[:, 0, -LANES].astype(jnp.int32)

    def answer(asked, tags, chunk, part, size, place, places, shared=None):
        valid = (tags > 0).astype(jnp.int32)
        slots = jnp.maximum(tags - 1, 0)
        return attend(
            asked, neighbour_keys, neighbour_values, valid, slots, width, chunk, part, size,
            place, places, shared,
        )

    wide = width + LANES
    far_second = to_partner(held_queries[:, width:])
    near_index, near_use = within(owners, base, half)
    far_index, far_use = within(far_owners, base, half)
    far_out = spread([far_first], far_carried, *far_picked, span_len, 0)
    far_asked = exchange(far_out)
    near_asked, _ = pinned(near_asked, far_out)
    near_tags = slots_of(near_asked)
    near_first = answer(near_asked, near_tags, 0, 0, width, 0, 2)
    near_second = answer(near_asked, near_tags, 1, 1, width, 1, 2)
    far_asked, far_second, weight, near_first, near_second = pinned(
        far_asked, far_second, out_weight, near_first, near_second
    )

    middle = row_width // 2
    mixed = spread([far_second], far_carried, *far_picked, span_len, 1, near_first)
    next_asked = exchange(mixed)
    far_asked, near_second, _ = pinned(far_asked, near_second, mixed)
    far_weight = [to_partner(weight[:middle])] if by_plane else []
    far_tags = slots_of(far_asked)
    mixed = answer(far_asked, far_tags, 0, 0, wide, 0, 2, near_second)
    mixed, next_asked, weight, *far_weight = pinned(mixed, next_asked, weight, *far_weight)

    far_back = exchange(mixed)
    if by_plane:
        far_weight.append(to_partner(weight[middle:]))
    far_parts = answer(next_asked, far_tags, 1, 1, wide, 0, 1)
    far_back, far_parts, weight, *far_weight = pinned(far_back, far_parts, weight, *far_weight)
    near_back, next_back = next_asked, far_back

    far_merged = merge_far(far_back, 0, wide, far_index, far_use, blocks)
    far_home = to_partner(far_merged)
    far_back = exchange(far_parts)
    far_home, far_back, weight = pinned(far_home, far_back, weight)

    def swap(x, by):
        return lax.ppermute(x, "dp", [(i, i ^ by) for i in range(peer_count)])

    def plane_rows(moved):
        return [moved] + [swap(moved, by) for by in range(1, PLANE)] if by_plane else [moved]

    far_merged = merge_far(far_back, 0, wide, far_index, far_use, blocks)
    far_home, near_back, weight, _ = pinned(far_home, near_back, weight, far_merged)
    next_home = to_partner(far_merged)
    sources = plane_rows(
        merge_all(near_back, 0, wide, near_index, near_use, blocks, far_home)
    )
    near_swap = [swap(weight, PLANE)] if by_plane else []
    count = len(sources)
    next_home, next_back = pinned(next_home, next_back)
    next_home, next_back, *held = pinned(next_home, next_back, *sources, *near_swap)
    sources, near_swap = held[:count], held[count:]
    moved = merge_all(next_back, 1, wide, near_index, near_use, blocks, next_home)
    if by_plane:
        place = lax.rem(here, PLANE).reshape(1)
        stay = lax.axis_index("tensor").astype(jnp.int32).reshape(1)
        far_weight = jnp.concatenate(far_weight, axis=0)
        far_weight, moved = pinned(far_weight, moved)
        shards = [weight, *near_swap, far_weight, swap(far_weight, PLANE)]
        line = jnp.stack(
            [here // PLANE, (here ^ PLANE) // PLANE, partner // PLANE, (partner ^ PLANE) // PLANE]
        )
        first_rows = [moved_part[rows : rows + 1] for moved_part in (sources[0], moved)]
        sources += plane_rows(moved)
        first_row = jnp.concatenate(first_rows, axis=1)
        below = functools.reduce(
            jnp.add,
            [
                lax.ppermute(
                    first_row,
                    "dp",
                    [(i + PLANE, i + at) for i in range(0, peer_count - PLANE, PLANE)],
                )
                for at in range(PLANE)
            ],
        )
        keep, send = project(sources, below, shards, place, stay)
        summed = add_cores(keep, lax.ppermute(send, "tensor", [(0, 1), (1, 0)]), place)
        branches = [summed[0]] + [swap(summed[by], by) for by in range(1, PLANE)]
    else:
        whole_weight = lax.all_gather(out_weight, "dp", axis=1, tiled=True)
        moved = jnp.concatenate([sources[0], moved], axis=1)
        below = shifted(moved[rows : rows + 1], "dp", -1)
        cross_rows = jnp.concatenate([moved[: rows - 1], below], axis=0)
        branch = jnp.dot(cross_rows, whole_weight, preferred_element_type=jnp.float32)
        branches = [
            lax.psum_scatter(
                branch.astype(jnp.bfloat16), "tensor", scatter_dimension=0, tiled=True
            )
        ]
        place = line = jnp.zeros((1,), jnp.int32)
    return tuple(
        add_norm(
            place, line, branches, out_weight.shape[1], residual, drop_mask, norm_gain, norm_bias
        )
    )


def solution(mesh):
    placed = (
        P("dp", "tensor"),
        P("dp", None, "tensor"),
        P("dp", None, "tensor"),
        P(("dp", "tensor"), None),
        P("tensor", "dp"),
        P(("dp", "tensor"), None),
        P(),
        P(),
        P("dp", None),
        P("dp", None),
    )
    return jax.shard_map(
        local,
        mesh=mesh,
        in_specs=placed,
        out_specs=(P(("dp", "tensor"), None), P(("dp", "tensor"), None)),
        check_vma=False,
    )
```

```python
import functools

import jax
import jax.numpy as jnp
from jax import lax
from jax.experimental import pallas as pl
from jax.experimental.pallas import tpu as pltpu
from jax.sharding import PartitionSpec as P

HEAD = 128
LANES = 128
MIB = 1024 * 1024
ROW_TILE = 16
PLANE = 4

keep_rate = 0.9
norm_eps = 1e-05


def shifted(x, axis, by):
    count = lax.axis_size(axis)
    pairs = [(i, i + by) for i in range(count) if 0 <= i + by < count]
    return lax.ppermute(x, axis, pairs)


def spread_kernel(count, column, block_ref, slot_ref, carried_ref, *refs):
    pieces = refs[:count]
    out_ref, moved, tags, sems = refs[-4:]
    peers, span_len, _ = out_ref.shape
    rows, piece_width = pieces[0].shape
    row_width = moved.shape[1]
    at = 0
    for piece in pieces:
        for start in range(0, piece_width, 512):
            size = min(512, piece_width - start)
            held = piece[:, start : start + size].astype(jnp.float32)
            rolled = pltpu.roll(held, 1, 0)
            first = lax.broadcasted_iota(jnp.int32, (rows, size), 0) == 0
            above = carried_ref[0:1, at : at + size].astype(jnp.float32)
            moved[:, at : at + size] = jnp.where(first, above, rolled).astype(moved.dtype)
            at += size

    def copies(peer):
        start = pl.multiple_of(block_ref[peer] * span_len, span_len)
        yield pltpu.make_async_copy(
            moved.at[pl.ds(start, span_len)],
            out_ref.at[peer, :, pl.ds(column, row_width)],
            sems.at[0, peer],
        )
        yield pltpu.make_async_copy(
            tags.at[peer],
            out_ref.at[peer, :, pl.ds(column + row_width, LANES)],
            sems.at[1, peer],
        )

    for peer in range(peers):
        slot = slot_ref[peer].astype(jnp.float32)
        tags[peer] = jnp.full((span_len, LANES), slot, jnp.float32).astype(tags.dtype)
        for copy in copies(peer):
            copy.start()
    for peer in range(peers):
        for copy in copies(peer):
            copy.wait()


def spread(pieces, carried, block_of_peer, slot_of_peer, span_len, chunk, shared=None):
    peers = block_of_peer.shape[0]
    rows, piece_width = pieces[0].shape
    row_width = piece_width * len(pieces)
    wide = row_width + LANES
    whole = wide if shared is None else shared.shape[2]
    extra = [] if shared is None else [shared]
    return pl.pallas_call(
        functools.partial(spread_kernel, len(pieces), whole - wide),
        grid_spec=pltpu.PrefetchScalarGridSpec(
            num_scalar_prefetch=2,
            grid=(1,),
            in_specs=[pl.BlockSpec((1, row_width), lambda i, *_: (0, chunk))]
            + [pl.BlockSpec((rows, piece_width), lambda i, *_: (0, 0))] * len(pieces)
            + [pl.BlockSpec(memory_space=pl.ANY)] * len(extra),
            out_specs=pl.BlockSpec(memory_space=pl.ANY),
            scratch_shapes=[
                pltpu.VMEM((rows, row_width), carried.dtype),
                pltpu.VMEM((peers, span_len, LANES), carried.dtype),
                pltpu.SemaphoreType.DMA((2, peers)),
            ],
        ),
        out_shape=jax.ShapeDtypeStruct((peers, span_len, whole), carried.dtype),
        input_output_aliases={3 + len(pieces): 0} if extra else {},
        compiler_params=pltpu.CompilerParams(vmem_limit_bytes=10 * MIB),
        name="spread_queries",
    )(block_of_peer, slot_of_peer, carried, *pieces, *extra)


def pack_levels(stats, heads):
    part = lax.broadcasted_iota(jnp.int32, stats.shape, 1) // heads
    high = stats.astype(jnp.bfloat16).astype(jnp.float32)
    rest = stats - high
    middle = rest.astype(jnp.bfloat16).astype(jnp.float32)
    low = rest - middle
    return jnp.where(part == 0, high, jnp.where(part == 1, middle, jnp.where(part == 2, low, 0.0)))


def unpack_levels(packed, heads):
    packed = packed.astype(jnp.float32)
    return (
        packed
        + pltpu.roll(packed, LANES - heads, 1)
        + pltpu.roll(packed, LANES - 2 * heads, 1)
    )


def attend_kernel(chunk, valid_ref, slot_ref, query_ref, key_ref, value_ref, *refs):
    out_ref, key_held, value_held, sems = refs[-4:]
    span_len = query_ref.shape[1]
    _, length, row_width = key_held.shape
    heads = row_width // HEAD
    group = min(heads, 4)
    peer = pl.program_id(0)
    peers = pl.num_programs(0)

    def copies(at):
        buffer = lax.rem(at, 2)
        for kind, (ref, held) in enumerate(((key_ref, key_held), (value_ref, value_held))):
            yield pltpu.make_async_copy(
                ref.at[slot_ref[at], :, pl.ds(chunk * row_width, row_width)],
                held.at[buffer],
                sems.at[kind, buffer],
            )

    def fetch(at):
        for copy in copies(at):
            copy.start()

    following = jnp.minimum(peer + 1, peers - 1)

    @pl.when((peer == 0) & (valid_ref[0] > 0))
    def _():
        fetch(0)

    @pl.when((peer + 1 < peers) & (valid_ref[following] > 0))
    def _():
        fetch(following)

    @pl.when(valid_ref[peer] > 0)
    def _():
        for copy in copies(peer):
            copy.wait()
        buffer = lax.rem(peer, 2)
        lane = lax.broadcasted_iota(jnp.int32, (span_len, LANES), 1)
        stats = jnp.zeros((span_len, LANES), jnp.float32)
        ones = jnp.ones((length, HEAD), jnp.bfloat16)
        for first in range(0, heads, group):
            chosen = range(first, first + group)
            cuts = [slice(head * HEAD, (head + 1) * HEAD) for head in chosen]
            scores = [
                lax.dot_general(
                    query_ref[0, :, cut],
                    key_held[buffer, :, cut],
                    (((1,), (1,)), ((), ())),
                    preferred_element_type=jnp.float32,
                )
                * HEAD ** (-0.5)
                for cut in cuts
            ]
            peaks = [jnp.max(score, axis=1, keepdims=True) for score in scores]
            raised = [
                jnp.exp(score - peak).astype(jnp.bfloat16) for score, peak in zip(scores, peaks)
            ]
            sums = [
                jnp.dot(
                    weight,
                    jnp.concatenate([value_held[buffer, :, cut], ones], axis=1),
                    preferred_element_type=jnp.float32,
                )
                for weight, cut in zip(raised, cuts)
            ]
            for head, cut, peak, both in zip(chosen, cuts, peaks, sums):
                total = both[:, HEAD:]
                out_ref[0, :, cut] = (both[:, :HEAD] / total).astype(out_ref.dtype)
                stats = jnp.where(lane % heads == head, peak + jnp.log(total), stats)
        out_ref[0, :, row_width:] = pack_levels(stats, heads).astype(out_ref.dtype)


def attend(asked, keys, values, valid, slots, width, chunk, part, size, place, places, shared):
    peers, span_len, _ = asked.shape
    length = keys.shape[1]
    heads = width // HEAD
    wide = width + LANES
    extra = [] if shared is None else [shared]
    return pl.pallas_call(
        functools.partial(attend_kernel, chunk),
        grid_spec=pltpu.PrefetchScalarGridSpec(
            num_scalar_prefetch=2,
            grid=(peers,),
            in_specs=[
                pl.BlockSpec((1, span_len, size), lambda i, v, s: (i, 0, part)),
                pl.BlockSpec(memory_space=pltpu.HBM),
                pl.BlockSpec(memory_space=pltpu.HBM),
            ]
            + [pl.BlockSpec(memory_space=pl.ANY)] * len(extra),
            out_specs=pl.BlockSpec((1, span_len, wide), lambda i, v, s: (i, 0, place)),
            scratch_shapes=[
                pltpu.VMEM((2, length, width), keys.dtype),
                pltpu.VMEM((2, length, width), keys.dtype),
                pltpu.SemaphoreType.DMA((2, 2)),
            ],
        ),
        out_shape=jax.ShapeDtypeStruct((peers, span_len, places * wide), asked.dtype),
        input_output_aliases={5: 0} if extra else {},
        compiler_params=pltpu.CompilerParams(vmem_limit_bytes=12 * MIB),
        cost_estimate=pl.CostEstimate(
            flops=4 * peers * heads * span_len * length * HEAD,
            bytes_accessed=2 * peers * width * (2 * span_len + 2 * length),
            transcendentals=peers * heads * span_len * length,
        ),
        name="attend_blocks",
    )(valid, slots, asked, keys, values, *extra)


def merge_block(uses, parts):
    row_width = parts[0].shape[2] - LANES
    heads = row_width // HEAD

    def masked(use, held, other):
        return held if use is None else jnp.where(use, held, other)

    levels = [
        masked(use, unpack_levels(ref[0, :, row_width:], heads), -1e30)
        for use, ref in zip(uses, parts)
    ]
    highest = functools.reduce(jnp.maximum, levels)
    weights = [jnp.exp(level - highest) for level in levels]
    total = functools.reduce(jnp.add, weights)
    weights = [weight / total for weight in weights]
    for head in range(heads):
        cut = slice(head * HEAD, (head + 1) * HEAD)
        merged = functools.reduce(
            jnp.add,
            [
                weight[:, head : head + 1]
                * masked(use, ref[0, :, cut].astype(jnp.float32), 0.0)
                for use, weight, ref in zip(uses, weights, parts)
            ],
        )
        yield cut, merged
    lane = lax.broadcasted_iota(jnp.int32, highest.shape, 1)
    level = jnp.where(lane < heads, highest + jnp.log(total), 0.0)
    level = level + pltpu.roll(level, heads, 1) + pltpu.roll(level, 2 * heads, 1)
    yield slice(row_width, row_width + LANES), pack_levels(level, heads)


def merge_far_kernel(picked, index_ref, use_ref, *refs):
    block = pl.program_id(0)
    uses = [use_ref[block * picked + r] > 0 for r in range(picked)]
    out_ref = refs[-1]
    for cut, merged in merge_block(uses, refs[:-1]):
        out_ref[0, :, cut] = merged.astype(out_ref.dtype)


def merge_all_kernel(picked, index_ref, use_ref, *refs):
    out_ref, kept = refs[-2:]
    parts = refs[:-2]
    span_len = parts[0].shape[1]
    rows, row_width = out_ref.shape
    rows -= ROW_TILE
    step = pl.program_id(0)
    block = rows // span_len - 1 - step
    uses = [use_ref[block * picked + r] > 0 for r in range(picked)] + [None]
    start = pl.multiple_of(block * span_len, span_len)
    last = lax.broadcasted_iota(jnp.int32, (span_len, HEAD), 0) == span_len - 1

    @pl.when(step == 0)
    def _():
        kept[...] = jnp.zeros_like(kept)

    for cut, merged in merge_block(uses, parts):
        if cut.start < row_width:
            moved = pltpu.roll(merged, span_len - 1, 0)
            moved = jnp.where(last, kept[0:1, cut], moved)
            out_ref[pl.ds(start, span_len), cut] = moved.astype(out_ref.dtype)
            kept[:, cut] = merged[:8]
            out_ref[rows:, cut] = merged[:ROW_TILE].astype(out_ref.dtype)


def merge_far(parts, column, wide, index, use, blocks):
    span_len = parts.shape[1]
    picked = index.shape[0] // blocks
    specs = [
        pl.BlockSpec(
            (1, span_len, wide),
            functools.partial(lambda r, i, index, use: (index[i * picked + r], 0, column), r),
        )
        for r in range(picked)
    ]
    return pl.pallas_call(
        functools.partial(merge_far_kernel, picked),
        grid_spec=pltpu.PrefetchScalarGridSpec(
            num_scalar_prefetch=2,
            grid=(blocks,),
            in_specs=specs,
            out_specs=pl.BlockSpec((1, span_len, wide), lambda i, *_: (i, 0, 0)),
        ),
        out_shape=jax.ShapeDtypeStruct((blocks, span_len, wide), parts.dtype),
        compiler_params=pltpu.CompilerParams(vmem_limit_bytes=10 * MIB),
        name="merge_far",
    )(index, use, *([parts] * picked))


def merge_all(parts, column, wide, index, use, blocks, far):
    span_len = parts.shape[1]
    row_width = wide - LANES
    picked = index.shape[0] // blocks
    rows = blocks * span_len
    specs = [
        pl.BlockSpec(
            (1, span_len, wide),
            functools.partial(
                lambda r, i, index, use: (index[(blocks - 1 - i) * picked + r], 0, column), r
            ),
        )
        for r in range(picked)
    ]
    specs.append(pl.BlockSpec((1, span_len, wide), lambda i, *_: (blocks - 1 - i, 0, 0)))
    return pl.pallas_call(
        functools.partial(merge_all_kernel, picked),
        grid_spec=pltpu.PrefetchScalarGridSpec(
            num_scalar_prefetch=2,
            grid=(blocks,),
            in_specs=specs,
            out_specs=pl.BlockSpec((rows + ROW_TILE, row_width), lambda i, *_: (0, 0)),
            scratch_shapes=[pltpu.VMEM((8, row_width), jnp.float32)],
        ),
        out_shape=jax.ShapeDtypeStruct((rows + ROW_TILE, row_width), parts.dtype),
        compiler_params=pltpu.CompilerParams(vmem_limit_bytes=10 * MIB),
        name="merge_all",
    )(index, use, *([parts] * picked), far)


def project_kernel(count, shard_of, place_ref, stay_ref, *refs):
    sources, below_ref, weights = refs[:count], refs[count], refs[count + 1 : -7]
    keep_ref, send_ref, rows_ref, first_ref, held_ref, row_sems, weight_sems = refs[-7:]
    half = keep_ref.shape[0]
    part = half // PLANE
    tile = held_ref.shape[2]

    def source_copies():
        for at, ref in enumerate(sources):
            member = place_ref[0] ^ (at % PLANE)
            width = ref.shape[1]
            cut = pl.ds(at // PLANE * width, width)
            for side in range(2):
                to = pl.multiple_of(side * half + member * part, part)
                yield pltpu.make_async_copy(
                    ref.at[pl.ds(side * part, part)],
                    rows_ref.at[pl.ds(to, part), cut],
                    row_sems.at[at, side],
                )
            to = pl.multiple_of(member * ROW_TILE, ROW_TILE)
            yield pltpu.make_async_copy(
                ref.at[pl.ds(2 * part, ROW_TILE)],
                first_ref.at[pl.ds(to, ROW_TILE), cut],
                row_sems.at[at, 2],
            )

    def weight_copies(shard):
        at = 0
        for piece, (ref, of) in enumerate(zip(weights, shard_of)):
            if of == shard:
                size = ref.shape[0]
                yield pltpu.make_async_copy(
                    ref, held_ref.at[shard, pl.ds(at, size)], weight_sems.at[piece]
                )
                at += size

    for copy in source_copies():
        copy.start()
    shards = held_ref.shape[0]
    for shard in range(shards):
        for copy in weight_copies(shard):
            copy.start()
    for copy in source_copies():
        copy.wait()
    shape = (ROW_TILE, rows_ref.shape[1])
    last = lax.broadcasted_iota(jnp.int32, shape, 0) == ROW_TILE - 1
    for member in range(PLANE):
        if member < PLANE - 1:
            at = (member + 1) * ROW_TILE
            below = first_ref[at : at + ROW_TILE].astype(jnp.float32)[0:1]
        else:
            below = below_ref[...].astype(jnp.float32)[0:1]
        end = half + (member + 1) * part
        held = rows_ref[end - ROW_TILE : end].astype(jnp.float32)
        rows_ref[end - ROW_TILE : end] = jnp.where(last, below, held).astype(rows_ref.dtype)
    stay = pl.multiple_of(stay_ref[0] * half, half)
    go = pl.multiple_of((1 - stay_ref[0]) * half, half)
    for shard in range(shards):
        for copy in weight_copies(shard):
            copy.wait()
        for start, ref in ((go, send_ref), (stay, keep_ref)):
            ref[:, shard * tile : (shard + 1) * tile] = jnp.dot(
                rows_ref[pl.ds(start, half)],
                held_ref[shard],
                preferred_element_type=jnp.float32,
            ).astype(ref.dtype)


def project(sources, below, weights, place, stay):
    height = sources[0].shape[0]
    row_width = below.shape[1]
    rows = PLANE * (height - ROW_TILE)
    shards = len(weights)
    tile = weights[0][0].shape[1]
    shard_of = [shard for shard, pieces in enumerate(weights) for _ in pieces]
    pieces = [piece for pieces in weights for piece in pieces]
    columns = shards * tile
    half = rows // 2
    kind = sources[0].dtype
    return pl.pallas_call(
        functools.partial(project_kernel, len(sources), shard_of),
        grid_spec=pltpu.PrefetchScalarGridSpec(
            num_scalar_prefetch=2,
            grid=(1,),
            in_specs=[pl.BlockSpec(memory_space=pltpu.HBM)] * len(sources)
            + [pl.BlockSpec((1, row_width), lambda i, *_: (0, 0))]
            + [pl.BlockSpec(memory_space=pltpu.HBM)] * len(pieces),
            out_specs=[pl.BlockSpec((half, columns), lambda i, *_: (0, 0))] * 2,
            scratch_shapes=[
                pltpu.VMEM((rows, row_width), kind),
                pltpu.VMEM((PLANE * ROW_TILE, row_width), kind),
                pltpu.VMEM((shards, row_width, tile), kind),
                pltpu.SemaphoreType.DMA((len(sources), 3)),
                pltpu.SemaphoreType.DMA((len(pieces),)),
            ],
        ),
        out_shape=[jax.ShapeDtypeStruct((half, columns), kind)] * 2,
        compiler_params=pltpu.CompilerParams(vmem_limit_bytes=20 * MIB),
        name="project_rows",
    )(place, stay, *sources, below, *pieces)


def add_kernel(place_ref, keep_ref, other_ref, *outs):
    for at, ref in enumerate(outs):
        member = place_ref[0] ^ at
        ref[...] = (
            keep_ref[member].astype(jnp.float32) + other_ref[member].astype(jnp.float32)
        ).astype(ref.dtype)


def add_cores(keep, other, place):
    half, columns = keep.shape
    part = half // PLANE
    tile = min(columns, 512)
    folded = (PLANE, part, columns)
    return pl.pallas_call(
        add_kernel,
        grid_spec=pltpu.PrefetchScalarGridSpec(
            num_scalar_prefetch=1,
            grid=(columns // tile,),
            in_specs=[pl.BlockSpec((PLANE, part, tile), lambda i, *_: (0, 0, i))] * 2,
            out_specs=[pl.BlockSpec((part, tile), lambda i, *_: (0, i))] * PLANE,
        ),
        out_shape=[jax.ShapeDtypeStruct((part, columns), keep.dtype)] * PLANE,
        compiler_params=pltpu.CompilerParams(vmem_limit_bytes=10 * MIB),
        name="add_cores",
    )(place, keep.reshape(folded), other.reshape(folded))


def norm_kernel(strip, place_ref, line_ref, *refs):
    branches = refs[:-7]
    residual_ref, mask_ref, gain_ref, bias_ref, next_ref, normed_ref, branch_ref = refs[-7:]
    if len(branches) == 1:
        branch_ref[...] = branches[0][...].astype(jnp.float32)
    else:
        for at, ref in enumerate(branches):
            member = place_ref[0] ^ at
            for shard in range(ref.shape[1] // strip):
                to = pl.multiple_of((line_ref[shard] * PLANE + member) * strip, strip)
                branch_ref[:, pl.ds(to, strip)] = ref[
                    :, shard * strip : (shard + 1) * strip
                ].astype(jnp.float32)
    keep_scale = mask_ref[...].astype(jnp.float32) * (1.0 / keep_rate)
    stream = residual_ref[...].astype(jnp.float32) + keep_scale * branch_ref[...]
    centre = jnp.mean(stream, axis=1, keepdims=True)
    moved = stream - centre
    spread_of = jnp.mean(jnp.square(moved), axis=1, keepdims=True)
    normed = moved * lax.rsqrt(spread_of + norm_eps) * gain_ref[...] + bias_ref[...]
    next_ref[...] = stream.astype(next_ref.dtype)
    normed_ref[...] = normed.astype(normed_ref.dtype)


def add_norm(place, line, branches, strip, residual, drop_mask, gain, bias):
    rows, columns = residual.shape
    tile = min(32, rows)
    row_spec = pl.BlockSpec((tile, columns), lambda i, *_: (i, 0))
    branch_spec = pl.BlockSpec((tile, branches[0].shape[1]), lambda i, *_: (i, 0))
    flat_spec = pl.BlockSpec((1, columns), lambda i, *_: (0, 0))
    return pl.pallas_call(
        functools.partial(norm_kernel, strip),
        grid_spec=pltpu.PrefetchScalarGridSpec(
            num_scalar_prefetch=2,
            grid=(rows // tile,),
            in_specs=[branch_spec] * len(branches) + [row_spec, row_spec, flat_spec, flat_spec],
            out_specs=[row_spec, row_spec],
            scratch_shapes=[pltpu.VMEM((tile, columns), jnp.float32)],
        ),
        out_shape=[jax.ShapeDtypeStruct((rows, columns), residual.dtype)] * 2,
        compiler_params=pltpu.CompilerParams(vmem_limit_bytes=20 * MIB),
        name="add_norm",
    )(place, line, *branches, residual, drop_mask, gain[None], bias[None])


def pick_requests(owners, slots, peers, per_block):
    selector = owners[None, :] == peers[:, None]
    pair_block = jnp.arange(owners.shape[0], dtype=jnp.int32) // per_block
    return (
        jnp.sum(jnp.where(selector, pair_block[None, :], 0), axis=1),
        jnp.sum(jnp.where(selector, slots[None, :] + 1, 0), axis=1),
    )


def within(owners, base, half):
    index = owners - base
    use = (index >= 0) & (index < half)
    return jnp.where(use, index, 0), use.astype(jnp.int32)


def local(
    queries,
    neighbour_keys,
    neighbour_values,
    residual,
    out_weight,
    drop_mask,
    norm_gain,
    norm_bias,
    neighbour_owner,
    neighbour_slot,
):
    peer_count = lax.axis_size("dp")
    side_count = lax.axis_size("tensor")
    half = peer_count // 2
    halves = [list(range(half)), list(range(half, peer_count))]
    across = [(i, (i + half) % peer_count) for i in range(peer_count)]
    by_plane = side_count == 2 and peer_count == 4 * PLANE
    blocks, per_block = neighbour_owner.shape
    rows, row_width = queries.shape
    span_len = rows // blocks
    here = lax.axis_index("dp").astype(jnp.int32)
    upper = here // half
    base = upper * half
    partner = lax.rem(here + half, peer_count)

    def exchange(x):
        return lax.all_to_all(
            x, "dp", split_axis=0, concat_axis=0, tiled=True, axis_index_groups=halves
        )

    def swap(x, by):
        return lax.ppermute(x, "dp", [(i, i ^ by) for i in range(peer_count)])

    def pinned(*values):
        return lax.optimization_barrier(values)

    def to_partner(x):
        return lax.ppermute(x, "dp", across)

    chunks = 2
    width = row_width // chunks
    far_first = to_partner(queries[:, :width])
    carried = shifted(queries[-1:], "dp", 1)
    owners = neighbour_owner.reshape(-1)
    slot_rows = neighbour_slot.reshape(-1)
    near_peers = base + jnp.arange(half, dtype=jnp.int32)
    near_out = spread(
        [queries], carried, *pick_requests(owners, slot_rows, near_peers, per_block),
        span_len, 0,
    )
    near_asked = exchange(near_out)
    far_carried = lax.ppermute(
        queries[-1:], "dp", [(i - 1, (i + half) % peer_count) for i in range(1, peer_count)]
    )
    requests = owners.shape[0]
    far_table = to_partner(
        jnp.pad(jnp.concatenate([owners, slot_rows]), (0, LANES - 2 * requests))[None, :]
    )
    (far_first,) = pinned(far_first)
    far_first, far_carried, far_table, held_queries, weight, _ = pinned(
        far_first, far_carried, far_table, queries, out_weight, near_out
    )
    far_owners = far_table[0, :requests]
    far_picked = pick_requests(
        far_owners, far_table[0, requests : 2 * requests], near_peers, per_block
    )

    def slots_of(asked):
        return asked[:, 0, -LANES].astype(jnp.int32)

    def answer(asked, tags, chunk, part, size, place, places, shared=None):
        valid = (tags > 0).astype(jnp.int32)
        slots = jnp.maximum(tags - 1, 0)
        return attend(
            asked, neighbour_keys, neighbour_values, valid, slots, width, chunk, part, size,
            place, places, shared,
        )

    wide = width + LANES
    far_second = to_partner(held_queries[:, width:])
    near_index, near_use = within(owners, base, half)
    far_index, far_use = within(far_owners, base, half)
    far_out = spread([far_first], far_carried, *far_picked, span_len, 0)
    far_asked = exchange(far_out)
    near_asked, _ = pinned(near_asked, far_out)
    near_tags = slots_of(near_asked)
    near_first = answer(near_asked, near_tags, 0, 0, width, 0, 2)
    near_second = answer(near_asked, near_tags, 1, 1, width, 1, 2)
    middle = row_width // 2
    near_swap = [swap(weight[:middle], PLANE)] if by_plane else []
    far_asked, far_second, weight, near_first, near_second, *near_swap = pinned(
        far_asked, far_second, weight, near_first, near_second, *near_swap
    )

    mixed = spread([far_second], far_carried, *far_picked, span_len, 1, near_first)
    next_asked = exchange(mixed)
    far_asked, near_second, _ = pinned(far_asked, near_second, mixed)
    far_weight = [to_partner(weight[:middle])] if by_plane else []
    far_tags = slots_of(far_asked)
    mixed = answer(far_asked, far_tags, 0, 0, wide, 0, 2, near_second)
    mixed, next_asked, weight, *far_weight = pinned(mixed, next_asked, weight, *far_weight)

    far_back = exchange(mixed)
    if by_plane:
        far_weight.append(to_partner(weight[middle:]))
    far_parts = answer(next_asked, far_tags, 1, 1, wide, 0, 1)
    far_back, far_parts, weight, *far_weight = pinned(far_back, far_parts, weight, *far_weight)
    near_back, next_back = next_asked, far_back

    far_merged = merge_far(far_back, 0, wide, far_index, far_use, blocks)
    far_home = to_partner(far_merged)
    far_back = exchange(far_parts)
    if by_plane:
        near_swap.append(swap(weight[middle:], PLANE))
    far_home, far_back, *near_swap = pinned(far_home, far_back, *near_swap)

    def plane_rows(moved):
        return [moved] + [swap(moved, by) for by in range(1, PLANE)] if by_plane else [moved]

    far_merged = merge_far(far_back, 0, wide, far_index, far_use, blocks)
    far_home, near_back, _ = pinned(far_home, near_back, far_merged)
    next_home = to_partner(far_merged)
    sources = plane_rows(
        merge_all(near_back, 0, wide, near_index, near_use, blocks, far_home)
    )
    far_swap = [swap(piece, PLANE) for piece in far_weight]
    count = len(sources)
    (next_home,) = pinned(next_home)
    next_home, next_back, *held = pinned(next_home, next_back, *sources, *far_swap)
    sources, far_swap = held[:count], held[count:]
    moved = merge_all(next_back, 1, wide, near_index, near_use, blocks, next_home)
    if by_plane:
        place = lax.rem(here, PLANE).reshape(1)
        stay = lax.axis_index("tensor").astype(jnp.int32).reshape(1)
        shards = [[weight], near_swap, far_weight, far_swap]
        line = jnp.stack(
            [here // PLANE, (here ^ PLANE) // PLANE, partner // PLANE, (partner ^ PLANE) // PLANE]
        )
        first_rows = [moved_part[rows : rows + 1] for moved_part in (sources[0], moved)]
        sources += plane_rows(moved)
        first_row = jnp.concatenate(first_rows, axis=1)
        below = functools.reduce(
            jnp.add,
            [
                lax.ppermute(
                    first_row,
                    "dp",
                    [(i + PLANE, i + at) for i in range(0, peer_count - PLANE, PLANE)],
                )
                for at in range(PLANE)
            ],
        )
        keep, send = project(sources, below, shards, place, stay)
        summed = add_cores(keep, lax.ppermute(send, "tensor", [(0, 1), (1, 0)]), place)
        branches = [summed[0]] + [swap(summed[by], by) for by in range(1, PLANE)]
    else:
        whole_weight = lax.all_gather(out_weight, "dp", axis=1, tiled=True)
        moved = jnp.concatenate([sources[0], moved], axis=1)
        below = shifted(moved[rows : rows + 1], "dp", -1)
        cross_rows = jnp.concatenate([moved[: rows - 1], below], axis=0)
        branch = jnp.dot(cross_rows, whole_weight, preferred_element_type=jnp.float32)
        branches = [
            lax.psum_scatter(
                branch.astype(jnp.bfloat16), "tensor", scatter_dimension=0, tiled=True
            )
        ]
        place = line = jnp.zeros((1,), jnp.int32)
    return tuple(
        add_norm(
            place, line, branches, out_weight.shape[1], residual, drop_mask, norm_gain, norm_bias
        )
    )


def solution(mesh):
    placed = (
        P("dp", "tensor"),
        P("dp", None, "tensor"),
        P("dp", None, "tensor"),
        P(("dp", "tensor"), None),
        P("tensor", "dp"),
        P(("dp", "tensor"), None),
        P(),
        P(),
        P("dp", None),
        P("dp", None),
    )
    return jax.shard_map(
        local,
        mesh=mesh,
        in_specs=placed,
        out_specs=(P(("dp", "tensor"), None), P(("dp", "tensor"), None)),
        check_vma=False,
    )
```

```python
import functools

import jax
import jax.numpy as jnp
from jax import lax
from jax.experimental import pallas as pl
from jax.experimental.pallas import tpu as pltpu
from jax.sharding import PartitionSpec as P

HEAD = 128
LANES = 128
MIB = 1024 * 1024
ROW_TILE = 16
PLANE = 4

keep_rate = 0.9
norm_eps = 1e-05


def shifted(x, axis, by):
    count = lax.axis_size(axis)
    pairs = [(i, i + by) for i in range(count) if 0 <= i + by < count]
    return lax.ppermute(x, axis, pairs)


def spread_kernel(count, column, block_ref, slot_ref, carried_ref, *refs):
    pieces = refs[:count]
    out_ref, moved, tags, sems = refs[-4:]
    peers, span_len, _ = out_ref.shape
    rows, piece_width = pieces[0].shape
    row_width = moved.shape[1]
    at = 0
    for piece in pieces:
        for start in range(0, piece_width, 512):
            size = min(512, piece_width - start)
            held = piece[:, start : start + size].astype(jnp.float32)
            rolled = pltpu.roll(held, 1, 0)
            first = lax.broadcasted_iota(jnp.int32, (rows, size), 0) == 0
            above = carried_ref[0:1, at : at + size].astype(jnp.float32)
            moved[:, at : at + size] = jnp.where(first, above, rolled).astype(moved.dtype)
            at += size

    def copies(peer):
        start = pl.multiple_of(block_ref[peer] * span_len, span_len)
        yield pltpu.make_async_copy(
            moved.at[pl.ds(start, span_len)],
            out_ref.at[peer, :, pl.ds(column, row_width)],
            sems.at[0, peer],
        )
        yield pltpu.make_async_copy(
            tags.at[peer],
            out_ref.at[peer, :, pl.ds(column + row_width, LANES)],
            sems.at[1, peer],
        )

    for peer in range(peers):
        slot = slot_ref[peer].astype(jnp.float32)
        tags[peer] = jnp.full((span_len, LANES), slot, jnp.float32).astype(tags.dtype)
        for copy in copies(peer):
            copy.start()
    for peer in range(peers):
        for copy in copies(peer):
            copy.wait()


def spread(pieces, carried, block_of_peer, slot_of_peer, span_len, chunk, shared=None):
    peers = block_of_peer.shape[0]
    rows, piece_width = pieces[0].shape
    row_width = piece_width * len(pieces)
    wide = row_width + LANES
    whole = wide if shared is None else shared.shape[2]
    extra = [] if shared is None else [shared]
    return pl.pallas_call(
        functools.partial(spread_kernel, len(pieces), whole - wide),
        grid_spec=pltpu.PrefetchScalarGridSpec(
            num_scalar_prefetch=2,
            grid=(1,),
            in_specs=[pl.BlockSpec((1, row_width), lambda i, *_: (0, chunk))]
            + [pl.BlockSpec((rows, piece_width), lambda i, *_: (0, 0))] * len(pieces)
            + [pl.BlockSpec(memory_space=pl.ANY)] * len(extra),
            out_specs=pl.BlockSpec(memory_space=pl.ANY),
            scratch_shapes=[
                pltpu.VMEM((rows, row_width), carried.dtype),
                pltpu.VMEM((peers, span_len, LANES), carried.dtype),
                pltpu.SemaphoreType.DMA((2, peers)),
            ],
        ),
        out_shape=jax.ShapeDtypeStruct((peers, span_len, whole), carried.dtype),
        input_output_aliases={3 + len(pieces): 0} if extra else {},
        compiler_params=pltpu.CompilerParams(vmem_limit_bytes=60 * MIB),
        name="spread_queries",
    )(block_of_peer, slot_of_peer, carried, *pieces, *extra)


def pack_levels(stats, heads):
    part = lax.broadcasted_iota(jnp.int32, stats.shape, 1) // heads
    high = stats.astype(jnp.bfloat16).astype(jnp.float32)
    rest = stats - high
    middle = rest.astype(jnp.bfloat16).astype(jnp.float32)
    low = rest - middle
    return jnp.where(part == 0, high, jnp.where(part == 1, middle, jnp.where(part == 2, low, 0.0)))


def unpack_levels(packed, heads):
    packed = packed.astype(jnp.float32)
    return (
        packed
        + pltpu.roll(packed, LANES - heads, 1)
        + pltpu.roll(packed, LANES - 2 * heads, 1)
    )


def attend_kernel(chunk, tag_ref, query_ref, key_ref, value_ref, *refs):
    out_ref, key_held, value_held, sems = refs[-4:]
    span_len = query_ref.shape[1]
    _, length, row_width = key_held.shape
    heads = row_width // HEAD
    group = min(heads, 4)
    peer = pl.program_id(0)
    peers = pl.num_programs(0)

    def tag_of(at):
        return tag_ref[at, 0:1, 0:1].astype(jnp.float32)[0, 0].astype(jnp.int32)

    def copies(at):
        buffer = lax.rem(at, 2)
        slot = jnp.maximum(tag_of(at) - 1, 0)
        for kind, (ref, held) in enumerate(((key_ref, key_held), (value_ref, value_held))):
            yield pltpu.make_async_copy(
                ref.at[slot, :, pl.ds(chunk * row_width, row_width)],
                held.at[buffer],
                sems.at[kind, buffer],
            )

    def fetch(at):
        for copy in copies(at):
            copy.start()

    following = jnp.minimum(peer + 1, peers - 1)

    @pl.when((peer == 0) & (tag_of(0) > 0))
    def _():
        fetch(0)

    @pl.when((peer + 1 < peers) & (tag_of(following) > 0))
    def _():
        fetch(following)

    @pl.when(tag_of(peer) > 0)
    def _():
        for copy in copies(peer):
            copy.wait()
        buffer = lax.rem(peer, 2)
        lane = lax.broadcasted_iota(jnp.int32, (span_len, LANES), 1)
        stats = jnp.zeros((span_len, LANES), jnp.float32)
        ones = jnp.ones((length, HEAD), jnp.bfloat16)
        for first in range(0, heads, group):
            chosen = range(first, first + group)
            cuts = [slice(head * HEAD, (head + 1) * HEAD) for head in chosen]
            scores = [
                lax.dot_general(
                    query_ref[0, :, cut],
                    key_held[buffer, :, cut],
                    (((1,), (1,)), ((), ())),
                    preferred_element_type=jnp.float32,
                )
                * HEAD ** (-0.5)
                for cut in cuts
            ]
            peaks = [jnp.max(score, axis=1, keepdims=True) for score in scores]
            raised = [
                jnp.exp(score - peak).astype(jnp.bfloat16) for score, peak in zip(scores, peaks)
            ]
            sums = [
                jnp.dot(
                    weight,
                    jnp.concatenate([value_held[buffer, :, cut], ones], axis=1),
                    preferred_element_type=jnp.float32,
                )
                for weight, cut in zip(raised, cuts)
            ]
            for head, cut, peak, both in zip(chosen, cuts, peaks, sums):
                total = both[:, HEAD:]
                out_ref[0, :, cut] = (both[:, :HEAD] / total).astype(out_ref.dtype)
                stats = jnp.where(lane % heads == head, peak + jnp.log(total), stats)
        out_ref[0, :, row_width:] = pack_levels(stats, heads).astype(out_ref.dtype)


def attend(asked, tags, keys, values, width, chunk, part, size, place, places, shared, weigh):
    peers, span_len, _ = asked.shape
    length = keys.shape[1]
    heads = width // HEAD
    wide = width + LANES
    tag_at = tags.shape[2] // LANES - 1
    extra = [] if shared is None else [shared]
    return pl.pallas_call(
        functools.partial(attend_kernel, chunk),
        grid=(peers,),
        in_specs=[
            pl.BlockSpec((peers, ROW_TILE, LANES), lambda i: (0, 0, tag_at)),
            pl.BlockSpec((1, span_len, size), lambda i: (i, 0, part)),
            pl.BlockSpec(memory_space=pl.ANY),
            pl.BlockSpec(memory_space=pl.ANY),
        ]
        + [pl.BlockSpec(memory_space=pl.ANY)] * len(extra),
        out_specs=pl.BlockSpec((1, span_len, wide), lambda i: (i, 0, place)),
        scratch_shapes=[
            pltpu.VMEM((2, length, width), keys.dtype),
            pltpu.VMEM((2, length, width), keys.dtype),
            pltpu.SemaphoreType.DMA((2, 2)),
        ],
        out_shape=jax.ShapeDtypeStruct((peers, span_len, places * wide), asked.dtype),
        input_output_aliases={4: 0} if extra else {},
        compiler_params=pltpu.CompilerParams(vmem_limit_bytes=58 * MIB),
        cost_estimate=pl.CostEstimate(
            flops=4 * weigh * peers * heads * span_len * length * HEAD,
            bytes_accessed=2 * weigh * peers * width * (2 * span_len + 2 * length),
            transcendentals=peers * heads * span_len * length,
        ),
        name="attend_blocks",
    )(tags, asked, keys, values, *extra)


def merge_block(uses, parts):
    row_width = parts[0].shape[2] - LANES
    heads = row_width // HEAD

    def masked(use, held, other):
        return held if use is None else jnp.where(use, held, other)

    levels = [
        masked(use, unpack_levels(ref[0, :, row_width:], heads), -1e30)
        for use, ref in zip(uses, parts)
    ]
    highest = functools.reduce(jnp.maximum, levels)
    weights = [jnp.exp(level - highest) for level in levels]
    total = functools.reduce(jnp.add, weights)
    weights = [weight / total for weight in weights]
    for head in range(heads):
        cut = slice(head * HEAD, (head + 1) * HEAD)
        merged = functools.reduce(
            jnp.add,
            [
                weight[:, head : head + 1]
                * masked(use, ref[0, :, cut].astype(jnp.float32), 0.0)
                for use, weight, ref in zip(uses, weights, parts)
            ],
        )
        yield cut, merged
    lane = lax.broadcasted_iota(jnp.int32, highest.shape, 1)
    level = jnp.where(lane < heads, highest + jnp.log(total), 0.0)
    level = level + pltpu.roll(level, heads, 1) + pltpu.roll(level, 2 * heads, 1)
    yield slice(row_width, row_width + LANES), pack_levels(level, heads)


def merge_far_kernel(picked, index_ref, use_ref, *refs):
    block = pl.program_id(0)
    uses = [use_ref[block * picked + r] > 0 for r in range(picked)]
    out_ref = refs[-1]
    for cut, merged in merge_block(uses, refs[:-1]):
        out_ref[0, :, cut] = merged.astype(out_ref.dtype)


def merge_all_kernel(picked, index_ref, use_ref, *refs):
    parts = refs[: picked + 1]
    out_ref, first_ref, kept = refs[-3:]
    span_len = parts[0].shape[1]
    rows, row_width = out_ref.shape
    rows -= ROW_TILE
    step = pl.program_id(0)
    block = rows // span_len - 1 - step
    uses = [use_ref[block * picked + r] > 0 for r in range(picked)] + [None]
    start = pl.multiple_of(block * span_len, span_len)
    last = lax.broadcasted_iota(jnp.int32, (span_len, HEAD), 0) == span_len - 1

    @pl.when(step == 0)
    def _():
        kept[...] = jnp.zeros_like(kept)

    for cut, merged in merge_block(uses, parts):
        if cut.start < row_width:
            moved = pltpu.roll(merged, span_len - 1, 0)
            moved = jnp.where(last, kept[0:1, cut], moved)
            out_ref[pl.ds(start, span_len), cut] = moved.astype(out_ref.dtype)
            kept[:, cut] = merged[:8]
            first = merged[:ROW_TILE].astype(out_ref.dtype)
            out_ref[rows:, cut] = first
            first_ref[:, cut] = first


def merge_far(parts, column, wide, index, use, blocks):
    span_len = parts.shape[1]
    picked = index.shape[0] // blocks
    specs = [
        pl.BlockSpec(
            (1, span_len, wide),
            functools.partial(lambda r, i, index, use: (index[i * picked + r], 0, column), r),
        )
        for r in range(picked)
    ]
    return pl.pallas_call(
        functools.partial(merge_far_kernel, picked),
        grid_spec=pltpu.PrefetchScalarGridSpec(
            num_scalar_prefetch=2,
            grid=(blocks,),
            in_specs=specs,
            out_specs=pl.BlockSpec((1, span_len, wide), lambda i, *_: (i, 0, 0)),
        ),
        out_shape=jax.ShapeDtypeStruct((blocks, span_len, wide), parts.dtype),
        compiler_params=pltpu.CompilerParams(vmem_limit_bytes=10 * MIB),
        name="merge_far",
    )(index, use, *([parts] * picked))


def merge_all(parts, column, wide, index, use, blocks, far):
    span_len = parts.shape[1]
    row_width = wide - LANES
    picked = index.shape[0] // blocks
    rows = blocks * span_len
    specs = [
        pl.BlockSpec(
            (1, span_len, wide),
            functools.partial(
                lambda r, i, index, use: (index[(blocks - 1 - i) * picked + r], 0, column), r
            ),
        )
        for r in range(picked)
    ]
    specs.append(pl.BlockSpec((1, span_len, wide), lambda i, *_: (blocks - 1 - i, 0, 0)))
    return pl.pallas_call(
        functools.partial(merge_all_kernel, picked),
        grid_spec=pltpu.PrefetchScalarGridSpec(
            num_scalar_prefetch=2,
            grid=(blocks,),
            in_specs=specs,
            out_specs=[
                pl.BlockSpec((rows + ROW_TILE, row_width), lambda i, *_: (0, 0)),
                pl.BlockSpec((ROW_TILE, row_width), lambda i, *_: (0, 0)),
            ],
            scratch_shapes=[pltpu.VMEM((8, row_width), jnp.float32)],
        ),
        out_shape=[
            jax.ShapeDtypeStruct((rows + ROW_TILE, row_width), parts.dtype),
            jax.ShapeDtypeStruct((ROW_TILE, row_width), parts.dtype),
        ],
        compiler_params=pltpu.CompilerParams(vmem_limit_bytes=10 * MIB),
        name="merge_all",
    )(index, use, *([parts] * picked), far)


def project_kernel(starts, place_ref, stay_ref, *refs):
    sources, belows = refs[:PLANE], refs[PLANE : 2 * PLANE]
    shards = len(starts)
    weights, before = refs[2 * PLANE : 2 * PLANE + shards], refs[2 * PLANE + shards : -7]
    keep_ref, send_ref, rows_ref, first_ref, held_ref, row_sems, weight_sems = refs[-7:]
    half = keep_ref.shape[0]
    part = half // PLANE
    _, width, tile = held_ref.shape

    def source_copies():
        for at, ref in enumerate(sources):
            member = place_ref[0] ^ at
            for side in range(2):
                to = pl.multiple_of(side * half + member * part, part)
                yield pltpu.make_async_copy(
                    ref.at[pl.ds(side * part, part)],
                    rows_ref.at[pl.ds(to, part)],
                    row_sems.at[at, side],
                )
            to = pl.multiple_of(member * ROW_TILE, ROW_TILE)
            yield pltpu.make_async_copy(
                ref.at[pl.ds(2 * part, ROW_TILE)],
                first_ref.at[pl.ds(to, ROW_TILE)],
                row_sems.at[at, 2],
            )

    def weight_copy(shard):
        return pltpu.make_async_copy(
            weights[shard].at[pl.ds(starts[shard], width)],
            held_ref.at[shard],
            weight_sems.at[shard],
        )

    for copy in source_copies():
        copy.start()
    for shard in range(shards):
        weight_copy(shard).start()
    for copy in source_copies():
        copy.wait()
    last = lax.broadcasted_iota(jnp.int32, (ROW_TILE, width), 0) == ROW_TILE - 1
    for member in range(PLANE):
        if member < PLANE - 1:
            at = (member + 1) * ROW_TILE
            below = first_ref[at : at + ROW_TILE].astype(jnp.float32)
        else:
            below = functools.reduce(jnp.add, [ref[...].astype(jnp.float32) for ref in belows])
        end = half + (member + 1) * part
        held = rows_ref[end - ROW_TILE : end].astype(jnp.float32)
        rows_ref[end - ROW_TILE : end] = jnp.where(last, below[0:1], held).astype(rows_ref.dtype)
    stay = pl.multiple_of(stay_ref[0] * half, half)
    go = pl.multiple_of((1 - stay_ref[0]) * half, half)
    for shard in range(shards):
        weight_copy(shard).wait()
        cut = slice(shard * tile, (shard + 1) * tile)
        for at, (start, ref) in enumerate(((stay, keep_ref), (go, send_ref))):
            result = jnp.dot(
                rows_ref[pl.ds(start, half)], held_ref[shard], preferred_element_type=jnp.float32
            )
            if before:
                result = result + before[at][:, cut]
            ref[:, cut] = result.astype(ref.dtype)


def project(sources, belows, weights, place, stay, before, kind):
    height, width = sources[0].shape
    rows = PLANE * (height - ROW_TILE)
    shards = len(weights)
    starts = [start for _, start in weights]
    tile = weights[0][0].shape[1]
    columns = shards * tile
    half = rows // 2
    row_spec = pl.BlockSpec((ROW_TILE, width), lambda i, *_: (0, 0))
    half_spec = pl.BlockSpec((half, columns), lambda i, *_: (0, 0))
    return pl.pallas_call(
        functools.partial(project_kernel, starts),
        grid_spec=pltpu.PrefetchScalarGridSpec(
            num_scalar_prefetch=2,
            grid=(1,),
            in_specs=[pl.BlockSpec(memory_space=pl.ANY)] * PLANE
            + [row_spec] * PLANE
            + [pl.BlockSpec(memory_space=pl.ANY)] * shards
            + [half_spec] * len(before),
            out_specs=[half_spec] * 2,
            scratch_shapes=[
                pltpu.VMEM((rows, width), sources[0].dtype),
                pltpu.VMEM((PLANE * ROW_TILE, width), sources[0].dtype),
                pltpu.VMEM((shards, width, tile), sources[0].dtype),
                pltpu.SemaphoreType.DMA((PLANE, 3)),
                pltpu.SemaphoreType.DMA((shards,)),
            ],
        ),
        out_shape=[jax.ShapeDtypeStruct((half, columns), kind)] * 2,
        compiler_params=pltpu.CompilerParams(vmem_limit_bytes=28 * MIB),
        cost_estimate=pl.CostEstimate(
            flops=2 * rows * width * columns,
            bytes_accessed=2 * width * (rows + columns) + 8 * rows * columns,
            transcendentals=0,
        ),
        name="project_rows",
    )(place, stay, *sources, *belows, *[weight for weight, _ in weights], *before)


def add_kernel(place_ref, keep_ref, other_ref, *outs):
    for at, ref in enumerate(outs):
        member = place_ref[0] ^ at
        ref[...] = (
            keep_ref[member].astype(jnp.float32) + other_ref[member].astype(jnp.float32)
        ).astype(ref.dtype)


def add_cores(keep, other, place):
    half, columns = keep.shape
    part = half // PLANE
    tile = min(columns, 512)
    folded = (PLANE, part, columns)
    return pl.pallas_call(
        add_kernel,
        grid_spec=pltpu.PrefetchScalarGridSpec(
            num_scalar_prefetch=1,
            grid=(columns // tile,),
            in_specs=[pl.BlockSpec((PLANE, part, tile), lambda i, *_: (0, 0, i))] * 2,
            out_specs=[pl.BlockSpec((part, tile), lambda i, *_: (0, i))] * PLANE,
        ),
        out_shape=[jax.ShapeDtypeStruct((part, columns), keep.dtype)] * PLANE,
        compiler_params=pltpu.CompilerParams(vmem_limit_bytes=10 * MIB),
        name="add_cores",
    )(place, keep.reshape(folded), other.reshape(folded))


def norm_kernel(strip, place_ref, line_ref, *refs):
    branches = refs[:-7]
    residual_ref, mask_ref, gain_ref, bias_ref, next_ref, normed_ref, branch_ref = refs[-7:]
    if len(branches) == 1:
        branch_ref[...] = branches[0][...].astype(jnp.float32)
    else:
        for at, ref in enumerate(branches):
            member = place_ref[0] ^ at
            for shard in range(ref.shape[1] // strip):
                to = pl.multiple_of((line_ref[shard] * PLANE + member) * strip, strip)
                branch_ref[:, pl.ds(to, strip)] = ref[
                    :, shard * strip : (shard + 1) * strip
                ].astype(jnp.float32)
    keep_scale = mask_ref[...].astype(jnp.float32) * (1.0 / keep_rate)
    stream = residual_ref[...].astype(jnp.float32) + keep_scale * branch_ref[...]
    centre = jnp.mean(stream, axis=1, keepdims=True)
    moved = stream - centre
    spread_of = jnp.mean(jnp.square(moved), axis=1, keepdims=True)
    normed = moved * lax.rsqrt(spread_of + norm_eps) * gain_ref[...] + bias_ref[...]
    next_ref[...] = stream.astype(next_ref.dtype)
    normed_ref[...] = normed.astype(normed_ref.dtype)


def add_norm(place, line, branches, strip, residual, drop_mask, gain, bias):
    rows, columns = residual.shape
    tile = min(32, rows)
    row_spec = pl.BlockSpec((tile, columns), lambda i, *_: (i, 0))
    branch_spec = pl.BlockSpec((tile, branches[0].shape[1]), lambda i, *_: (i, 0))
    flat_spec = pl.BlockSpec((1, columns), lambda i, *_: (0, 0))
    return pl.pallas_call(
        functools.partial(norm_kernel, strip),
        grid_spec=pltpu.PrefetchScalarGridSpec(
            num_scalar_prefetch=2,
            grid=(rows // tile,),
            in_specs=[branch_spec] * len(branches) + [row_spec, row_spec, flat_spec, flat_spec],
            out_specs=[row_spec, row_spec],
            scratch_shapes=[pltpu.VMEM((tile, columns), jnp.float32)],
        ),
        out_shape=[jax.ShapeDtypeStruct((rows, columns), residual.dtype)] * 2,
        compiler_params=pltpu.CompilerParams(vmem_limit_bytes=20 * MIB),
        name="add_norm",
    )(place, line, *branches, residual, drop_mask, gain[None], bias[None])


def pick_requests(owners, slots, peers, per_block):
    selector = owners[None, :] == peers[:, None]
    pair_block = jnp.arange(owners.shape[0], dtype=jnp.int32) // per_block
    return (
        jnp.sum(jnp.where(selector, pair_block[None, :], 0), axis=1),
        jnp.sum(jnp.where(selector, slots[None, :] + 1, 0), axis=1),
    )


def within(owners, base, half):
    index = owners - base
    use = (index >= 0) & (index < half)
    return jnp.where(use, index, 0), use.astype(jnp.int32)


def local(
    queries,
    neighbour_keys,
    neighbour_values,
    residual,
    out_weight,
    drop_mask,
    norm_gain,
    norm_bias,
    neighbour_owner,
    neighbour_slot,
):
    peer_count = lax.axis_size("dp")
    side_count = lax.axis_size("tensor")
    half = peer_count // 2
    halves = [list(range(half)), list(range(half, peer_count))]
    across = [(i, (i + half) % peer_count) for i in range(peer_count)]
    by_plane = side_count == 2 and peer_count == 4 * PLANE
    blocks, per_block = neighbour_owner.shape
    rows, row_width = queries.shape
    span_len = rows // blocks
    here = lax.axis_index("dp").astype(jnp.int32)
    upper = here // half
    base = upper * half
    partner = lax.rem(here + half, peer_count)

    def exchange(x):
        return lax.all_to_all(
            x, "dp", split_axis=0, concat_axis=0, tiled=True, axis_index_groups=halves
        )

    def swap(x, by):
        return lax.ppermute(x, "dp", [(i, i ^ by) for i in range(peer_count)])

    def pinned(*values):
        return lax.optimization_barrier(values)

    def to_partner(x):
        return lax.ppermute(x, "dp", across)

    chunks = 2
    width = row_width // chunks
    far_first = to_partner(queries[:, :width])
    middle = row_width // 2
    carried = shifted(queries[-1:], "dp", 1)
    owners = neighbour_owner.reshape(-1)
    slot_rows = neighbour_slot.reshape(-1)
    near_peers = base + jnp.arange(half, dtype=jnp.int32)
    near_out = spread(
        [queries], carried, *pick_requests(owners, slot_rows, near_peers, per_block),
        span_len, 0,
    )
    near_asked = exchange(near_out)
    far_carried = lax.ppermute(
        queries[-1:], "dp", [(i - 1, (i + half) % peer_count) for i in range(1, peer_count)]
    )
    requests = owners.shape[0]
    far_table = to_partner(
        jnp.pad(jnp.concatenate([owners, slot_rows]), (0, LANES - 2 * requests))[None, :]
    )
    far_first, far_carried, far_table, second, weight, _ = pinned(
        far_first, far_carried, far_table, queries[:, width:], out_weight, near_out
    )
    far_owners = far_table[0, :requests]
    far_picked = pick_requests(
        far_owners, far_table[0, requests : 2 * requests], near_peers, per_block
    )

    def answer(asked, tags, chunk, part, size, place, places, shared=None, weigh=1):
        return attend(
            asked, tags, neighbour_keys, neighbour_values, width, chunk, part, size,
            place, places, shared, weigh,
        )

    wide = width + LANES
    far_second = to_partner(second)
    near_index, near_use = within(owners, base, half)
    far_index, far_use = within(far_owners, base, half)
    far_out = spread([far_first], far_carried, *far_picked, span_len, 0)
    far_asked = exchange(far_out)
    near_asked, _ = pinned(near_asked, far_out)
    near_first = answer(near_asked, near_asked, 0, 0, width, 0, 2)
    near_second = answer(near_asked, near_asked, 1, 1, width, 1, 2)
    (
        far_asked, far_second, near_first, near_second, near_index, near_use, far_index,
        far_use, weight, *weight_halves,
    ) = pinned(
        far_asked, far_second, near_first, near_second, near_index, near_use, far_index,
        far_use, weight, weight[:middle], weight[middle:],
    )

    mixed = spread([far_second], far_carried, *far_picked, span_len, 1, near_first)
    next_asked = exchange(mixed)
    far_weight = [to_partner(weight_halves[0])] if by_plane else []
    tags, near_second, _, *far_weight = pinned(far_asked, near_second, mixed, *far_weight)
    mixed = answer(tags, tags, 0, 0, wide, 0, 2, near_second, weigh=16)
    mixed, next_asked, weight_half = pinned(mixed, next_asked, weight_halves[1])

    far_back = exchange(mixed)
    if by_plane:
        far_weight.append(to_partner(weight_half))
    next_asked, *far_weight = pinned(next_asked, *far_weight)
    far_parts = answer(next_asked, tags, 1, 1, wide, 0, 1, weigh=16)
    far_back, far_parts = pinned(far_back, far_parts)
    near_back, next_back = next_asked, far_back

    far_merged = merge_far(far_back, 0, wide, far_index, far_use, blocks)
    far_home = to_partner(far_merged)
    far_back = exchange(far_parts)
    far_home, far_back, *far_weight = pinned(far_home, far_back, *far_weight)

    def to_plane(moved, first):
        if not by_plane:
            return [moved, first]
        down = [
            lax.ppermute(
                first, "dp", [(i + PLANE, i + at) for i in range(0, peer_count - PLANE, PLANE)]
            )
            for at in range(PLANE)
        ]
        return [moved] + [swap(moved, by) for by in range(1, PLANE)] + down

    far_merged = merge_far(far_back, 0, wide, far_index, far_use, blocks)
    far_home, near_back, far_merged, near_half, *far_weight = pinned(
        far_home, near_back, far_merged, weight_halves[0], *far_weight
    )
    next_home = to_partner(far_merged)
    sources = to_plane(*merge_all(near_back, 0, wide, near_index, near_use, blocks, far_home))
    swaps = [swap(far_weight[0], PLANE), swap(near_half, PLANE)] if by_plane else []
    count = len(sources)
    (next_home,) = pinned(next_home)
    next_home, next_back, weight_half, *held = pinned(
        next_home, next_back, weight_halves[1], *sources, *swaps, *far_weight
    )
    sources, held = held[:count], held[count:]
    moved, first = merge_all(next_back, 1, wide, near_index, near_use, blocks, next_home)
    if by_plane:
        place = lax.rem(here, PLANE).reshape(1)
        stay = lax.axis_index("tensor").astype(jnp.int32).reshape(1)
        far_swap, near_swap, *far_weight = held
        moved, first, weight_half, far_half = pinned(moved, first, weight_half, far_weight[1])
        next_sources = to_plane(moved, first)
        near_next, far_next = swap(weight_half, PLANE), swap(far_half, PLANE)
        done = project(
            sources[:PLANE], sources[PLANE:],
            [(weight, 0), (near_swap, 0), (far_weight[0], 0), (far_swap, 0)],
            place, stay, [], jnp.float32,
        )
        keep, send = project(
            next_sources[:PLANE], next_sources[PLANE:],
            [(weight, middle), (near_next, 0), (far_half, 0), (far_next, 0)],
            place, stay, done, moved.dtype,
        )
        line = jnp.stack(
            [here // PLANE, (here ^ PLANE) // PLANE, partner // PLANE, (partner ^ PLANE) // PLANE]
        )
        summed = add_cores(keep, lax.ppermute(send, "tensor", [(0, 1), (1, 0)]), place)
        branches = [summed[0]] + [swap(summed[by], by) for by in range(1, PLANE)]
    else:
        whole_weight = lax.all_gather(out_weight, "dp", axis=1, tiled=True)
        moved = jnp.concatenate([sources[0], moved], axis=1)
        below = shifted(jnp.concatenate([sources[1], first], axis=1)[:1], "dp", -1)
        cross_rows = jnp.concatenate([moved[: rows - 1], below], axis=0)
        branch = jnp.dot(cross_rows, whole_weight, preferred_element_type=jnp.float32)
        branches = [
            lax.psum_scatter(
                branch.astype(jnp.bfloat16), "tensor", scatter_dimension=0, tiled=True
            )
        ]
        place = line = jnp.zeros((1,), jnp.int32)
    return tuple(
        add_norm(
            place, line, branches, out_weight.shape[1], residual, drop_mask, norm_gain, norm_bias
        )
    )


def solution(mesh):
    placed = (
        P("dp", "tensor"),
        P("dp", None, "tensor"),
        P("dp", None, "tensor"),
        P(("dp", "tensor"), None),
        P("tensor", "dp"),
        P(("dp", "tensor"), None),
        P(),
        P(),
        P("dp", None),
        P("dp", None),
    )
    return jax.shard_map(
        local,
        mesh=mesh,
        in_specs=placed,
        out_specs=(P(("dp", "tensor"), None), P(("dp", "tensor"), None)),
        check_vma=False,
    )
```

```python
import functools

import jax
import jax.numpy as jnp
from jax import lax
from jax.experimental import pallas as pl
from jax.experimental.pallas import tpu as pltpu
from jax.sharding import PartitionSpec as P

HEAD = 128
LANES = 128
MIB = 1024 * 1024
ROW_TILE = 16
PLANE = 4

keep_rate = 0.9
norm_eps = 1e-05


def shifted(x, axis, by):
    count = lax.axis_size(axis)
    pairs = [(i, i + by) for i in range(count) if 0 <= i + by < count]
    return lax.ppermute(x, axis, pairs)


def spread_kernel(count, column, block_ref, slot_ref, carried_ref, *refs):
    pieces = refs[:count]
    out_ref, moved, tags, sems = refs[-4:]
    peers, span_len, _ = out_ref.shape
    rows, piece_width = pieces[0].shape
    row_width = moved.shape[1]
    at = 0
    for piece in pieces:
        for start in range(0, piece_width, 512):
            size = min(512, piece_width - start)
            held = piece[:, start : start + size].astype(jnp.float32)
            rolled = pltpu.roll(held, 1, 0)
            first = lax.broadcasted_iota(jnp.int32, (rows, size), 0) == 0
            above = carried_ref[0:1, at : at + size].astype(jnp.float32)
            moved[:, at : at + size] = jnp.where(first, above, rolled).astype(moved.dtype)
            at += size

    def copies(peer):
        start = pl.multiple_of(block_ref[peer] * span_len, span_len)
        yield pltpu.make_async_copy(
            moved.at[pl.ds(start, span_len)],
            out_ref.at[peer, :, pl.ds(column, row_width)],
            sems.at[0, peer],
        )
        yield pltpu.make_async_copy(
            tags.at[peer],
            out_ref.at[peer, :, pl.ds(column + row_width, LANES)],
            sems.at[1, peer],
        )

    for peer in range(peers):
        slot = slot_ref[peer].astype(jnp.float32)
        tags[peer] = jnp.full((span_len, LANES), slot, jnp.float32).astype(tags.dtype)
        for copy in copies(peer):
            copy.start()
    for peer in range(peers):
        for copy in copies(peer):
            copy.wait()


def spread(pieces, carried, block_of_peer, slot_of_peer, span_len, chunk, shared=None):
    peers = block_of_peer.shape[0]
    rows, piece_width = pieces[0].shape
    row_width = piece_width * len(pieces)
    wide = row_width + LANES
    whole = wide if shared is None else shared.shape[2]
    extra = [] if shared is None else [shared]
    return pl.pallas_call(
        functools.partial(spread_kernel, len(pieces), whole - wide),
        grid_spec=pltpu.PrefetchScalarGridSpec(
            num_scalar_prefetch=2,
            grid=(1,),
            in_specs=[pl.BlockSpec((1, row_width), lambda i, *_: (0, chunk))]
            + [pl.BlockSpec((rows, piece_width), lambda i, *_: (0, 0))] * len(pieces)
            + [pl.BlockSpec(memory_space=pl.ANY)] * len(extra),
            out_specs=pl.BlockSpec(memory_space=pl.ANY),
            scratch_shapes=[
                pltpu.VMEM((rows, row_width), carried.dtype),
                pltpu.VMEM((peers, span_len, LANES), carried.dtype),
                pltpu.SemaphoreType.DMA((2, peers)),
            ],
        ),
        out_shape=jax.ShapeDtypeStruct((peers, span_len, whole), carried.dtype),
        input_output_aliases={3 + len(pieces): 0} if extra else {},
        compiler_params=pltpu.CompilerParams(vmem_limit_bytes=(60 if extra else 10) * MIB),
        name="spread_queries",
    )(block_of_peer, slot_of_peer, carried, *pieces, *extra)


def pack_levels(stats, heads):
    part = lax.broadcasted_iota(jnp.int32, stats.shape, 1) // heads
    high = stats.astype(jnp.bfloat16).astype(jnp.float32)
    rest = stats - high
    middle = rest.astype(jnp.bfloat16).astype(jnp.float32)
    low = rest - middle
    return jnp.where(part == 0, high, jnp.where(part == 1, middle, jnp.where(part == 2, low, 0.0)))


def unpack_levels(packed, heads):
    packed = packed.astype(jnp.float32)
    return (
        packed
        + pltpu.roll(packed, LANES - heads, 1)
        + pltpu.roll(packed, LANES - 2 * heads, 1)
    )


def attend_kernel(chunk, tag_ref, query_ref, key_ref, value_ref, *refs):
    out_ref, key_held, value_held, sems = refs[-4:]
    span_len = query_ref.shape[1]
    _, length, row_width = key_held.shape
    heads = row_width // HEAD
    group = min(heads, 4)
    peer = pl.program_id(0)
    peers = pl.num_programs(0)

    def tag_of(at):
        return tag_ref[at, 0:1, 0:1].astype(jnp.float32)[0, 0].astype(jnp.int32)

    def copies(at):
        buffer = lax.rem(at, 2)
        slot = jnp.maximum(tag_of(at) - 1, 0)
        for kind, (ref, held) in enumerate(((key_ref, key_held), (value_ref, value_held))):
            yield pltpu.make_async_copy(
                ref.at[slot, :, pl.ds(chunk * row_width, row_width)],
                held.at[buffer],
                sems.at[kind, buffer],
            )

    def fetch(at):
        for copy in copies(at):
            copy.start()

    following = jnp.minimum(peer + 1, peers - 1)

    @pl.when((peer == 0) & (tag_of(0) > 0))
    def _():
        fetch(0)

    @pl.when((peer + 1 < peers) & (tag_of(following) > 0))
    def _():
        fetch(following)

    @pl.when(tag_of(peer) > 0)
    def _():
        for copy in copies(peer):
            copy.wait()
        buffer = lax.rem(peer, 2)
        lane = lax.broadcasted_iota(jnp.int32, (span_len, LANES), 1)
        stats = jnp.zeros((span_len, LANES), jnp.float32)
        ones = jnp.ones((length, HEAD), jnp.bfloat16)
        for first in range(0, heads, group):
            chosen = range(first, first + group)
            cuts = [slice(head * HEAD, (head + 1) * HEAD) for head in chosen]
            scores = [
                lax.dot_general(
                    query_ref[0, :, cut],
                    key_held[buffer, :, cut],
                    (((1,), (1,)), ((), ())),
                    preferred_element_type=jnp.float32,
                )
                * HEAD ** (-0.5)
                for cut in cuts
            ]
            peaks = [jnp.max(score, axis=1, keepdims=True) for score in scores]
            raised = [
                jnp.exp(score - peak).astype(jnp.bfloat16) for score, peak in zip(scores, peaks)
            ]
            sums = [
                jnp.dot(
                    weight,
                    jnp.concatenate([value_held[buffer, :, cut], ones], axis=1),
                    preferred_element_type=jnp.float32,
                )
                for weight, cut in zip(raised, cuts)
            ]
            for head, cut, peak, both in zip(chosen, cuts, peaks, sums):
                total = both[:, HEAD:]
                out_ref[0, :, cut] = (both[:, :HEAD] / total).astype(out_ref.dtype)
                stats = jnp.where(lane % heads == head, peak + jnp.log(total), stats)
        out_ref[0, :, row_width:] = pack_levels(stats, heads).astype(out_ref.dtype)


def attend(asked, tags, keys, values, width, chunk, part, size, place, places, shared):
    peers, span_len, _ = asked.shape
    length = keys.shape[1]
    heads = width // HEAD
    wide = width + LANES
    tag_at = tags.shape[2] // LANES - 1
    extra = [] if shared is None else [shared]
    return pl.pallas_call(
        functools.partial(attend_kernel, chunk),
        grid=(peers,),
        in_specs=[
            pl.BlockSpec((peers, ROW_TILE, LANES), lambda i: (0, 0, tag_at)),
            pl.BlockSpec((1, span_len, size), lambda i: (i, 0, part)),
            pl.BlockSpec(memory_space=pl.ANY),
            pl.BlockSpec(memory_space=pl.ANY),
        ]
        + [pl.BlockSpec(memory_space=pl.ANY)] * len(extra),
        out_specs=pl.BlockSpec((1, span_len, wide), lambda i: (i, 0, place)),
        scratch_shapes=[
            pltpu.VMEM((2, length, width), keys.dtype),
            pltpu.VMEM((2, length, width), keys.dtype),
            pltpu.SemaphoreType.DMA((2, 2)),
        ],
        out_shape=jax.ShapeDtypeStruct((peers, span_len, places * wide), asked.dtype),
        input_output_aliases={4: 0} if extra else {},
        compiler_params=pltpu.CompilerParams(vmem_limit_bytes=58 * MIB),
        cost_estimate=pl.CostEstimate(
            flops=4 * peers * heads * span_len * length * HEAD,
            bytes_accessed=2 * peers * width * (2 * span_len + 2 * length),
            transcendentals=peers * heads * span_len * length,
        ),
        name="attend_blocks",
    )(tags, asked, keys, values, *extra)


def merge_block(uses, parts):
    row_width = parts[0].shape[2] - LANES
    heads = row_width // HEAD

    def masked(use, held, other):
        return held if use is None else jnp.where(use, held, other)

    levels = [
        masked(use, unpack_levels(ref[0, :, row_width:], heads), -1e30)
        for use, ref in zip(uses, parts)
    ]
    highest = functools.reduce(jnp.maximum, levels)
    weights = [jnp.exp(level - highest) for level in levels]
    total = functools.reduce(jnp.add, weights)
    weights = [weight / total for weight in weights]
    for head in range(heads):
        cut = slice(head * HEAD, (head + 1) * HEAD)
        merged = functools.reduce(
            jnp.add,
            [
                weight[:, head : head + 1]
                * masked(use, ref[0, :, cut].astype(jnp.float32), 0.0)
                for use, weight, ref in zip(uses, weights, parts)
            ],
        )
        yield cut, merged
    lane = lax.broadcasted_iota(jnp.int32, highest.shape, 1)
    level = jnp.where(lane < heads, highest + jnp.log(total), 0.0)
    level = level + pltpu.roll(level, heads, 1) + pltpu.roll(level, 2 * heads, 1)
    yield slice(row_width, row_width + LANES), pack_levels(level, heads)


def merge_far_kernel(picked, index_ref, use_ref, *refs):
    block = pl.program_id(0)
    uses = [use_ref[block * picked + r] > 0 for r in range(picked)]
    out_ref = refs[-1]
    for cut, merged in merge_block(uses, refs[:-1]):
        out_ref[0, :, cut] = merged.astype(out_ref.dtype)


def merge_all_kernel(picked, earlier, index_ref, use_ref, *refs):
    parts = refs[: picked + 1]
    out_ref, first_ref, kept = refs[-3:]
    span_len = parts[0].shape[1]
    rows, row_width = out_ref.shape
    rows -= ROW_TILE
    step = pl.program_id(0)
    block = rows // span_len - 1 - step
    uses = [use_ref[block * picked + r] > 0 for r in range(picked)] + [None]
    start = pl.multiple_of(block * span_len, span_len)
    last = lax.broadcasted_iota(jnp.int32, (span_len, HEAD), 0) == span_len - 1
    at = first_ref.shape[1] - row_width

    @pl.when(step == 0)
    def _():
        kept[...] = jnp.zeros_like(kept)
        if earlier:
            first_ref[:, :at] = refs[picked + 1][...]

    for cut, merged in merge_block(uses, parts):
        if cut.start < row_width:
            moved = pltpu.roll(merged, span_len - 1, 0)
            moved = jnp.where(last, kept[0:1, cut], moved)
            out_ref[pl.ds(start, span_len), cut] = moved.astype(out_ref.dtype)
            kept[:, cut] = merged[:8]
            first = merged[:ROW_TILE].astype(out_ref.dtype)
            out_ref[rows:, cut] = first
            first_ref[:, at + cut.start : at + cut.stop] = first


def merge_far(parts, column, wide, index, use, blocks):
    span_len = parts.shape[1]
    picked = index.shape[0] // blocks
    specs = [
        pl.BlockSpec(
            (1, span_len, wide),
            functools.partial(lambda r, i, index, use: (index[i * picked + r], 0, column), r),
        )
        for r in range(picked)
    ]
    return pl.pallas_call(
        functools.partial(merge_far_kernel, picked),
        grid_spec=pltpu.PrefetchScalarGridSpec(
            num_scalar_prefetch=2,
            grid=(blocks,),
            in_specs=specs,
            out_specs=pl.BlockSpec((1, span_len, wide), lambda i, *_: (i, 0, 0)),
        ),
        out_shape=jax.ShapeDtypeStruct((blocks, span_len, wide), parts.dtype),
        compiler_params=pltpu.CompilerParams(vmem_limit_bytes=10 * MIB),
        name="merge_far",
    )(index, use, *([parts] * picked))


def merge_all(parts, column, wide, index, use, blocks, far, earlier=None):
    span_len = parts.shape[1]
    row_width = wide - LANES
    picked = index.shape[0] // blocks
    rows = blocks * span_len
    specs = [
        pl.BlockSpec(
            (1, span_len, wide),
            functools.partial(
                lambda r, i, index, use: (index[(blocks - 1 - i) * picked + r], 0, column), r
            ),
        )
        for r in range(picked)
    ]
    specs.append(pl.BlockSpec((1, span_len, wide), lambda i, *_: (blocks - 1 - i, 0, 0)))
    extra = [] if earlier is None else [earlier]
    first_width = row_width * (1 + len(extra))
    specs += [pl.BlockSpec((ROW_TILE, row_width), lambda i, *_: (0, 0))] * len(extra)
    return pl.pallas_call(
        functools.partial(merge_all_kernel, picked, len(extra)),
        grid_spec=pltpu.PrefetchScalarGridSpec(
            num_scalar_prefetch=2,
            grid=(blocks,),
            in_specs=specs,
            out_specs=[
                pl.BlockSpec((rows + ROW_TILE, row_width), lambda i, *_: (0, 0)),
                pl.BlockSpec((ROW_TILE, first_width), lambda i, *_: (0, 0)),
            ],
            scratch_shapes=[pltpu.VMEM((8, row_width), jnp.float32)],
        ),
        out_shape=[
            jax.ShapeDtypeStruct((rows + ROW_TILE, row_width), parts.dtype),
            jax.ShapeDtypeStruct((ROW_TILE, first_width), parts.dtype),
        ],
        compiler_params=pltpu.CompilerParams(vmem_limit_bytes=10 * MIB),
        name="merge_all",
    )(index, use, *([parts] * picked), far, *extra)


def project_kernel(starts, place_ref, stay_ref, *refs):
    sources, refs = refs[:PLANE], refs[PLANE:]
    last_part = len(starts) > PLANE
    belows, refs = (refs[:PLANE], refs[PLANE:]) if last_part else ([], refs)
    weights, before = refs[: len(starts)], refs[len(starts) : -7]
    keep_ref, send_ref, rows_ref, first_ref, held_ref, row_sems, weight_sems = refs[-7:]
    half = keep_ref.shape[0]
    part = half // PLANE
    _, width, tile = held_ref.shape

    def source_copies():
        for at, ref in enumerate(sources):
            member = place_ref[0] ^ at
            for side in range(2):
                to = pl.multiple_of(side * half + member * part, part)
                yield pltpu.make_async_copy(
                    ref.at[pl.ds(side * part, part)],
                    rows_ref.at[pl.ds(to, part)],
                    row_sems.at[at, side],
                )
            to = pl.multiple_of(member * ROW_TILE, ROW_TILE)
            yield pltpu.make_async_copy(
                ref.at[pl.ds(2 * part, ROW_TILE)],
                first_ref.at[pl.ds(to, ROW_TILE)],
                row_sems.at[at, 2],
            )

    def weight_copy(at):
        return pltpu.make_async_copy(
            weights[at].at[pl.ds(starts[at], width)], held_ref.at[at], weight_sems.at[at]
        )

    for copy in source_copies():
        copy.start()
    for at in range(len(starts)):
        weight_copy(at).start()
    for copy in source_copies():
        copy.wait()
    last = lax.broadcasted_iota(jnp.int32, (ROW_TILE, width), 0) == ROW_TILE - 1
    for member in range(PLANE):
        at = (member + 1) % PLANE * ROW_TILE
        below = first_ref[at : at + ROW_TILE].astype(jnp.float32)[0:1]
        if member == PLANE - 1:
            below = jnp.zeros_like(below)
        end = half + (member + 1) * part
        held = rows_ref[end - ROW_TILE : end].astype(jnp.float32)
        rows_ref[end - ROW_TILE : end] = jnp.where(last, below, held).astype(rows_ref.dtype)
    if last_part:
        below = functools.reduce(jnp.add, [ref[...].astype(jnp.float32) for ref in belows])
        below = below.astype(rows_ref.dtype)
    stay = pl.multiple_of(stay_ref[0] * half, half)
    go = pl.multiple_of((1 - stay_ref[0]) * half, half)
    for shard in range(PLANE):
        weight_copy(shard).wait()
        if last_part:
            weight_copy(PLANE + shard).wait()
        cut = slice(shard * tile, (shard + 1) * tile)
        for at, (start, ref) in enumerate(((stay, keep_ref), (go, send_ref))):
            result = jnp.dot(
                rows_ref[pl.ds(start, half)], held_ref[shard], preferred_element_type=jnp.float32
            )
            if last_part:
                result = result + before[at][:, cut]
            ref[:, cut] = result.astype(ref.dtype)
        if last_part:
            row = functools.reduce(
                jnp.add,
                [
                    jnp.dot(
                        below[:, side * width : (side + 1) * width],
                        held_ref[at],
                        preferred_element_type=jnp.float32,
                    )
                    for side, at in ((0, PLANE + shard), (1, shard))
                ],
            )[0:1]
            at_end = lax.broadcasted_iota(jnp.int32, (ROW_TILE, tile), 0) == ROW_TILE - 1
            for upper, ref in ((stay_ref[0] > 0, keep_ref), (stay_ref[0] == 0, send_ref)):

                @pl.when(upper)
                def _():
                    held = ref[half - ROW_TILE :, cut].astype(jnp.float32)
                    ref[half - ROW_TILE :, cut] = jnp.where(at_end, row, held).astype(ref.dtype)


def project(sources, belows, weights, place, stay, before, kind):
    height, width = sources[0].shape
    rows = PLANE * (height - ROW_TILE)
    starts = [start for _, start in weights]
    tile = weights[0][0].shape[1]
    columns = PLANE * tile
    half = rows // 2
    half_spec = pl.BlockSpec((half, columns), lambda i, *_: (0, 0))
    return pl.pallas_call(
        functools.partial(project_kernel, starts),
        grid_spec=pltpu.PrefetchScalarGridSpec(
            num_scalar_prefetch=2,
            grid=(1,),
            in_specs=[pl.BlockSpec(memory_space=pl.ANY)] * PLANE
            + [pl.BlockSpec(row.shape, lambda i, *_: (0, 0)) for row in belows]
            + [pl.BlockSpec(memory_space=pl.ANY)] * len(starts)
            + [half_spec] * len(before),
            out_specs=[half_spec] * 2,
            scratch_shapes=[
                pltpu.VMEM((rows, width), sources[0].dtype),
                pltpu.VMEM((PLANE * ROW_TILE, width), sources[0].dtype),
                pltpu.VMEM((len(starts), width, tile), sources[0].dtype),
                pltpu.SemaphoreType.DMA((PLANE, 3)),
                pltpu.SemaphoreType.DMA((len(starts),)),
            ],
        ),
        out_shape=[jax.ShapeDtypeStruct((half, columns), kind)] * 2,
        compiler_params=pltpu.CompilerParams(vmem_limit_bytes=30 * MIB),
        cost_estimate=pl.CostEstimate(
            flops=2 * rows * width * columns,
            bytes_accessed=2 * width * (rows + columns) + 8 * rows * columns,
            transcendentals=0,
        ),
        name="project_rows",
    )(place, stay, *sources, *belows, *[weight for weight, _ in weights], *before)


def add_kernel(place_ref, keep_ref, other_ref, *outs):
    for at, ref in enumerate(outs):
        member = place_ref[0] ^ at
        ref[...] = (
            keep_ref[member].astype(jnp.float32) + other_ref[member].astype(jnp.float32)
        ).astype(ref.dtype)


def add_cores(keep, other, place):
    half, columns = keep.shape
    part = half // PLANE
    tile = min(columns, 512)
    folded = (PLANE, part, columns)
    return pl.pallas_call(
        add_kernel,
        grid_spec=pltpu.PrefetchScalarGridSpec(
            num_scalar_prefetch=1,
            grid=(columns // tile,),
            in_specs=[pl.BlockSpec((PLANE, part, tile), lambda i, *_: (0, 0, i))] * 2,
            out_specs=[pl.BlockSpec((part, tile), lambda i, *_: (0, i))] * PLANE,
        ),
        out_shape=[jax.ShapeDtypeStruct((part, columns), keep.dtype)] * PLANE,
        compiler_params=pltpu.CompilerParams(vmem_limit_bytes=10 * MIB),
        name="add_cores",
    )(place, keep.reshape(folded), other.reshape(folded))


def norm_kernel(strip, place_ref, line_ref, *refs):
    branches = refs[:-7]
    residual_ref, mask_ref, gain_ref, bias_ref, next_ref, normed_ref, branch_ref = refs[-7:]
    if len(branches) == 1:
        branch_ref[...] = branches[0][...].astype(jnp.float32)
    else:
        for at, ref in enumerate(branches):
            member = place_ref[0] ^ at
            for shard in range(ref.shape[1] // strip):
                to = pl.multiple_of((line_ref[shard] * PLANE + member) * strip, strip)
                branch_ref[:, pl.ds(to, strip)] = ref[
                    :, shard * strip : (shard + 1) * strip
                ].astype(jnp.float32)
    keep_scale = mask_ref[...].astype(jnp.float32) * (1.0 / keep_rate)
    stream = residual_ref[...].astype(jnp.float32) + keep_scale * branch_ref[...]
    centre = jnp.mean(stream, axis=1, keepdims=True)
    moved = stream - centre
    spread_of = jnp.mean(jnp.square(moved), axis=1, keepdims=True)
    normed = moved * lax.rsqrt(spread_of + norm_eps) * gain_ref[...] + bias_ref[...]
    next_ref[...] = stream.astype(next_ref.dtype)
    normed_ref[...] = normed.astype(normed_ref.dtype)


def add_norm(place, line, branches, strip, residual, drop_mask, gain, bias):
    rows, columns = residual.shape
    tile = min(32, rows)
    row_spec = pl.BlockSpec((tile, columns), lambda i, *_: (i, 0))
    branch_spec = pl.BlockSpec((tile, branches[0].shape[1]), lambda i, *_: (i, 0))
    flat_spec = pl.BlockSpec((1, columns), lambda i, *_: (0, 0))
    return pl.pallas_call(
        functools.partial(norm_kernel, strip),
        grid_spec=pltpu.PrefetchScalarGridSpec(
            num_scalar_prefetch=2,
            grid=(rows // tile,),
            in_specs=[branch_spec] * len(branches) + [row_spec, row_spec, flat_spec, flat_spec],
            out_specs=[row_spec, row_spec],
            scratch_shapes=[pltpu.VMEM((tile, columns), jnp.float32)],
        ),
        out_shape=[jax.ShapeDtypeStruct((rows, columns), residual.dtype)] * 2,
        compiler_params=pltpu.CompilerParams(vmem_limit_bytes=20 * MIB),
        name="add_norm",
    )(place, line, *branches, residual, drop_mask, gain[None], bias[None])


def pick_requests(owners, slots, peers, per_block):
    selector = owners[None, :] == peers[:, None]
    pair_block = jnp.arange(owners.shape[0], dtype=jnp.int32) // per_block
    return (
        jnp.sum(jnp.where(selector, pair_block[None, :], 0), axis=1),
        jnp.sum(jnp.where(selector, slots[None, :] + 1, 0), axis=1),
    )


def within(owners, base, half):
    index = owners - base
    use = (index >= 0) & (index < half)
    return jnp.where(use, index, 0), use.astype(jnp.int32)


def local(
    queries,
    neighbour_keys,
    neighbour_values,
    residual,
    out_weight,
    drop_mask,
    norm_gain,
    norm_bias,
    neighbour_owner,
    neighbour_slot,
):
    peer_count = lax.axis_size("dp")
    side_count = lax.axis_size("tensor")
    half = peer_count // 2
    halves = [list(range(half)), list(range(half, peer_count))]
    across = [(i, (i + half) % peer_count) for i in range(peer_count)]
    by_plane = side_count == 2 and peer_count == 4 * PLANE
    blocks, per_block = neighbour_owner.shape
    rows, row_width = queries.shape
    span_len = rows // blocks
    here = lax.axis_index("dp").astype(jnp.int32)
    upper = here // half
    base = upper * half
    partner = lax.rem(here + half, peer_count)

    def exchange(x):
        return lax.all_to_all(
            x, "dp", split_axis=0, concat_axis=0, tiled=True, axis_index_groups=halves
        )

    def swap(x, by):
        return lax.ppermute(x, "dp", [(i, i ^ by) for i in range(peer_count)])

    def pinned(*values):
        return lax.optimization_barrier(values)

    def to_partner(x):
        return lax.ppermute(x, "dp", across)

    chunks = 2
    width = row_width // chunks
    far_first = to_partner(queries[:, :width])
    middle = row_width // 2
    carried = shifted(queries[-1:], "dp", 1)
    owners = neighbour_owner.reshape(-1)
    slot_rows = neighbour_slot.reshape(-1)
    near_peers = base + jnp.arange(half, dtype=jnp.int32)
    far_carried = lax.ppermute(
        queries[-1:], "dp", [(i - 1, (i + half) % peer_count) for i in range(1, peer_count)]
    )
    requests = owners.shape[0]
    far_table = to_partner(
        jnp.pad(jnp.concatenate([owners, slot_rows]), (0, LANES - 2 * requests))[None, :]
    )
    carried, far_carried, far_table = pinned(carried, far_carried, far_table)
    near_out = spread(
        [queries], carried, *pick_requests(owners, slot_rows, near_peers, per_block),
        span_len, 0,
    )
    near_asked = exchange(near_out)
    far_first, far_carried, far_table, second, weight, _ = pinned(
        far_first, far_carried, far_table, queries[:, width:], out_weight, near_out
    )
    far_owners = far_table[0, :requests]
    far_picked = pick_requests(
        far_owners, far_table[0, requests : 2 * requests], near_peers, per_block
    )

    def answer(asked, tags, chunk, part, size, place, places, shared=None):
        return attend(
            asked, tags, neighbour_keys, neighbour_values, width, chunk, part, size,
            place, places, shared,
        )

    wide = width + LANES
    far_second = to_partner(second)
    near_index, near_use = within(owners, base, half)
    far_index, far_use = within(far_owners, base, half)
    far_out = spread([far_first], far_carried, *far_picked, span_len, 0)
    far_asked = exchange(far_out)
    near_asked, _ = pinned(near_asked, far_out)
    near_first = answer(near_asked, near_asked, 0, 0, width, 0, 2)
    near_second = answer(near_asked, near_asked, 1, 1, width, 1, 2)
    (
        far_asked, far_second, near_first, near_second, near_index, near_use, far_index,
        far_use, weight, *weight_halves,
    ) = pinned(
        far_asked, far_second, near_first, near_second, near_index, near_use, far_index,
        far_use, weight, weight[:middle], weight[middle:],
    )

    mixed = spread([far_second], far_carried, *far_picked, span_len, 1, near_first)
    next_asked = exchange(mixed)
    far_weight = [to_partner(weight_halves[0])] if by_plane else []
    tags, near_second, _ = pinned(far_asked, near_second, mixed)
    mixed = answer(tags, tags, 0, 0, wide, 0, 2, near_second)
    mixed, next_asked, weight_half, *far_weight = pinned(
        mixed, next_asked, weight_halves[1], *far_weight
    )

    far_back = exchange(mixed)
    if by_plane:
        far_weight.append(to_partner(weight_half))
    far_parts = answer(next_asked, tags, 1, 1, wide, 0, 1)
    far_back, far_parts, *far_weight = pinned(far_back, far_parts, *far_weight)
    near_back, next_back = next_asked, far_back

    far_merged = merge_far(far_back, 0, wide, far_index, far_use, blocks)
    far_home = to_partner(far_merged)
    far_back = exchange(far_parts)
    far_home, far_back, weight, *far_weight = pinned(far_home, far_back, weight, *far_weight)

    def to_plane(moved):
        return [moved] + [swap(moved, by) for by in range(1, PLANE)] if by_plane else [moved]

    far_merged = merge_far(far_back, 0, wide, far_index, far_use, blocks)
    far_home, near_back, far_merged, weight, *far_weight = pinned(
        far_home, near_back, far_merged, weight, *far_weight
    )
    next_home = to_partner(far_merged)
    moved, first = merge_all(near_back, 0, wide, near_index, near_use, blocks, far_home)
    sources = to_plane(moved)
    swaps = [swap(weight, PLANE)] if by_plane else []
    count = len(sources)
    (next_home,) = pinned(next_home)
    next_home, next_back, *held = pinned(next_home, next_back, *sources, *swaps, *far_weight)
    sources, held = held[:count], held[count:]
    moved, first = merge_all(
        next_back, 1, wide, near_index, near_use, blocks, next_home, first
    )
    if by_plane:
        place = lax.rem(here, PLANE).reshape(1)
        stay = lax.axis_index("tensor").astype(jnp.int32).reshape(1)
        near_swap, *far_weight = held
        moved, first, *far_weight = pinned(moved, first, *far_weight)
        next_sources = to_plane(moved)
        far_swap = [swap(piece, PLANE) for piece in far_weight]
        belows = [
            lax.ppermute(
                first, "dp", [(i + PLANE, i + at) for i in range(0, peer_count - PLANE, PLANE)]
            )
            for at in range(PLANE)
        ]
        first_weights = [(weight, 0), (near_swap, 0), (far_weight[0], 0), (far_swap[0], 0)]
        next_weights = [
            (weight, middle), (near_swap, middle), (far_weight[1], 0), (far_swap[1], 0)
        ]
        done = project(sources, [], first_weights, place, stay, [], jnp.float32)
        keep, send = project(
            next_sources, belows, next_weights + first_weights, place, stay, done, moved.dtype
        )
        line = jnp.stack(
            [here // PLANE, (here ^ PLANE) // PLANE, partner // PLANE, (partner ^ PLANE) // PLANE]
        )
        summed = add_cores(keep, lax.ppermute(send, "tensor", [(0, 1), (1, 0)]), place)
        branches = [summed[0]] + [swap(summed[by], by) for by in range(1, PLANE)]
    else:
        whole_weight = lax.all_gather(out_weight, "dp", axis=1, tiled=True)
        moved = jnp.concatenate([sources[0], moved], axis=1)
        below = shifted(first[:1], "dp", -1)
        cross_rows = jnp.concatenate([moved[: rows - 1], below], axis=0)
        branch = jnp.dot(cross_rows, whole_weight, preferred_element_type=jnp.float32)
        branches = [
            lax.psum_scatter(
                branch.astype(jnp.bfloat16), "tensor", scatter_dimension=0, tiled=True
            )
        ]
        place = line = jnp.zeros((1,), jnp.int32)
    return tuple(
        add_norm(
            place, line, branches, out_weight.shape[1], residual, drop_mask, norm_gain, norm_bias
        )
    )


def solution(mesh):
    placed = (
        P("dp", "tensor"),
        P("dp", None, "tensor"),
        P("dp", None, "tensor"),
        P(("dp", "tensor"), None),
        P("tensor", "dp"),
        P(("dp", "tensor"), None),
        P(),
        P(),
        P("dp", None),
        P("dp", None),
    )
    return jax.shard_map(
        local,
        mesh=mesh,
        in_specs=placed,
        out_specs=(P(("dp", "tensor"), None), P(("dp", "tensor"), None)),
        check_vma=False,
    )
```

```python
import functools

import jax
import jax.numpy as jnp
from jax import lax
from jax.experimental import pallas as pl
from jax.experimental.pallas import tpu as pltpu
from jax.sharding import PartitionSpec as P

HEAD = 128
LANES = 128
MIB = 1024 * 1024
ROW_TILE = 16
PLANE = 4

keep_rate = 0.9
norm_eps = 1e-05


def shifted(x, axis, by):
    count = lax.axis_size(axis)
    pairs = [(i, i + by) for i in range(count) if 0 <= i + by < count]
    return lax.ppermute(x, axis, pairs)


def spread_kernel(count, column, block_ref, slot_ref, carried_ref, *refs):
    pieces = refs[:count]
    out_ref, moved, tags, sems = refs[-4:]
    peers, span_len, _ = out_ref.shape
    rows, piece_width = pieces[0].shape
    row_width = moved.shape[1]
    at = 0
    for piece in pieces:
        for start in range(0, piece_width, 512):
            size = min(512, piece_width - start)
            held = piece[:, start : start + size].astype(jnp.float32)
            rolled = pltpu.roll(held, 1, 0)
            first = lax.broadcasted_iota(jnp.int32, (rows, size), 0) == 0
            above = carried_ref[0:1, at : at + size].astype(jnp.float32)
            moved[:, at : at + size] = jnp.where(first, above, rolled).astype(moved.dtype)
            at += size

    def copies(peer):
        start = pl.multiple_of(block_ref[peer] * span_len, span_len)
        yield pltpu.make_async_copy(
            moved.at[pl.ds(start, span_len)],
            out_ref.at[peer, :, pl.ds(column, row_width)],
            sems.at[0, peer],
        )
        yield pltpu.make_async_copy(
            tags.at[peer],
            out_ref.at[peer, :, pl.ds(column + row_width, LANES)],
            sems.at[1, peer],
        )

    for peer in range(peers):
        slot = slot_ref[peer].astype(jnp.float32)
        tags[peer] = jnp.full((span_len, LANES), slot, jnp.float32).astype(tags.dtype)
        for copy in copies(peer):
            copy.start()
    for peer in range(peers):
        for copy in copies(peer):
            copy.wait()


def spread(pieces, carried, block_of_peer, slot_of_peer, span_len, chunk, shared=None):
    peers = block_of_peer.shape[0]
    rows, piece_width = pieces[0].shape
    row_width = piece_width * len(pieces)
    wide = row_width + LANES
    whole = wide if shared is None else shared.shape[2]
    extra = [] if shared is None else [shared]
    return pl.pallas_call(
        functools.partial(spread_kernel, len(pieces), whole - wide),
        grid_spec=pltpu.PrefetchScalarGridSpec(
            num_scalar_prefetch=2,
            grid=(1,),
            in_specs=[pl.BlockSpec((1, row_width), lambda i, *_: (0, chunk))]
            + [pl.BlockSpec((rows, piece_width), lambda i, *_: (0, 0))] * len(pieces)
            + [pl.BlockSpec(memory_space=pl.ANY)] * len(extra),
            out_specs=pl.BlockSpec(memory_space=pl.ANY),
            scratch_shapes=[
                pltpu.VMEM((rows, row_width), carried.dtype),
                pltpu.VMEM((peers, span_len, LANES), carried.dtype),
                pltpu.SemaphoreType.DMA((2, peers)),
            ],
        ),
        out_shape=jax.ShapeDtypeStruct((peers, span_len, whole), carried.dtype),
        input_output_aliases={3 + len(pieces): 0} if extra else {},
        compiler_params=pltpu.CompilerParams(vmem_limit_bytes=(60 if extra else 10) * MIB),
        name="spread_queries",
    )(block_of_peer, slot_of_peer, carried, *pieces, *extra)


def pack_levels(stats, heads):
    part = lax.broadcasted_iota(jnp.int32, stats.shape, 1) // heads
    high = stats.astype(jnp.bfloat16).astype(jnp.float32)
    rest = stats - high
    middle = rest.astype(jnp.bfloat16).astype(jnp.float32)
    low = rest - middle
    return jnp.where(part == 0, high, jnp.where(part == 1, middle, jnp.where(part == 2, low, 0.0)))


def unpack_levels(packed, heads):
    packed = packed.astype(jnp.float32)
    return (
        packed
        + pltpu.roll(packed, LANES - heads, 1)
        + pltpu.roll(packed, LANES - 2 * heads, 1)
    )


def attend_kernel(chunk, tag_ref, query_ref, key_ref, value_ref, *refs):
    out_ref, key_held, value_held, sems = refs[-4:]
    span_len = query_ref.shape[1]
    _, length, row_width = key_held.shape
    heads = row_width // HEAD
    group = min(heads, 4)
    peer = pl.program_id(0)
    peers = pl.num_programs(0)

    def tag_of(at):
        return tag_ref[at, 0:1, 0:1].astype(jnp.float32)[0, 0].astype(jnp.int32)

    def copies(at):
        buffer = lax.rem(at, 2)
        slot = jnp.maximum(tag_of(at) - 1, 0)
        for kind, (ref, held) in enumerate(((key_ref, key_held), (value_ref, value_held))):
            yield pltpu.make_async_copy(
                ref.at[slot, :, pl.ds(chunk * row_width, row_width)],
                held.at[buffer],
                sems.at[kind, buffer],
            )

    def fetch(at):
        for copy in copies(at):
            copy.start()

    following = jnp.minimum(peer + 1, peers - 1)

    @pl.when((peer == 0) & (tag_of(0) > 0))
    def _():
        fetch(0)

    @pl.when((peer + 1 < peers) & (tag_of(following) > 0))
    def _():
        fetch(following)

    @pl.when(tag_of(peer) > 0)
    def _():
        for copy in copies(peer):
            copy.wait()
        buffer = lax.rem(peer, 2)
        lane = lax.broadcasted_iota(jnp.int32, (span_len, LANES), 1)
        stats = jnp.zeros((span_len, LANES), jnp.float32)
        ones = jnp.ones((length, HEAD), jnp.bfloat16)
        for first in range(0, heads, group):
            chosen = range(first, first + group)
            cuts = [slice(head * HEAD, (head + 1) * HEAD) for head in chosen]
            scores = [
                lax.dot_general(
                    query_ref[0, :, cut],
                    key_held[buffer, :, cut],
                    (((1,), (1,)), ((), ())),
                    preferred_element_type=jnp.float32,
                )
                * HEAD ** (-0.5)
                for cut in cuts
            ]
            peaks = [jnp.max(score, axis=1, keepdims=True) for score in scores]
            raised = [
                jnp.exp(score - peak).astype(jnp.bfloat16) for score, peak in zip(scores, peaks)
            ]
            sums = [
                jnp.dot(
                    weight,
                    jnp.concatenate([value_held[buffer, :, cut], ones], axis=1),
                    preferred_element_type=jnp.float32,
                )
                for weight, cut in zip(raised, cuts)
            ]
            for head, cut, peak, both in zip(chosen, cuts, peaks, sums):
                total = both[:, HEAD:]
                out_ref[0, :, cut] = (both[:, :HEAD] / total).astype(out_ref.dtype)
                stats = jnp.where(lane % heads == head, peak + jnp.log(total), stats)
        out_ref[0, :, row_width:] = pack_levels(stats, heads).astype(out_ref.dtype)


def attend(asked, tags, keys, values, width, chunk, part, size, place, places, shared):
    peers, span_len, _ = asked.shape
    length = keys.shape[1]
    heads = width // HEAD
    wide = width + LANES
    tag_at = tags.shape[2] // LANES - 1
    extra = [] if shared is None else [shared]
    return pl.pallas_call(
        functools.partial(attend_kernel, chunk),
        grid=(peers,),
        in_specs=[
            pl.BlockSpec((peers, ROW_TILE, LANES), lambda i: (0, 0, tag_at)),
            pl.BlockSpec((1, span_len, size), lambda i: (i, 0, part)),
            pl.BlockSpec(memory_space=pl.ANY),
            pl.BlockSpec(memory_space=pl.ANY),
        ]
        + [pl.BlockSpec(memory_space=pl.ANY)] * len(extra),
        out_specs=pl.BlockSpec((1, span_len, wide), lambda i: (i, 0, place)),
        scratch_shapes=[
            pltpu.VMEM((2, length, width), keys.dtype),
            pltpu.VMEM((2, length, width), keys.dtype),
            pltpu.SemaphoreType.DMA((2, 2)),
        ],
        out_shape=jax.ShapeDtypeStruct((peers, span_len, places * wide), asked.dtype),
        input_output_aliases={4: 0} if extra else {},
        compiler_params=pltpu.CompilerParams(vmem_limit_bytes=58 * MIB),
        cost_estimate=pl.CostEstimate(
            flops=4 * peers * heads * span_len * length * HEAD,
            bytes_accessed=2 * peers * width * (2 * span_len + 2 * length),
            transcendentals=peers * heads * span_len * length,
        ),
        name="attend_blocks",
    )(tags, asked, keys, values, *extra)


def merge_block(uses, parts):
    row_width = parts[0].shape[2] - LANES
    heads = row_width // HEAD

    def masked(use, held, other):
        return held if use is None else jnp.where(use, held, other)

    levels = [
        masked(use, unpack_levels(ref[0, :, row_width:], heads), -1e30)
        for use, ref in zip(uses, parts)
    ]
    highest = functools.reduce(jnp.maximum, levels)
    weights = [jnp.exp(level - highest) for level in levels]
    total = functools.reduce(jnp.add, weights)
    weights = [weight / total for weight in weights]
    for head in range(heads):
        cut = slice(head * HEAD, (head + 1) * HEAD)
        merged = functools.reduce(
            jnp.add,
            [
                weight[:, head : head + 1]
                * masked(use, ref[0, :, cut].astype(jnp.float32), 0.0)
                for use, weight, ref in zip(uses, weights, parts)
            ],
        )
        yield cut, merged
    lane = lax.broadcasted_iota(jnp.int32, highest.shape, 1)
    level = jnp.where(lane < heads, highest + jnp.log(total), 0.0)
    level = level + pltpu.roll(level, heads, 1) + pltpu.roll(level, 2 * heads, 1)
    yield slice(row_width, row_width + LANES), pack_levels(level, heads)


def merge_far_kernel(picked, index_ref, use_ref, *refs):
    block = pl.program_id(0)
    uses = [use_ref[block * picked + r] > 0 for r in range(picked)]
    out_ref = refs[-1]
    for cut, merged in merge_block(uses, refs[:-1]):
        out_ref[0, :, cut] = merged.astype(out_ref.dtype)


def merge_all_kernel(picked, earlier, index_ref, use_ref, *refs):
    parts = refs[: picked + 1]
    out_ref, first_ref, kept = refs[-3:]
    span_len = parts[0].shape[1]
    rows, row_width = out_ref.shape
    rows -= ROW_TILE
    step = pl.program_id(0)
    block = rows // span_len - 1 - step
    uses = [use_ref[block * picked + r] > 0 for r in range(picked)] + [None]
    start = pl.multiple_of(block * span_len, span_len)
    last = lax.broadcasted_iota(jnp.int32, (span_len, HEAD), 0) == span_len - 1
    at = first_ref.shape[1] - row_width

    @pl.when(step == 0)
    def _():
        kept[...] = jnp.zeros_like(kept)
        if earlier:
            first_ref[:, :at] = refs[picked + 1][...]

    for cut, merged in merge_block(uses, parts):
        if cut.start < row_width:
            moved = pltpu.roll(merged, span_len - 1, 0)
            moved = jnp.where(last, kept[0:1, cut], moved)
            out_ref[pl.ds(start, span_len), cut] = moved.astype(out_ref.dtype)
            kept[:, cut] = merged[:8]
            first = merged[:ROW_TILE].astype(out_ref.dtype)
            out_ref[rows:, cut] = first
            first_ref[:, at + cut.start : at + cut.stop] = first


def merge_far(parts, column, wide, index, use, blocks):
    span_len = parts.shape[1]
    picked = index.shape[0] // blocks
    specs = [
        pl.BlockSpec(
            (1, span_len, wide),
            functools.partial(lambda r, i, index, use: (index[i * picked + r], 0, column), r),
        )
        for r in range(picked)
    ]
    return pl.pallas_call(
        functools.partial(merge_far_kernel, picked),
        grid_spec=pltpu.PrefetchScalarGridSpec(
            num_scalar_prefetch=2,
            grid=(blocks,),
            in_specs=specs,
            out_specs=pl.BlockSpec((1, span_len, wide), lambda i, *_: (i, 0, 0)),
        ),
        out_shape=jax.ShapeDtypeStruct((blocks, span_len, wide), parts.dtype),
        compiler_params=pltpu.CompilerParams(vmem_limit_bytes=10 * MIB),
        name="merge_far",
    )(index, use, *([parts] * picked))


def merge_all(parts, column, wide, index, use, blocks, far, earlier=None):
    span_len = parts.shape[1]
    row_width = wide - LANES
    picked = index.shape[0] // blocks
    rows = blocks * span_len
    specs = [
        pl.BlockSpec(
            (1, span_len, wide),
            functools.partial(
                lambda r, i, index, use: (index[(blocks - 1 - i) * picked + r], 0, column), r
            ),
        )
        for r in range(picked)
    ]
    specs.append(pl.BlockSpec((1, span_len, wide), lambda i, *_: (blocks - 1 - i, 0, 0)))
    extra = [] if earlier is None else [earlier]
    first_width = row_width * (1 + len(extra))
    specs += [pl.BlockSpec((ROW_TILE, row_width), lambda i, *_: (0, 0))] * len(extra)
    return pl.pallas_call(
        functools.partial(merge_all_kernel, picked, len(extra)),
        grid_spec=pltpu.PrefetchScalarGridSpec(
            num_scalar_prefetch=2,
            grid=(blocks,),
            in_specs=specs,
            out_specs=[
                pl.BlockSpec((rows + ROW_TILE, row_width), lambda i, *_: (0, 0)),
                pl.BlockSpec((ROW_TILE, first_width), lambda i, *_: (0, 0)),
            ],
            scratch_shapes=[pltpu.VMEM((8, row_width), jnp.float32)],
        ),
        out_shape=[
            jax.ShapeDtypeStruct((rows + ROW_TILE, row_width), parts.dtype),
            jax.ShapeDtypeStruct((ROW_TILE, first_width), parts.dtype),
        ],
        compiler_params=pltpu.CompilerParams(vmem_limit_bytes=10 * MIB),
        name="merge_all",
    )(index, use, *([parts] * picked), far, *extra)


def project_kernel(starts, place_ref, stay_ref, *refs):
    sources, refs = refs[:PLANE], refs[PLANE:]
    last_part = len(starts) > PLANE
    belows, refs = (refs[:PLANE], refs[PLANE:]) if last_part else ([], refs)
    weights, before = refs[: len(starts)], refs[len(starts) : -7]
    keep_ref, send_ref, rows_ref, first_ref, held_ref, row_sems, weight_sems = refs[-7:]
    half = keep_ref.shape[0]
    part = half // PLANE
    _, width, tile = held_ref.shape

    def source_copies():
        for at, ref in enumerate(sources):
            member = place_ref[0] ^ at
            for side in range(2):
                to = pl.multiple_of(side * half + member * part, part)
                yield pltpu.make_async_copy(
                    ref.at[pl.ds(side * part, part)],
                    rows_ref.at[pl.ds(to, part)],
                    row_sems.at[at, side],
                )
            to = pl.multiple_of(member * ROW_TILE, ROW_TILE)
            yield pltpu.make_async_copy(
                ref.at[pl.ds(2 * part, ROW_TILE)],
                first_ref.at[pl.ds(to, ROW_TILE)],
                row_sems.at[at, 2],
            )

    def weight_copy(at):
        return pltpu.make_async_copy(
            weights[at].at[pl.ds(starts[at], width)], held_ref.at[at], weight_sems.at[at]
        )

    for copy in source_copies():
        copy.start()
    for at in range(len(starts)):
        weight_copy(at).start()
    for copy in source_copies():
        copy.wait()
    last = lax.broadcasted_iota(jnp.int32, (ROW_TILE, width), 0) == ROW_TILE - 1
    for member in range(PLANE):
        at = (member + 1) % PLANE * ROW_TILE
        below = first_ref[at : at + ROW_TILE].astype(jnp.float32)[0:1]
        if member == PLANE - 1:
            below = jnp.zeros_like(below)
        end = half + (member + 1) * part
        held = rows_ref[end - ROW_TILE : end].astype(jnp.float32)
        rows_ref[end - ROW_TILE : end] = jnp.where(last, below, held).astype(rows_ref.dtype)
    if last_part:
        below = functools.reduce(jnp.add, [ref[...].astype(jnp.float32) for ref in belows])
        below = below.astype(rows_ref.dtype)
    stay = pl.multiple_of(stay_ref[0] * half, half)
    go = pl.multiple_of((1 - stay_ref[0]) * half, half)
    for shard in range(PLANE):
        weight_copy(shard).wait()
        if last_part:
            weight_copy(PLANE + shard).wait()
        cut = slice(shard * tile, (shard + 1) * tile)
        for at, (start, ref) in enumerate(((stay, keep_ref), (go, send_ref))):
            result = jnp.dot(
                rows_ref[pl.ds(start, half)], held_ref[shard], preferred_element_type=jnp.float32
            )
            if last_part:
                result = result + before[at][:, cut]
            ref[:, cut] = result.astype(ref.dtype)
        if last_part:
            row = functools.reduce(
                jnp.add,
                [
                    jnp.dot(
                        below[:, side * width : (side + 1) * width],
                        held_ref[at],
                        preferred_element_type=jnp.float32,
                    )
                    for side, at in ((0, PLANE + shard), (1, shard))
                ],
            )[0:1]
            at_end = lax.broadcasted_iota(jnp.int32, (ROW_TILE, tile), 0) == ROW_TILE - 1
            for upper, ref in ((stay_ref[0] > 0, keep_ref), (stay_ref[0] == 0, send_ref)):

                @pl.when(upper)
                def _():
                    held = ref[half - ROW_TILE :, cut].astype(jnp.float32)
                    ref[half - ROW_TILE :, cut] = jnp.where(at_end, row, held).astype(ref.dtype)


def project(sources, belows, weights, place, stay, before, kind):
    height, width = sources[0].shape
    rows = PLANE * (height - ROW_TILE)
    starts = [start for _, start in weights]
    tile = weights[0][0].shape[1]
    columns = PLANE * tile
    half = rows // 2
    half_spec = pl.BlockSpec((half, columns), lambda i, *_: (0, 0))
    return pl.pallas_call(
        functools.partial(project_kernel, starts),
        grid_spec=pltpu.PrefetchScalarGridSpec(
            num_scalar_prefetch=2,
            grid=(1,),
            in_specs=[pl.BlockSpec(memory_space=pl.ANY)] * PLANE
            + [pl.BlockSpec(row.shape, lambda i, *_: (0, 0)) for row in belows]
            + [pl.BlockSpec(memory_space=pl.ANY)] * len(starts)
            + [half_spec] * len(before),
            out_specs=[half_spec] * 2,
            scratch_shapes=[
                pltpu.VMEM((rows, width), sources[0].dtype),
                pltpu.VMEM((PLANE * ROW_TILE, width), sources[0].dtype),
                pltpu.VMEM((len(starts), width, tile), sources[0].dtype),
                pltpu.SemaphoreType.DMA((PLANE, 3)),
                pltpu.SemaphoreType.DMA((len(starts),)),
            ],
        ),
        out_shape=[jax.ShapeDtypeStruct((half, columns), kind)] * 2,
        compiler_params=pltpu.CompilerParams(vmem_limit_bytes=30 * MIB),
        cost_estimate=pl.CostEstimate(
            flops=2 * rows * width * columns,
            bytes_accessed=2 * width * (rows + columns) + 8 * rows * columns,
            transcendentals=0,
        ),
        name="project_rows",
    )(place, stay, *sources, *belows, *[weight for weight, _ in weights], *before)


def add_kernel(place_ref, keep_ref, other_ref, *outs):
    for at, ref in enumerate(outs):
        member = place_ref[0] ^ at
        ref[...] = (
            keep_ref[member].astype(jnp.float32) + other_ref[member].astype(jnp.float32)
        ).astype(ref.dtype)


def add_cores(keep, other, place):
    half, columns = keep.shape
    part = half // PLANE
    tile = min(columns, 512)
    folded = (PLANE, part, columns)
    return pl.pallas_call(
        add_kernel,
        grid_spec=pltpu.PrefetchScalarGridSpec(
            num_scalar_prefetch=1,
            grid=(columns // tile,),
            in_specs=[pl.BlockSpec((PLANE, part, tile), lambda i, *_: (0, 0, i))] * 2,
            out_specs=[pl.BlockSpec((part, tile), lambda i, *_: (0, i))] * PLANE,
        ),
        out_shape=[jax.ShapeDtypeStruct((part, columns), keep.dtype)] * PLANE,
        compiler_params=pltpu.CompilerParams(vmem_limit_bytes=10 * MIB),
        name="add_cores",
    )(place, keep.reshape(folded), other.reshape(folded))


def norm_kernel(strip, place_ref, line_ref, *refs):
    branches = refs[:-7]
    residual_ref, mask_ref, gain_ref, bias_ref, next_ref, normed_ref, branch_ref = refs[-7:]
    if len(branches) == 1:
        branch_ref[...] = branches[0][...].astype(jnp.float32)
    else:
        for at, ref in enumerate(branches):
            member = place_ref[0] ^ at
            for shard in range(ref.shape[1] // strip):
                to = pl.multiple_of((line_ref[shard] * PLANE + member) * strip, strip)
                branch_ref[:, pl.ds(to, strip)] = ref[
                    :, shard * strip : (shard + 1) * strip
                ].astype(jnp.float32)
    keep_scale = mask_ref[...].astype(jnp.float32) * (1.0 / keep_rate)
    stream = residual_ref[...].astype(jnp.float32) + keep_scale * branch_ref[...]
    centre = jnp.mean(stream, axis=1, keepdims=True)
    moved = stream - centre
    spread_of = jnp.mean(jnp.square(moved), axis=1, keepdims=True)
    normed = moved * lax.rsqrt(spread_of + norm_eps) * gain_ref[...] + bias_ref[...]
    next_ref[...] = stream.astype(next_ref.dtype)
    normed_ref[...] = normed.astype(normed_ref.dtype)


def add_norm(place, line, branches, strip, residual, drop_mask, gain, bias):
    rows, columns = residual.shape
    tile = min(32, rows)
    row_spec = pl.BlockSpec((tile, columns), lambda i, *_: (i, 0))
    branch_spec = pl.BlockSpec((tile, branches[0].shape[1]), lambda i, *_: (i, 0))
    flat_spec = pl.BlockSpec((1, columns), lambda i, *_: (0, 0))
    return pl.pallas_call(
        functools.partial(norm_kernel, strip),
        grid_spec=pltpu.PrefetchScalarGridSpec(
            num_scalar_prefetch=2,
            grid=(rows // tile,),
            in_specs=[branch_spec] * len(branches) + [row_spec, row_spec, flat_spec, flat_spec],
            out_specs=[row_spec, row_spec],
            scratch_shapes=[pltpu.VMEM((tile, columns), jnp.float32)],
        ),
        out_shape=[jax.ShapeDtypeStruct((rows, columns), residual.dtype)] * 2,
        compiler_params=pltpu.CompilerParams(vmem_limit_bytes=20 * MIB),
        name="add_norm",
    )(place, line, *branches, residual, drop_mask, gain[None], bias[None])


def pick_requests(owners, slots, peers, per_block):
    selector = owners[None, :] == peers[:, None]
    pair_block = jnp.arange(owners.shape[0], dtype=jnp.int32) // per_block
    return (
        jnp.sum(jnp.where(selector, pair_block[None, :], 0), axis=1),
        jnp.sum(jnp.where(selector, slots[None, :] + 1, 0), axis=1),
    )


def within(owners, base, half):
    index = owners - base
    use = (index >= 0) & (index < half)
    return jnp.where(use, index, 0), use.astype(jnp.int32)


def local(
    queries,
    neighbour_keys,
    neighbour_values,
    residual,
    out_weight,
    drop_mask,
    norm_gain,
    norm_bias,
    neighbour_owner,
    neighbour_slot,
):
    peer_count = lax.axis_size("dp")
    side_count = lax.axis_size("tensor")
    half = peer_count // 2
    halves = [list(range(half)), list(range(half, peer_count))]
    across = [(i, (i + half) % peer_count) for i in range(peer_count)]
    by_plane = side_count == 2 and peer_count == 4 * PLANE
    blocks, per_block = neighbour_owner.shape
    rows, row_width = queries.shape
    span_len = rows // blocks
    here = lax.axis_index("dp").astype(jnp.int32)
    upper = here // half
    base = upper * half
    partner = lax.rem(here + half, peer_count)

    def exchange(x):
        return lax.all_to_all(
            x, "dp", split_axis=0, concat_axis=0, tiled=True, axis_index_groups=halves
        )

    def swap(x, by):
        return lax.ppermute(x, "dp", [(i, i ^ by) for i in range(peer_count)])

    def pinned(*values):
        return lax.optimization_barrier(values)

    def to_partner(x):
        return lax.ppermute(x, "dp", across)

    chunks = 2
    width = row_width // chunks
    far_first = to_partner(queries[:, :width])
    middle = row_width // 2
    carried = shifted(queries[-1:], "dp", 1)
    owners = neighbour_owner.reshape(-1)
    slot_rows = neighbour_slot.reshape(-1)
    near_peers = base + jnp.arange(half, dtype=jnp.int32)
    far_carried = lax.ppermute(
        queries[-1:], "dp", [(i - 1, (i + half) % peer_count) for i in range(1, peer_count)]
    )
    requests = owners.shape[0]
    far_table = to_partner(
        jnp.pad(jnp.concatenate([owners, slot_rows]), (0, LANES - 2 * requests))[None, :]
    )
    near_out = spread(
        [queries], carried, *pick_requests(owners, slot_rows, near_peers, per_block),
        span_len, 0,
    )
    near_asked = exchange(near_out)
    far_first, far_carried, far_table, second, weight, _ = pinned(
        far_first, far_carried, far_table, queries[:, width:], out_weight, near_out
    )
    far_owners = far_table[0, :requests]
    far_picked = pick_requests(
        far_owners, far_table[0, requests : 2 * requests], near_peers, per_block
    )

    def answer(asked, tags, chunk, part, size, place, places, shared=None):
        return attend(
            asked, tags, neighbour_keys, neighbour_values, width, chunk, part, size,
            place, places, shared,
        )

    wide = width + LANES
    far_second = to_partner(second)
    near_index, near_use = within(owners, base, half)
    far_index, far_use = within(far_owners, base, half)
    far_out = spread([far_first], far_carried, *far_picked, span_len, 0)
    far_asked = exchange(far_out)
    near_asked, _ = pinned(near_asked, far_out)
    near_first = answer(near_asked, near_asked, 0, 0, width, 0, 2)
    near_second = answer(near_asked, near_asked, 1, 1, width, 1, 2)
    (
        far_asked, far_second, near_first, near_second, near_index, near_use, far_index,
        far_use, weight, *weight_halves,
    ) = pinned(
        far_asked, far_second, near_first, near_second, near_index, near_use, far_index,
        far_use, weight, weight[:middle], weight[middle:],
    )

    mixed = spread([far_second], far_carried, *far_picked, span_len, 1, near_first)
    next_asked = exchange(mixed)
    far_weight = [to_partner(weight_halves[0])] if by_plane else []
    tags, near_second, _ = pinned(far_asked, near_second, mixed)
    mixed = answer(tags, tags, 0, 0, wide, 0, 2, near_second)
    mixed, next_asked, weight_half, *far_weight = pinned(
        mixed, next_asked, weight_halves[1], *far_weight
    )

    far_back = exchange(mixed)
    if by_plane:
        far_weight.append(to_partner(weight_half))
    far_parts = answer(next_asked, tags, 1, 1, wide, 0, 1)
    far_back, far_parts, *far_weight = pinned(far_back, far_parts, *far_weight)
    near_back, next_back = next_asked, far_back

    far_merged = merge_far(far_back, 0, wide, far_index, far_use, blocks)
    far_home = to_partner(far_merged)
    far_back = exchange(far_parts)
    far_home, far_back, weight, *far_weight = pinned(far_home, far_back, weight, *far_weight)

    def to_plane(moved):
        return [moved] + [swap(moved, by) for by in range(1, PLANE)] if by_plane else [moved]

    far_merged = merge_far(far_back, 0, wide, far_index, far_use, blocks)
    far_home, near_back, far_merged, weight, *far_weight = pinned(
        far_home, near_back, far_merged, weight, *far_weight
    )
    next_home = to_partner(far_merged)
    moved, first = merge_all(near_back, 0, wide, near_index, near_use, blocks, far_home)
    sources = to_plane(moved)
    swaps = [swap(weight, PLANE)] if by_plane else []
    count = len(sources)
    (next_home,) = pinned(next_home)
    next_home, next_back, *held = pinned(next_home, next_back, *sources, *swaps, *far_weight)
    sources, held = held[:count], held[count:]
    moved, first = merge_all(
        next_back, 1, wide, near_index, near_use, blocks, next_home, first
    )
    if by_plane:
        place = lax.rem(here, PLANE).reshape(1)
        stay = lax.axis_index("tensor").astype(jnp.int32).reshape(1)
        near_swap, *far_weight = held
        moved, first, *far_weight = pinned(moved, first, *far_weight)
        next_sources = to_plane(moved)
        far_swap = [swap(piece, PLANE) for piece in far_weight]
        first_weights = [(weight, 0), (near_swap, 0), (far_weight[0], 0), (far_swap[0], 0)]
        next_weights = [
            (weight, middle), (near_swap, middle), (far_weight[1], 0), (far_swap[1], 0)
        ]
        done = project(sources, [], first_weights, place, stay, [], jnp.float32)
        first, *done = pinned(first, *done)
        belows = [
            lax.ppermute(
                first, "dp", [(i + PLANE, i + at) for i in range(0, peer_count - PLANE, PLANE)]
            )
            for at in range(PLANE)
        ]
        keep, send = project(
            next_sources, belows, next_weights + first_weights, place, stay, done, moved.dtype
        )
        line = jnp.stack(
            [here // PLANE, (here ^ PLANE) // PLANE, partner // PLANE, (partner ^ PLANE) // PLANE]
        )
        summed = add_cores(keep, lax.ppermute(send, "tensor", [(0, 1), (1, 0)]), place)
        branches = [summed[0]] + [swap(summed[by], by) for by in range(1, PLANE)]
    else:
        whole_weight = lax.all_gather(out_weight, "dp", axis=1, tiled=True)
        moved = jnp.concatenate([sources[0], moved], axis=1)
        below = shifted(first[:1], "dp", -1)
        cross_rows = jnp.concatenate([moved[: rows - 1], below], axis=0)
        branch = jnp.dot(cross_rows, whole_weight, preferred_element_type=jnp.float32)
        branches = [
            lax.psum_scatter(
                branch.astype(jnp.bfloat16), "tensor", scatter_dimension=0, tiled=True
            )
        ]
        place = line = jnp.zeros((1,), jnp.int32)
    return tuple(
        add_norm(
            place, line, branches, out_weight.shape[1], residual, drop_mask, norm_gain, norm_bias
        )
    )


def solution(mesh):
    placed = (
        P("dp", "tensor"),
        P("dp", None, "tensor"),
        P("dp", None, "tensor"),
        P(("dp", "tensor"), None),
        P("tensor", "dp"),
        P(("dp", "tensor"), None),
        P(),
        P(),
        P("dp", None),
        P("dp", None),
    )
    return jax.shard_map(
        local,
        mesh=mesh,
        in_specs=placed,
        out_specs=(P(("dp", "tensor"), None), P(("dp", "tensor"), None)),
        check_vma=False,
    )
```

```python
import functools

import jax
import jax.numpy as jnp
from jax import lax
from jax.experimental import pallas as pl
from jax.experimental.pallas import tpu as pltpu
from jax.sharding import PartitionSpec as P

HEAD = 128
LANES = 128
MIB = 1024 * 1024
ROW_TILE = 16
PLANE = 4

keep_rate = 0.9
norm_eps = 1e-05


def shifted(x, axis, by):
    count = lax.axis_size(axis)
    pairs = [(i, i + by) for i in range(count) if 0 <= i + by < count]
    return lax.ppermute(x, axis, pairs)


def spread_kernel(count, column, block_ref, slot_ref, carried_ref, *refs):
    pieces = refs[:count]
    out_ref, moved, tags, sems = refs[-4:]
    peers, span_len, _ = out_ref.shape
    rows, piece_width = pieces[0].shape
    row_width = moved.shape[1]
    at = 0
    for piece in pieces:
        for start in range(0, piece_width, 512):
            size = min(512, piece_width - start)
            held = piece[:, start : start + size].astype(jnp.float32)
            rolled = pltpu.roll(held, 1, 0)
            first = lax.broadcasted_iota(jnp.int32, (rows, size), 0) == 0
            above = carried_ref[0:1, at : at + size].astype(jnp.float32)
            moved[:, at : at + size] = jnp.where(first, above, rolled).astype(moved.dtype)
            at += size

    def copies(peer):
        start = pl.multiple_of(block_ref[peer] * span_len, span_len)
        yield pltpu.make_async_copy(
            moved.at[pl.ds(start, span_len)],
            out_ref.at[peer, :, pl.ds(column, row_width)],
            sems.at[0, peer],
        )
        yield pltpu.make_async_copy(
            tags.at[peer],
            out_ref.at[peer, :, pl.ds(column + row_width, LANES)],
            sems.at[1, peer],
        )

    for peer in range(peers):
        slot = slot_ref[peer].astype(jnp.float32)
        tags[peer] = jnp.full((span_len, LANES), slot, jnp.float32).astype(tags.dtype)
        for copy in copies(peer):
            copy.start()
    for peer in range(peers):
        for copy in copies(peer):
            copy.wait()


def spread(pieces, carried, block_of_peer, slot_of_peer, span_len, chunk, shared=None):
    peers = block_of_peer.shape[0]
    rows, piece_width = pieces[0].shape
    row_width = piece_width * len(pieces)
    wide = row_width + LANES
    whole = wide if shared is None else shared.shape[2]
    extra = [] if shared is None else [shared]
    return pl.pallas_call(
        functools.partial(spread_kernel, len(pieces), whole - wide),
        grid_spec=pltpu.PrefetchScalarGridSpec(
            num_scalar_prefetch=2,
            grid=(1,),
            in_specs=[pl.BlockSpec((1, row_width), lambda i, *_: (0, chunk))]
            + [pl.BlockSpec((rows, piece_width), lambda i, *_: (0, 0))] * len(pieces)
            + [pl.BlockSpec(memory_space=pl.ANY)] * len(extra),
            out_specs=pl.BlockSpec(memory_space=pl.ANY),
            scratch_shapes=[
                pltpu.VMEM((rows, row_width), carried.dtype),
                pltpu.VMEM((peers, span_len, LANES), carried.dtype),
                pltpu.SemaphoreType.DMA((2, peers)),
            ],
        ),
        out_shape=jax.ShapeDtypeStruct((peers, span_len, whole), carried.dtype),
        input_output_aliases={3 + len(pieces): 0} if extra else {},
        compiler_params=pltpu.CompilerParams(vmem_limit_bytes=(60 if extra else 10) * MIB),
        name="spread_queries",
    )(block_of_peer, slot_of_peer, carried, *pieces, *extra)


def pack_levels(stats, heads):
    part = lax.broadcasted_iota(jnp.int32, stats.shape, 1) // heads
    high = stats.astype(jnp.bfloat16).astype(jnp.float32)
    rest = stats - high
    middle = rest.astype(jnp.bfloat16).astype(jnp.float32)
    low = rest - middle
    return jnp.where(part == 0, high, jnp.where(part == 1, middle, jnp.where(part == 2, low, 0.0)))


def unpack_levels(packed, heads):
    packed = packed.astype(jnp.float32)
    return (
        packed
        + pltpu.roll(packed, LANES - heads, 1)
        + pltpu.roll(packed, LANES - 2 * heads, 1)
    )


def attend_kernel(chunk, tag_ref, query_ref, key_ref, value_ref, *refs):
    out_ref, key_held, value_held, sems = refs[-4:]
    span_len = query_ref.shape[1]
    _, length, row_width = key_held.shape
    heads = row_width // HEAD
    group = min(heads, 4)
    peer = pl.program_id(0)
    peers = pl.num_programs(0)

    def tag_of(at):
        return tag_ref[at, 0:1, 0:1].astype(jnp.float32)[0, 0].astype(jnp.int32)

    def copies(at):
        buffer = lax.rem(at, 2)
        slot = jnp.maximum(tag_of(at) - 1, 0)
        for kind, (ref, held) in enumerate(((key_ref, key_held), (value_ref, value_held))):
            yield pltpu.make_async_copy(
                ref.at[slot, :, pl.ds(chunk * row_width, row_width)],
                held.at[buffer],
                sems.at[kind, buffer],
            )

    def fetch(at):
        for copy in copies(at):
            copy.start()

    following = jnp.minimum(peer + 1, peers - 1)

    @pl.when((peer == 0) & (tag_of(0) > 0))
    def _():
        fetch(0)

    @pl.when((peer + 1 < peers) & (tag_of(following) > 0))
    def _():
        fetch(following)

    @pl.when(tag_of(peer) > 0)
    def _():
        for copy in copies(peer):
            copy.wait()
        buffer = lax.rem(peer, 2)
        lane = lax.broadcasted_iota(jnp.int32, (span_len, LANES), 1)
        stats = jnp.zeros((span_len, LANES), jnp.float32)
        ones = jnp.ones((length, HEAD), jnp.bfloat16)
        for first in range(0, heads, group):
            chosen = range(first, first + group)
            cuts = [slice(head * HEAD, (head + 1) * HEAD) for head in chosen]
            scores = [
                lax.dot_general(
                    query_ref[0, :, cut],
                    key_held[buffer, :, cut],
                    (((1,), (1,)), ((), ())),
                    preferred_element_type=jnp.float32,
                )
                * HEAD ** (-0.5)
                for cut in cuts
            ]
            peaks = [jnp.max(score, axis=1, keepdims=True) for score in scores]
            raised = [
                jnp.exp(score - peak).astype(jnp.bfloat16) for score, peak in zip(scores, peaks)
            ]
            sums = [
                jnp.dot(
                    weight,
                    jnp.concatenate([value_held[buffer, :, cut], ones], axis=1),
                    preferred_element_type=jnp.float32,
                )
                for weight, cut in zip(raised, cuts)
            ]
            for head, cut, peak, both in zip(chosen, cuts, peaks, sums):
                total = both[:, HEAD:]
                out_ref[0, :, cut] = (both[:, :HEAD] / total).astype(out_ref.dtype)
                stats = jnp.where(lane % heads == head, peak + jnp.log(total), stats)
        out_ref[0, :, row_width:] = pack_levels(stats, heads).astype(out_ref.dtype)


def attend(asked, tags, keys, values, width, chunk, part, size, place, places, shared):
    peers, span_len, _ = asked.shape
    length = keys.shape[1]
    heads = width // HEAD
    wide = width + LANES
    tag_at = tags.shape[2] // LANES - 1
    extra = [] if shared is None else [shared]
    return pl.pallas_call(
        functools.partial(attend_kernel, chunk),
        grid=(peers,),
        in_specs=[
            pl.BlockSpec((peers, ROW_TILE, LANES), lambda i: (0, 0, tag_at)),
            pl.BlockSpec((1, span_len, size), lambda i: (i, 0, part)),
            pl.BlockSpec(memory_space=pl.ANY),
            pl.BlockSpec(memory_space=pl.ANY),
        ]
        + [pl.BlockSpec(memory_space=pl.ANY)] * len(extra),
        out_specs=pl.BlockSpec((1, span_len, wide), lambda i: (i, 0, place)),
        scratch_shapes=[
            pltpu.VMEM((2, length, width), keys.dtype),
            pltpu.VMEM((2, length, width), keys.dtype),
            pltpu.SemaphoreType.DMA((2, 2)),
        ],
        out_shape=jax.ShapeDtypeStruct((peers, span_len, places * wide), asked.dtype),
        input_output_aliases={4: 0} if extra else {},
        compiler_params=pltpu.CompilerParams(vmem_limit_bytes=58 * MIB),
        cost_estimate=pl.CostEstimate(
            flops=4 * peers * heads * span_len * length * HEAD,
            bytes_accessed=2 * peers * width * (2 * span_len + 2 * length),
            transcendentals=peers * heads * span_len * length,
        ),
        name="attend_blocks",
    )(tags, asked, keys, values, *extra)


def merge_block(uses, parts):
    row_width = parts[0].shape[2] - LANES
    heads = row_width // HEAD

    def masked(use, held, other):
        return held if use is None else jnp.where(use, held, other)

    levels = [
        masked(use, unpack_levels(ref[0, :, row_width:], heads), -1e30)
        for use, ref in zip(uses, parts)
    ]
    highest = functools.reduce(jnp.maximum, levels)
    weights = [jnp.exp(level - highest) for level in levels]
    total = functools.reduce(jnp.add, weights)
    weights = [weight / total for weight in weights]
    for head in range(heads):
        cut = slice(head * HEAD, (head + 1) * HEAD)
        merged = functools.reduce(
            jnp.add,
            [
                weight[:, head : head + 1]
                * masked(use, ref[0, :, cut].astype(jnp.float32), 0.0)
                for use, weight, ref in zip(uses, weights, parts)
            ],
        )
        yield cut, merged
    lane = lax.broadcasted_iota(jnp.int32, highest.shape, 1)
    level = jnp.where(lane < heads, highest + jnp.log(total), 0.0)
    level = level + pltpu.roll(level, heads, 1) + pltpu.roll(level, 2 * heads, 1)
    yield slice(row_width, row_width + LANES), pack_levels(level, heads)


def merge_far_kernel(picked, index_ref, use_ref, *refs):
    block = pl.program_id(0)
    uses = [use_ref[block * picked + r] > 0 for r in range(picked)]
    out_ref = refs[-1]
    for cut, merged in merge_block(uses, refs[:-1]):
        out_ref[0, :, cut] = merged.astype(out_ref.dtype)


def merge_all_kernel(picked, earlier, index_ref, use_ref, *refs):
    parts = refs[: picked + 1]
    out_ref, first_ref, kept = refs[-3:]
    span_len = parts[0].shape[1]
    rows, row_width = out_ref.shape
    rows -= ROW_TILE
    step = pl.program_id(0)
    block = rows // span_len - 1 - step
    uses = [use_ref[block * picked + r] > 0 for r in range(picked)] + [None]
    start = pl.multiple_of(block * span_len, span_len)
    last = lax.broadcasted_iota(jnp.int32, (span_len, HEAD), 0) == span_len - 1
    at = first_ref.shape[1] - row_width

    @pl.when(step == 0)
    def _():
        kept[...] = jnp.zeros_like(kept)
        if earlier:
            first_ref[:, :at] = refs[picked + 1][...]

    for cut, merged in merge_block(uses, parts):
        if cut.start < row_width:
            moved = pltpu.roll(merged, span_len - 1, 0)
            moved = jnp.where(last, kept[0:1, cut], moved)
            out_ref[pl.ds(start, span_len), cut] = moved.astype(out_ref.dtype)
            kept[:, cut] = merged[:8]
            first = merged[:ROW_TILE].astype(out_ref.dtype)
            out_ref[rows:, cut] = first
            first_ref[:, at + cut.start : at + cut.stop] = first


def merge_far(parts, column, wide, index, use, blocks):
    span_len = parts.shape[1]
    picked = index.shape[0] // blocks
    specs = [
        pl.BlockSpec(
            (1, span_len, wide),
            functools.partial(lambda r, i, index, use: (index[i * picked + r], 0, column), r),
        )
        for r in range(picked)
    ]
    return pl.pallas_call(
        functools.partial(merge_far_kernel, picked),
        grid_spec=pltpu.PrefetchScalarGridSpec(
            num_scalar_prefetch=2,
            grid=(blocks,),
            in_specs=specs,
            out_specs=pl.BlockSpec((1, span_len, wide), lambda i, *_: (i, 0, 0)),
        ),
        out_shape=jax.ShapeDtypeStruct((blocks, span_len, wide), parts.dtype),
        compiler_params=pltpu.CompilerParams(vmem_limit_bytes=10 * MIB),
        name="merge_far",
    )(index, use, *([parts] * picked))


def merge_all(parts, column, wide, index, use, blocks, far, earlier=None):
    span_len = parts.shape[1]
    row_width = wide - LANES
    picked = index.shape[0] // blocks
    rows = blocks * span_len
    specs = [
        pl.BlockSpec(
            (1, span_len, wide),
            functools.partial(
                lambda r, i, index, use: (index[(blocks - 1 - i) * picked + r], 0, column), r
            ),
        )
        for r in range(picked)
    ]
    specs.append(pl.BlockSpec((1, span_len, wide), lambda i, *_: (blocks - 1 - i, 0, 0)))
    extra = [] if earlier is None else [earlier]
    first_width = row_width * (1 + len(extra))
    specs += [pl.BlockSpec((ROW_TILE, row_width), lambda i, *_: (0, 0))] * len(extra)
    return pl.pallas_call(
        functools.partial(merge_all_kernel, picked, len(extra)),
        grid_spec=pltpu.PrefetchScalarGridSpec(
            num_scalar_prefetch=2,
            grid=(blocks,),
            in_specs=specs,
            out_specs=[
                pl.BlockSpec((rows + ROW_TILE, row_width), lambda i, *_: (0, 0)),
                pl.BlockSpec((ROW_TILE, first_width), lambda i, *_: (0, 0)),
            ],
            scratch_shapes=[pltpu.VMEM((8, row_width), jnp.float32)],
        ),
        out_shape=[
            jax.ShapeDtypeStruct((rows + ROW_TILE, row_width), parts.dtype),
            jax.ShapeDtypeStruct((ROW_TILE, first_width), parts.dtype),
        ],
        compiler_params=pltpu.CompilerParams(vmem_limit_bytes=10 * MIB),
        name="merge_all",
    )(index, use, *([parts] * picked), far, *extra)


def project_kernel(starts, place_ref, stay_ref, *refs):
    sources, refs = refs[:PLANE], refs[PLANE:]
    last_part = len(starts) > PLANE
    belows, refs = (refs[:PLANE], refs[PLANE:]) if last_part else ([], refs)
    weights, before = refs[: len(starts)], refs[len(starts) : -7]
    keep_ref, send_ref, rows_ref, first_ref, held_ref, row_sems, weight_sems = refs[-7:]
    half = keep_ref.shape[0]
    part = half // PLANE
    _, width, tile = held_ref.shape

    def source_copies():
        for at, ref in enumerate(sources):
            member = place_ref[0] ^ at
            for side in range(2):
                to = pl.multiple_of(side * half + member * part, part)
                yield pltpu.make_async_copy(
                    ref.at[pl.ds(side * part, part)],
                    rows_ref.at[pl.ds(to, part)],
                    row_sems.at[at, side],
                )
            to = pl.multiple_of(member * ROW_TILE, ROW_TILE)
            yield pltpu.make_async_copy(
                ref.at[pl.ds(2 * part, ROW_TILE)],
                first_ref.at[pl.ds(to, ROW_TILE)],
                row_sems.at[at, 2],
            )

    def weight_copy(at):
        return pltpu.make_async_copy(
            weights[at].at[pl.ds(starts[at], width)], held_ref.at[at], weight_sems.at[at]
        )

    for copy in source_copies():
        copy.start()
    for at in range(len(starts)):
        weight_copy(at).start()
    for copy in source_copies():
        copy.wait()
    last = lax.broadcasted_iota(jnp.int32, (ROW_TILE, width), 0) == ROW_TILE - 1
    for member in range(PLANE):
        at = (member + 1) % PLANE * ROW_TILE
        below = first_ref[at : at + ROW_TILE].astype(jnp.float32)[0:1]
        if member == PLANE - 1:
            below = jnp.zeros_like(below)
            if last_part:
                under = functools.reduce(jnp.add, [ref[...].astype(jnp.float32) for ref in belows])
                below = under[0:1, width:]
        end = half + (member + 1) * part
        held = rows_ref[end - ROW_TILE : end].astype(jnp.float32)
        rows_ref[end - ROW_TILE : end] = jnp.where(last, below, held).astype(rows_ref.dtype)
    if last_part:
        under = under[:, :width].astype(rows_ref.dtype)
    stay = pl.multiple_of(stay_ref[0] * half, half)
    go = pl.multiple_of((1 - stay_ref[0]) * half, half)
    for shard in range(PLANE):
        weight_copy(shard).wait()
        if last_part:
            weight_copy(PLANE + shard).wait()
        cut = slice(shard * tile, (shard + 1) * tile)
        for at, (start, ref) in enumerate(((stay, keep_ref), (go, send_ref))):
            result = jnp.dot(
                rows_ref[pl.ds(start, half)], held_ref[shard], preferred_element_type=jnp.float32
            )
            if last_part:
                result = result + before[at][:, cut]
            ref[:, cut] = result.astype(ref.dtype)
        if last_part:
            row = jnp.dot(under, held_ref[PLANE + shard], preferred_element_type=jnp.float32)[0:1]
            at_end = lax.broadcasted_iota(jnp.int32, (ROW_TILE, tile), 0) == ROW_TILE - 1
            for upper, ref in ((stay_ref[0] > 0, keep_ref), (stay_ref[0] == 0, send_ref)):

                @pl.when(upper)
                def _():
                    held = ref[half - ROW_TILE :, cut].astype(jnp.float32)
                    ref[half - ROW_TILE :, cut] = jnp.where(at_end, held + row, held).astype(ref.dtype)


def project(sources, belows, weights, place, stay, before, kind):
    height, width = sources[0].shape
    rows = PLANE * (height - ROW_TILE)
    starts = [start for _, start in weights]
    tile = weights[0][0].shape[1]
    columns = PLANE * tile
    half = rows // 2
    half_spec = pl.BlockSpec((half, columns), lambda i, *_: (0, 0))
    return pl.pallas_call(
        functools.partial(project_kernel, starts),
        grid_spec=pltpu.PrefetchScalarGridSpec(
            num_scalar_prefetch=2,
            grid=(1,),
            in_specs=[pl.BlockSpec(memory_space=pl.ANY)] * PLANE
            + [pl.BlockSpec(row.shape, lambda i, *_: (0, 0)) for row in belows]
            + [pl.BlockSpec(memory_space=pl.ANY)] * len(starts)
            + [half_spec] * len(before),
            out_specs=[half_spec] * 2,
            scratch_shapes=[
                pltpu.VMEM((rows, width), sources[0].dtype),
                pltpu.VMEM((PLANE * ROW_TILE, width), sources[0].dtype),
                pltpu.VMEM((len(starts), width, tile), sources[0].dtype),
                pltpu.SemaphoreType.DMA((PLANE, 3)),
                pltpu.SemaphoreType.DMA((len(starts),)),
            ],
        ),
        out_shape=[jax.ShapeDtypeStruct((half, columns), kind)] * 2,
        compiler_params=pltpu.CompilerParams(vmem_limit_bytes=30 * MIB),
        cost_estimate=pl.CostEstimate(
            flops=2 * rows * width * columns,
            bytes_accessed=2 * width * (rows + columns) + 8 * rows * columns,
            transcendentals=0,
        ),
        name="project_rows",
    )(place, stay, *sources, *belows, *[weight for weight, _ in weights], *before)


def add_kernel(place_ref, keep_ref, other_ref, *outs):
    for at, ref in enumerate(outs):
        member = place_ref[0] ^ at
        ref[...] = (
            keep_ref[member].astype(jnp.float32) + other_ref[member].astype(jnp.float32)
        ).astype(ref.dtype)


def add_cores(keep, other, place):
    half, columns = keep.shape
    part = half // PLANE
    tile = min(columns, 512)
    folded = (PLANE, part, columns)
    return pl.pallas_call(
        add_kernel,
        grid_spec=pltpu.PrefetchScalarGridSpec(
            num_scalar_prefetch=1,
            grid=(columns // tile,),
            in_specs=[pl.BlockSpec((PLANE, part, tile), lambda i, *_: (0, 0, i))] * 2,
            out_specs=[pl.BlockSpec((part, tile), lambda i, *_: (0, i))] * PLANE,
        ),
        out_shape=[jax.ShapeDtypeStruct((part, columns), keep.dtype)] * PLANE,
        compiler_params=pltpu.CompilerParams(vmem_limit_bytes=10 * MIB),
        name="add_cores",
    )(place, keep.reshape(folded), other.reshape(folded))


def norm_kernel(strip, place_ref, line_ref, *refs):
    branches = refs[:-7]
    residual_ref, mask_ref, gain_ref, bias_ref, next_ref, normed_ref, branch_ref = refs[-7:]
    if len(branches) == 1:
        branch_ref[...] = branches[0][...].astype(jnp.float32)
    else:
        for at, ref in enumerate(branches):
            member = place_ref[0] ^ at
            for shard in range(ref.shape[1] // strip):
                to = pl.multiple_of((line_ref[shard] * PLANE + member) * strip, strip)
                branch_ref[:, pl.ds(to, strip)] = ref[
                    :, shard * strip : (shard + 1) * strip
                ].astype(jnp.float32)
    keep_scale = mask_ref[...].astype(jnp.float32) * (1.0 / keep_rate)
    stream = residual_ref[...].astype(jnp.float32) + keep_scale * branch_ref[...]
    centre = jnp.mean(stream, axis=1, keepdims=True)
    moved = stream - centre
    spread_of = jnp.mean(jnp.square(moved), axis=1, keepdims=True)
    normed = moved * lax.rsqrt(spread_of + norm_eps) * gain_ref[...] + bias_ref[...]
    next_ref[...] = stream.astype(next_ref.dtype)
    normed_ref[...] = normed.astype(normed_ref.dtype)


def add_norm(place, line, branches, strip, residual, drop_mask, gain, bias):
    rows, columns = residual.shape
    tile = min(32, rows)
    row_spec = pl.BlockSpec((tile, columns), lambda i, *_: (i, 0))
    branch_spec = pl.BlockSpec((tile, branches[0].shape[1]), lambda i, *_: (i, 0))
    flat_spec = pl.BlockSpec((1, columns), lambda i, *_: (0, 0))
    return pl.pallas_call(
        functools.partial(norm_kernel, strip),
        grid_spec=pltpu.PrefetchScalarGridSpec(
            num_scalar_prefetch=2,
            grid=(rows // tile,),
            in_specs=[branch_spec] * len(branches) + [row_spec, row_spec, flat_spec, flat_spec],
            out_specs=[row_spec, row_spec],
            scratch_shapes=[pltpu.VMEM((tile, columns), jnp.float32)],
        ),
        out_shape=[jax.ShapeDtypeStruct((rows, columns), residual.dtype)] * 2,
        compiler_params=pltpu.CompilerParams(vmem_limit_bytes=60 * MIB),
        name="add_norm",
    )(place, line, *branches, residual, drop_mask, gain[None], bias[None])


def pick_requests(owners, slots, peers, per_block):
    selector = owners[None, :] == peers[:, None]
    pair_block = jnp.arange(owners.shape[0], dtype=jnp.int32) // per_block
    return (
        jnp.sum(jnp.where(selector, pair_block[None, :], 0), axis=1),
        jnp.sum(jnp.where(selector, slots[None, :] + 1, 0), axis=1),
    )


def within(owners, base, half):
    index = owners - base
    use = (index >= 0) & (index < half)
    return jnp.where(use, index, 0), use.astype(jnp.int32)


def local(
    queries,
    neighbour_keys,
    neighbour_values,
    residual,
    out_weight,
    drop_mask,
    norm_gain,
    norm_bias,
    neighbour_owner,
    neighbour_slot,
):
    peer_count = lax.axis_size("dp")
    side_count = lax.axis_size("tensor")
    half = peer_count // 2
    halves = [list(range(half)), list(range(half, peer_count))]
    across = [(i, (i + half) % peer_count) for i in range(peer_count)]
    by_plane = side_count == 2 and peer_count == 4 * PLANE
    blocks, per_block = neighbour_owner.shape
    rows, row_width = queries.shape
    span_len = rows // blocks
    here = lax.axis_index("dp").astype(jnp.int32)
    upper = here // half
    base = upper * half
    partner = lax.rem(here + half, peer_count)

    def exchange(x):
        return lax.all_to_all(
            x, "dp", split_axis=0, concat_axis=0, tiled=True, axis_index_groups=halves
        )

    def swap(x, by):
        return lax.ppermute(x, "dp", [(i, i ^ by) for i in range(peer_count)])

    def pinned(*values):
        return lax.optimization_barrier(values)

    def to_partner(x):
        return lax.ppermute(x, "dp", across)

    chunks = 2
    width = row_width // chunks
    far_first = to_partner(queries[:, :width])
    middle = row_width // 2
    carried = shifted(queries[-1:], "dp", 1)
    owners = neighbour_owner.reshape(-1)
    slot_rows = neighbour_slot.reshape(-1)
    near_peers = base + jnp.arange(half, dtype=jnp.int32)
    near_out = spread(
        [queries], carried, *pick_requests(owners, slot_rows, near_peers, per_block),
        span_len, 0,
    )
    near_asked = exchange(near_out)
    far_carried = lax.ppermute(
        queries[-1:], "dp", [(i - 1, (i + half) % peer_count) for i in range(1, peer_count)]
    )
    requests = owners.shape[0]
    far_table = to_partner(
        jnp.pad(jnp.concatenate([owners, slot_rows]), (0, LANES - 2 * requests))[None, :]
    )
    far_first, far_carried, far_table, second, weight, _ = pinned(
        far_first, far_carried, far_table, queries[:, width:], out_weight, near_out
    )
    far_owners = far_table[0, :requests]
    far_picked = pick_requests(
        far_owners, far_table[0, requests : 2 * requests], near_peers, per_block
    )

    def answer(asked, tags, chunk, part, size, place, places, shared=None):
        return attend(
            asked, tags, neighbour_keys, neighbour_values, width, chunk, part, size,
            place, places, shared,
        )

    wide = width + LANES
    far_second = to_partner(second)
    near_index, near_use = within(owners, base, half)
    far_index, far_use = within(far_owners, base, half)
    far_out = spread([far_first], far_carried, *far_picked, span_len, 0)
    far_asked = exchange(far_out)
    near_asked, _ = pinned(near_asked, far_out)
    near_first = answer(near_asked, near_asked, 0, 0, width, 0, 2)
    near_second = answer(near_asked, near_asked, 1, 1, width, 1, 2)
    (
        far_asked, far_second, near_first, near_second, near_index, near_use, far_index,
        far_use, weight, *weight_halves,
    ) = pinned(
        far_asked, far_second, near_first, near_second, near_index, near_use, far_index,
        far_use, weight, weight[:middle], weight[middle:],
    )

    mixed = spread([far_second], far_carried, *far_picked, span_len, 1, near_first)
    next_asked = exchange(mixed)
    far_weight = [to_partner(weight_halves[0])] if by_plane else []
    tags, near_second, _ = pinned(far_asked, near_second, mixed)
    mixed = answer(tags, tags, 0, 0, wide, 0, 2, near_second)
    mixed, next_asked, weight_half, *far_weight = pinned(
        mixed, next_asked, weight_halves[1], *far_weight
    )

    far_back = exchange(mixed)
    if by_plane:
        far_weight.append(to_partner(weight_half))
    far_parts = answer(next_asked, tags, 1, 1, wide, 0, 1)
    far_back, far_parts, *far_weight = pinned(far_back, far_parts, *far_weight)
    near_back, next_back = next_asked, far_back

    far_merged = merge_far(far_back, 0, wide, far_index, far_use, blocks)
    far_home = to_partner(far_merged)
    far_back = exchange(far_parts)
    joined = jnp.concatenate([weight_halves[0], *far_weight[:1]], axis=0)
    far_home, far_back, joined, far_weight = pinned(far_home, far_back, joined, far_weight)

    def to_plane(moved):
        return [moved] + [swap(moved, by) for by in range(1, PLANE)] if by_plane else [moved]

    far_merged = merge_far(far_back, 0, wide, far_index, far_use, blocks)
    far_home, near_back, far_merged, joined, far_weight = pinned(
        far_home, near_back, far_merged, joined, far_weight
    )
    next_home = to_partner(far_merged)
    moved, first = merge_all(near_back, 0, wide, near_index, near_use, blocks, far_home)
    sources = to_plane(moved)
    swaps = [swap(joined, PLANE)] if by_plane else []
    count = len(sources)
    (next_home,) = pinned(next_home)
    next_home, next_back, weight_half, far_weight, *held = pinned(
        next_home, next_back, weight_halves[1], far_weight, *sources, *swaps
    )
    sources, held = held[:count], held[count:]
    moved, first = merge_all(
        next_back, 1, wide, near_index, near_use, blocks, next_home, first
    )
    if by_plane:
        place = lax.rem(here, PLANE).reshape(1)
        stay = lax.axis_index("tensor").astype(jnp.int32).reshape(1)
        moved, first, weight_half, far_half = pinned(moved, first, weight_half, far_weight[1])
        next_sources = to_plane(moved)
        near_next, far_next = swap(weight_half, PLANE), swap(far_half, PLANE)
        belows = [
            lax.ppermute(
                first, "dp", [(i + PLANE, i + at) for i in range(0, peer_count - PLANE, PLANE)]
            )
            for at in range(PLANE)
        ]
        first_weights = [(weight, 0), (held[0], 0), (far_weight[0], 0), (held[0], middle)]
        next_weights = [(weight, middle), (near_next, 0), (far_half, 0), (far_next, 0)]
        done = project(sources, [], first_weights, place, stay, [], jnp.float32)
        keep, send = project(
            next_sources, belows, next_weights + first_weights, place, stay, done, moved.dtype
        )
        line = jnp.stack(
            [here // PLANE, (here ^ PLANE) // PLANE, partner // PLANE, (partner ^ PLANE) // PLANE]
        )
        summed = add_cores(keep, lax.ppermute(send, "tensor", [(0, 1), (1, 0)]), place)
        branches = [summed[0]] + [swap(summed[by], by) for by in range(1, PLANE)]
    else:
        whole_weight = lax.all_gather(out_weight, "dp", axis=1, tiled=True)
        moved = jnp.concatenate([sources[0], moved], axis=1)
        below = shifted(first[:1], "dp", -1)
        cross_rows = jnp.concatenate([moved[: rows - 1], below], axis=0)
        branch = jnp.dot(cross_rows, whole_weight, preferred_element_type=jnp.float32)
        branches = [
            lax.psum_scatter(
                branch.astype(jnp.bfloat16), "tensor", scatter_dimension=0, tiled=True
            )
        ]
        place = line = jnp.zeros((1,), jnp.int32)
    return tuple(
        add_norm(
            place, line, branches, out_weight.shape[1], residual, drop_mask, norm_gain, norm_bias
        )
    )


def solution(mesh):
    placed = (
        P("dp", "tensor"),
        P("dp", None, "tensor"),
        P("dp", None, "tensor"),
        P(("dp", "tensor"), None),
        P("tensor", "dp"),
        P(("dp", "tensor"), None),
        P(),
        P(),
        P("dp", None),
        P("dp", None),
    )
    return jax.shard_map(
        local,
        mesh=mesh,
        in_specs=placed,
        out_specs=(P(("dp", "tensor"), None), P(("dp", "tensor"), None)),
        check_vma=False,
    )
```

```python
import functools

import jax
import jax.numpy as jnp
from jax import lax
from jax.experimental import pallas as pl
from jax.experimental.pallas import tpu as pltpu
from jax.sharding import PartitionSpec as P

HEAD = 128
LANES = 128
MIB = 1024 * 1024
ROW_TILE = 16
PLANE = 4

keep_rate = 0.9
norm_eps = 1e-05


def shifted(x, axis, by):
    count = lax.axis_size(axis)
    pairs = [(i, i + by) for i in range(count) if 0 <= i + by < count]
    return lax.ppermute(x, axis, pairs)


def spread_kernel(count, column, block_ref, slot_ref, carried_ref, *refs):
    pieces = refs[:count]
    out_ref, moved, tags, sems = refs[-4:]
    peers, span_len, _ = out_ref.shape
    rows, piece_width = pieces[0].shape
    row_width = moved.shape[1]
    at = 0
    for piece in pieces:
        for start in range(0, piece_width, 512):
            size = min(512, piece_width - start)
            held = piece[:, start : start + size].astype(jnp.float32)
            rolled = pltpu.roll(held, 1, 0)
            first = lax.broadcasted_iota(jnp.int32, (rows, size), 0) == 0
            above = carried_ref[0:1, at : at + size].astype(jnp.float32)
            moved[:, at : at + size] = jnp.where(first, above, rolled).astype(moved.dtype)
            at += size

    def copies(peer):
        start = pl.multiple_of(block_ref[peer] * span_len, span_len)
        yield pltpu.make_async_copy(
            moved.at[pl.ds(start, span_len)],
            out_ref.at[peer, :, pl.ds(column, row_width)],
            sems.at[0, peer],
        )
        yield pltpu.make_async_copy(
            tags.at[peer],
            out_ref.at[peer, :, pl.ds(column + row_width, LANES)],
            sems.at[1, peer],
        )

    for peer in range(peers):
        slot = slot_ref[peer].astype(jnp.float32)
        tags[peer] = jnp.full((span_len, LANES), slot, jnp.float32).astype(tags.dtype)
        for copy in copies(peer):
            copy.start()
    for peer in range(peers):
        for copy in copies(peer):
            copy.wait()


def spread(pieces, carried, block_of_peer, slot_of_peer, span_len, chunk, shared=None):
    peers = block_of_peer.shape[0]
    rows, piece_width = pieces[0].shape
    row_width = piece_width * len(pieces)
    wide = row_width + LANES
    whole = wide if shared is None else shared.shape[2]
    extra = [] if shared is None else [shared]
    return pl.pallas_call(
        functools.partial(spread_kernel, len(pieces), whole - wide),
        grid_spec=pltpu.PrefetchScalarGridSpec(
            num_scalar_prefetch=2,
            grid=(1,),
            in_specs=[pl.BlockSpec((1, row_width), lambda i, *_: (0, chunk))]
            + [pl.BlockSpec((rows, piece_width), lambda i, *_: (0, 0))] * len(pieces)
            + [pl.BlockSpec(memory_space=pl.ANY)] * len(extra),
            out_specs=pl.BlockSpec(memory_space=pl.ANY),
            scratch_shapes=[
                pltpu.VMEM((rows, row_width), carried.dtype),
                pltpu.VMEM((peers, span_len, LANES), carried.dtype),
                pltpu.SemaphoreType.DMA((2, peers)),
            ],
        ),
        out_shape=jax.ShapeDtypeStruct((peers, span_len, whole), carried.dtype),
        input_output_aliases={3 + len(pieces): 0} if extra else {},
        compiler_params=pltpu.CompilerParams(vmem_limit_bytes=(60 if extra else 10) * MIB),
        name="spread_queries",
    )(block_of_peer, slot_of_peer, carried, *pieces, *extra)


def pack_levels(stats, heads):
    part = lax.broadcasted_iota(jnp.int32, stats.shape, 1) // heads
    high = stats.astype(jnp.bfloat16).astype(jnp.float32)
    rest = stats - high
    middle = rest.astype(jnp.bfloat16).astype(jnp.float32)
    low = rest - middle
    return jnp.where(part == 0, high, jnp.where(part == 1, middle, jnp.where(part == 2, low, 0.0)))


def unpack_levels(packed, heads):
    packed = packed.astype(jnp.float32)
    return (
        packed
        + pltpu.roll(packed, LANES - heads, 1)
        + pltpu.roll(packed, LANES - 2 * heads, 1)
    )


def attend_kernel(chunk, tag_ref, query_ref, key_ref, value_ref, *refs):
    out_ref, key_held, value_held, sems = refs[-4:]
    span_len = query_ref.shape[1]
    _, length, row_width = key_held.shape
    heads = row_width // HEAD
    group = min(heads, 4)
    peer = pl.program_id(0)
    peers = pl.num_programs(0)

    def tag_of(at):
        return tag_ref[at, 0:1, 0:1].astype(jnp.float32)[0, 0].astype(jnp.int32)

    def copies(at):
        buffer = lax.rem(at, 2)
        slot = jnp.maximum(tag_of(at) - 1, 0)
        for kind, (ref, held) in enumerate(((key_ref, key_held), (value_ref, value_held))):
            yield pltpu.make_async_copy(
                ref.at[slot, :, pl.ds(chunk * row_width, row_width)],
                held.at[buffer],
                sems.at[kind, buffer],
            )

    def fetch(at):
        for copy in copies(at):
            copy.start()

    following = jnp.minimum(peer + 1, peers - 1)

    @pl.when((peer == 0) & (tag_of(0) > 0))
    def _():
        fetch(0)

    @pl.when((peer + 1 < peers) & (tag_of(following) > 0))
    def _():
        fetch(following)

    @pl.when(tag_of(peer) > 0)
    def _():
        for copy in copies(peer):
            copy.wait()
        buffer = lax.rem(peer, 2)
        lane = lax.broadcasted_iota(jnp.int32, (span_len, LANES), 1)
        stats = jnp.zeros((span_len, LANES), jnp.float32)
        ones = jnp.ones((length, HEAD), jnp.bfloat16)
        for first in range(0, heads, group):
            chosen = range(first, first + group)
            cuts = [slice(head * HEAD, (head + 1) * HEAD) for head in chosen]
            scores = [
                lax.dot_general(
                    query_ref[0, :, cut],
                    key_held[buffer, :, cut],
                    (((1,), (1,)), ((), ())),
                    preferred_element_type=jnp.float32,
                )
                * HEAD ** (-0.5)
                for cut in cuts
            ]
            peaks = [jnp.max(score, axis=1, keepdims=True) for score in scores]
            raised = [
                jnp.exp(score - peak).astype(jnp.bfloat16) for score, peak in zip(scores, peaks)
            ]
            sums = [
                jnp.dot(
                    weight,
                    jnp.concatenate([value_held[buffer, :, cut], ones], axis=1),
                    preferred_element_type=jnp.float32,
                )
                for weight, cut in zip(raised, cuts)
            ]
            for head, cut, peak, both in zip(chosen, cuts, peaks, sums):
                total = both[:, HEAD:]
                out_ref[0, :, cut] = (both[:, :HEAD] / total).astype(out_ref.dtype)
                stats = jnp.where(lane % heads == head, peak + jnp.log(total), stats)
        out_ref[0, :, row_width:] = pack_levels(stats, heads).astype(out_ref.dtype)


def attend(asked, tags, keys, values, width, chunk, part, size, place, places, shared):
    peers, span_len, _ = asked.shape
    length = keys.shape[1]
    heads = width // HEAD
    wide = width + LANES
    tag_at = tags.shape[2] // LANES - 1
    extra = [] if shared is None else [shared]
    return pl.pallas_call(
        functools.partial(attend_kernel, chunk),
        grid=(peers,),
        in_specs=[
            pl.BlockSpec((peers, ROW_TILE, LANES), lambda i: (0, 0, tag_at)),
            pl.BlockSpec((1, span_len, size), lambda i: (i, 0, part)),
            pl.BlockSpec(memory_space=pl.ANY),
            pl.BlockSpec(memory_space=pl.ANY),
        ]
        + [pl.BlockSpec(memory_space=pl.ANY)] * len(extra),
        out_specs=pl.BlockSpec((1, span_len, wide), lambda i: (i, 0, place)),
        scratch_shapes=[
            pltpu.VMEM((2, length, width), keys.dtype),
            pltpu.VMEM((2, length, width), keys.dtype),
            pltpu.SemaphoreType.DMA((2, 2)),
        ],
        out_shape=jax.ShapeDtypeStruct((peers, span_len, places * wide), asked.dtype),
        input_output_aliases={4: 0} if extra else {},
        compiler_params=pltpu.CompilerParams(vmem_limit_bytes=54 * MIB),
        cost_estimate=pl.CostEstimate(
            flops=4 * peers * heads * span_len * length * HEAD,
            bytes_accessed=2 * peers * width * (2 * span_len + 2 * length),
            transcendentals=peers * heads * span_len * length,
        ),
        name="attend_blocks",
    )(tags, asked, keys, values, *extra)


def merge_block(uses, parts):
    row_width = parts[0].shape[2] - LANES
    heads = row_width // HEAD

    def masked(use, held, other):
        return held if use is None else jnp.where(use, held, other)

    levels = [
        masked(use, unpack_levels(ref[0, :, row_width:], heads), -1e30)
        for use, ref in zip(uses, parts)
    ]
    highest = functools.reduce(jnp.maximum, levels)
    weights = [jnp.exp(level - highest) for level in levels]
    total = functools.reduce(jnp.add, weights)
    weights = [weight / total for weight in weights]
    for head in range(heads):
        cut = slice(head * HEAD, (head + 1) * HEAD)
        merged = functools.reduce(
            jnp.add,
            [
                weight[:, head : head + 1]
                * masked(use, ref[0, :, cut].astype(jnp.float32), 0.0)
                for use, weight, ref in zip(uses, weights, parts)
            ],
        )
        yield cut, merged
    lane = lax.broadcasted_iota(jnp.int32, highest.shape, 1)
    level = jnp.where(lane < heads, highest + jnp.log(total), 0.0)
    level = level + pltpu.roll(level, heads, 1) + pltpu.roll(level, 2 * heads, 1)
    yield slice(row_width, row_width + LANES), pack_levels(level, heads)


def merge_far_kernel(picked, index_ref, use_ref, *refs):
    block = pl.program_id(0)
    uses = [use_ref[block * picked + r] > 0 for r in range(picked)]
    out_ref = refs[-1]
    for cut, merged in merge_block(uses, refs[:-1]):
        out_ref[0, :, cut] = merged.astype(out_ref.dtype)


def merge_all_kernel(picked, earlier, index_ref, use_ref, *refs):
    parts = refs[: picked + 1]
    out_ref, first_ref, kept = refs[-3:]
    span_len = parts[0].shape[1]
    rows, row_width = out_ref.shape
    rows -= ROW_TILE
    step = pl.program_id(0)
    block = rows // span_len - 1 - step
    uses = [use_ref[block * picked + r] > 0 for r in range(picked)] + [None]
    start = pl.multiple_of(block * span_len, span_len)
    last = lax.broadcasted_iota(jnp.int32, (span_len, HEAD), 0) == span_len - 1
    at = first_ref.shape[1] - row_width

    @pl.when(step == 0)
    def _():
        kept[...] = jnp.zeros_like(kept)
        if earlier:
            first_ref[:, :at] = refs[picked + 1][...]

    for cut, merged in merge_block(uses, parts):
        if cut.start < row_width:
            moved = pltpu.roll(merged, span_len - 1, 0)
            moved = jnp.where(last, kept[0:1, cut], moved)
            out_ref[pl.ds(start, span_len), cut] = moved.astype(out_ref.dtype)
            kept[:, cut] = merged[:8]
            first = merged[:ROW_TILE].astype(out_ref.dtype)
            out_ref[rows:, cut] = first
            first_ref[:, at + cut.start : at + cut.stop] = first


def merge_far(parts, column, wide, index, use, blocks):
    span_len = parts.shape[1]
    picked = index.shape[0] // blocks
    specs = [
        pl.BlockSpec(
            (1, span_len, wide),
            functools.partial(lambda r, i, index, use: (index[i * picked + r], 0, column), r),
        )
        for r in range(picked)
    ]
    return pl.pallas_call(
        functools.partial(merge_far_kernel, picked),
        grid_spec=pltpu.PrefetchScalarGridSpec(
            num_scalar_prefetch=2,
            grid=(blocks,),
            in_specs=specs,
            out_specs=pl.BlockSpec((1, span_len, wide), lambda i, *_: (i, 0, 0)),
        ),
        out_shape=jax.ShapeDtypeStruct((blocks, span_len, wide), parts.dtype),
        compiler_params=pltpu.CompilerParams(vmem_limit_bytes=10 * MIB),
        name="merge_far",
    )(index, use, *([parts] * picked))


def merge_all(parts, column, wide, index, use, blocks, far, earlier=None):
    span_len = parts.shape[1]
    row_width = wide - LANES
    picked = index.shape[0] // blocks
    rows = blocks * span_len
    specs = [
        pl.BlockSpec(
            (1, span_len, wide),
            functools.partial(
                lambda r, i, index, use: (index[(blocks - 1 - i) * picked + r], 0, column), r
            ),
        )
        for r in range(picked)
    ]
    specs.append(pl.BlockSpec((1, span_len, wide), lambda i, *_: (blocks - 1 - i, 0, 0)))
    extra = [] if earlier is None else [earlier]
    first_width = row_width * (1 + len(extra))
    specs += [pl.BlockSpec((ROW_TILE, row_width), lambda i, *_: (0, 0))] * len(extra)
    return pl.pallas_call(
        functools.partial(merge_all_kernel, picked, len(extra)),
        grid_spec=pltpu.PrefetchScalarGridSpec(
            num_scalar_prefetch=2,
            grid=(blocks,),
            in_specs=specs,
            out_specs=[
                pl.BlockSpec((rows + ROW_TILE, row_width), lambda i, *_: (0, 0)),
                pl.BlockSpec((ROW_TILE, first_width), lambda i, *_: (0, 0)),
            ],
            scratch_shapes=[pltpu.VMEM((8, row_width), jnp.float32)],
        ),
        out_shape=[
            jax.ShapeDtypeStruct((rows + ROW_TILE, row_width), parts.dtype),
            jax.ShapeDtypeStruct((ROW_TILE, first_width), parts.dtype),
        ],
        compiler_params=pltpu.CompilerParams(vmem_limit_bytes=10 * MIB),
        name="merge_all",
    )(index, use, *([parts] * picked), far, *extra)


def project_kernel(starts, place_ref, stay_ref, *refs):
    sources, refs = refs[:PLANE], refs[PLANE:]
    last_part = len(starts) > PLANE
    belows, refs = (refs[:PLANE], refs[PLANE:]) if last_part else ([], refs)
    weights, before = refs[: len(starts)], refs[len(starts) : -7]
    keep_ref, send_ref, rows_ref, first_ref, held_ref, row_sems, weight_sems = refs[-7:]
    half = keep_ref.shape[0]
    part = half // PLANE
    _, width, tile = held_ref.shape

    def source_copies():
        for at, ref in enumerate(sources):
            member = place_ref[0] ^ at
            for side in range(2):
                to = pl.multiple_of(side * half + member * part, part)
                yield pltpu.make_async_copy(
                    ref.at[pl.ds(side * part, part)],
                    rows_ref.at[pl.ds(to, part)],
                    row_sems.at[at, side],
                )
            to = pl.multiple_of(member * ROW_TILE, ROW_TILE)
            yield pltpu.make_async_copy(
                ref.at[pl.ds(2 * part, ROW_TILE)],
                first_ref.at[pl.ds(to, ROW_TILE)],
                row_sems.at[at, 2],
            )

    def weight_copy(at):
        return pltpu.make_async_copy(
            weights[at].at[pl.ds(starts[at], width)], held_ref.at[at], weight_sems.at[at]
        )

    for copy in source_copies():
        copy.start()
    for at in range(len(starts)):
        weight_copy(at).start()
    for copy in source_copies():
        copy.wait()
    last = lax.broadcasted_iota(jnp.int32, (ROW_TILE, width), 0) == ROW_TILE - 1
    for member in range(PLANE):
        at = (member + 1) % PLANE * ROW_TILE
        below = first_ref[at : at + ROW_TILE].astype(jnp.float32)[0:1]
        if member == PLANE - 1:
            below = jnp.zeros_like(below)
        end = half + (member + 1) * part
        held = rows_ref[end - ROW_TILE : end].astype(jnp.float32)
        rows_ref[end - ROW_TILE : end] = jnp.where(last, below, held).astype(rows_ref.dtype)
    if last_part:
        below = functools.reduce(jnp.add, [ref[...].astype(jnp.float32) for ref in belows])
        below = below.astype(rows_ref.dtype)
    stay = pl.multiple_of(stay_ref[0] * half, half)
    go = pl.multiple_of((1 - stay_ref[0]) * half, half)
    for shard in range(PLANE):
        weight_copy(shard).wait()
        if last_part:
            weight_copy(PLANE + shard).wait()
        cut = slice(shard * tile, (shard + 1) * tile)
        for at, (start, ref) in enumerate(((stay, keep_ref), (go, send_ref))):
            result = jnp.dot(
                rows_ref[pl.ds(start, half)], held_ref[shard], preferred_element_type=jnp.float32
            )
            if last_part:
                result = result + before[at][:, cut]
            ref[:, cut] = result.astype(ref.dtype)
        if last_part:
            row = functools.reduce(
                jnp.add,
                [
                    jnp.dot(
                        below[:, side * width : (side + 1) * width],
                        held_ref[at],
                        preferred_element_type=jnp.float32,
                    )
                    for side, at in ((0, PLANE + shard), (1, shard))
                ],
            )[0:1]
            at_end = lax.broadcasted_iota(jnp.int32, (ROW_TILE, tile), 0) == ROW_TILE - 1
            for upper, ref in ((stay_ref[0] > 0, keep_ref), (stay_ref[0] == 0, send_ref)):

                @pl.when(upper)
                def _():
                    held = ref[half - ROW_TILE :, cut].astype(jnp.float32)
                    ref[half - ROW_TILE :, cut] = jnp.where(at_end, row, held).astype(ref.dtype)


def project(sources, belows, weights, place, stay, before, kind):
    height, width = sources[0].shape
    rows = PLANE * (height - ROW_TILE)
    starts = [start for _, start in weights]
    tile = weights[0][0].shape[1]
    columns = PLANE * tile
    half = rows // 2
    half_spec = pl.BlockSpec((half, columns), lambda i, *_: (0, 0))
    return pl.pallas_call(
        functools.partial(project_kernel, starts),
        grid_spec=pltpu.PrefetchScalarGridSpec(
            num_scalar_prefetch=2,
            grid=(1,),
            in_specs=[pl.BlockSpec(memory_space=pl.ANY)] * PLANE
            + [pl.BlockSpec(row.shape, lambda i, *_: (0, 0)) for row in belows]
            + [pl.BlockSpec(memory_space=pl.ANY)] * len(starts)
            + [half_spec] * len(before),
            out_specs=[half_spec] * 2,
            scratch_shapes=[
                pltpu.VMEM((rows, width), sources[0].dtype),
                pltpu.VMEM((PLANE * ROW_TILE, width), sources[0].dtype),
                pltpu.VMEM((len(starts), width, tile), sources[0].dtype),
                pltpu.SemaphoreType.DMA((PLANE, 3)),
                pltpu.SemaphoreType.DMA((len(starts),)),
            ],
        ),
        out_shape=[jax.ShapeDtypeStruct((half, columns), kind)] * 2,
        compiler_params=pltpu.CompilerParams(vmem_limit_bytes=30 * MIB),
        cost_estimate=pl.CostEstimate(
            flops=2 * rows * width * columns,
            bytes_accessed=2 * width * (rows + columns) + 8 * rows * columns,
            transcendentals=0,
        ),
        name="project_rows",
    )(place, stay, *sources, *belows, *[weight for weight, _ in weights], *before)


def add_kernel(place_ref, keep_ref, other_ref, *outs):
    for at, ref in enumerate(outs):
        member = place_ref[0] ^ at
        ref[...] = (
            keep_ref[member].astype(jnp.float32) + other_ref[member].astype(jnp.float32)
        ).astype(ref.dtype)


def add_cores(keep, other, place):
    half, columns = keep.shape
    part = half // PLANE
    tile = min(columns, 512)
    folded = (PLANE, part, columns)
    return pl.pallas_call(
        add_kernel,
        grid_spec=pltpu.PrefetchScalarGridSpec(
            num_scalar_prefetch=1,
            grid=(columns // tile,),
            in_specs=[pl.BlockSpec((PLANE, part, tile), lambda i, *_: (0, 0, i))] * 2,
            out_specs=[pl.BlockSpec((part, tile), lambda i, *_: (0, i))] * PLANE,
        ),
        out_shape=[jax.ShapeDtypeStruct((part, columns), keep.dtype)] * PLANE,
        compiler_params=pltpu.CompilerParams(vmem_limit_bytes=10 * MIB),
        name="add_cores",
    )(place, keep.reshape(folded), other.reshape(folded))


def norm_kernel(strip, place_ref, line_ref, *refs):
    branches = refs[:-7]
    residual_ref, mask_ref, gain_ref, bias_ref, next_ref, normed_ref, branch_ref = refs[-7:]
    if len(branches) == 1:
        branch_ref[...] = branches[0][...].astype(jnp.float32)
    else:
        for at, ref in enumerate(branches):
            member = place_ref[0] ^ at
            for shard in range(ref.shape[1] // strip):
                to = pl.multiple_of((line_ref[shard] * PLANE + member) * strip, strip)
                branch_ref[:, pl.ds(to, strip)] = ref[
                    :, shard * strip : (shard + 1) * strip
                ].astype(jnp.float32)
    keep_scale = mask_ref[...].astype(jnp.float32) * (1.0 / keep_rate)
    stream = residual_ref[...].astype(jnp.float32) + keep_scale * branch_ref[...]
    centre = jnp.mean(stream, axis=1, keepdims=True)
    moved = stream - centre
    spread_of = jnp.mean(jnp.square(moved), axis=1, keepdims=True)
    normed = moved * lax.rsqrt(spread_of + norm_eps) * gain_ref[...] + bias_ref[...]
    next_ref[...] = stream.astype(next_ref.dtype)
    normed_ref[...] = normed.astype(normed_ref.dtype)


def add_norm(place, line, branches, strip, residual, drop_mask, gain, bias):
    rows, columns = residual.shape
    tile = min(32, rows)
    row_spec = pl.BlockSpec((tile, columns), lambda i, *_: (i, 0))
    branch_spec = pl.BlockSpec((tile, branches[0].shape[1]), lambda i, *_: (i, 0))
    flat_spec = pl.BlockSpec((1, columns), lambda i, *_: (0, 0))
    return pl.pallas_call(
        functools.partial(norm_kernel, strip),
        grid_spec=pltpu.PrefetchScalarGridSpec(
            num_scalar_prefetch=2,
            grid=(rows // tile,),
            in_specs=[branch_spec] * len(branches) + [row_spec, row_spec, flat_spec, flat_spec],
            out_specs=[row_spec, row_spec],
            scratch_shapes=[pltpu.VMEM((tile, columns), jnp.float32)],
        ),
        out_shape=[jax.ShapeDtypeStruct((rows, columns), residual.dtype)] * 2,
        compiler_params=pltpu.CompilerParams(vmem_limit_bytes=20 * MIB),
        name="add_norm",
    )(place, line, *branches, residual, drop_mask, gain[None], bias[None])


def pick_requests(owners, slots, peers, per_block):
    selector = owners[None, :] == peers[:, None]
    pair_block = jnp.arange(owners.shape[0], dtype=jnp.int32) // per_block
    return (
        jnp.sum(jnp.where(selector, pair_block[None, :], 0), axis=1),
        jnp.sum(jnp.where(selector, slots[None, :] + 1, 0), axis=1),
    )


def within(owners, base, half):
    index = owners - base
    use = (index >= 0) & (index < half)
    return jnp.where(use, index, 0), use.astype(jnp.int32)


def local(
    queries,
    neighbour_keys,
    neighbour_values,
    residual,
    out_weight,
    drop_mask,
    norm_gain,
    norm_bias,
    neighbour_owner,
    neighbour_slot,
):
    peer_count = lax.axis_size("dp")
    side_count = lax.axis_size("tensor")
    half = peer_count // 2
    halves = [list(range(half)), list(range(half, peer_count))]
    across = [(i, (i + half) % peer_count) for i in range(peer_count)]
    by_plane = side_count == 2 and peer_count == 4 * PLANE
    blocks, per_block = neighbour_owner.shape
    rows, row_width = queries.shape
    span_len = rows // blocks
    here = lax.axis_index("dp").astype(jnp.int32)
    upper = here // half
    base = upper * half
    partner = lax.rem(here + half, peer_count)

    def exchange(x):
        return lax.all_to_all(
            x, "dp", split_axis=0, concat_axis=0, tiled=True, axis_index_groups=halves
        )

    def swap(x, by):
        return lax.ppermute(x, "dp", [(i, i ^ by) for i in range(peer_count)])

    def pinned(*values):
        return lax.optimization_barrier(values)

    def to_partner(x):
        return lax.ppermute(x, "dp", across)

    chunks = 2
    width = row_width // chunks
    far_first = to_partner(queries[:, :width])
    middle = row_width // 2
    carried = shifted(queries[-1:], "dp", 1)
    owners = neighbour_owner.reshape(-1)
    slot_rows = neighbour_slot.reshape(-1)
    near_peers = base + jnp.arange(half, dtype=jnp.int32)
    near_out = spread(
        [queries], carried, *pick_requests(owners, slot_rows, near_peers, per_block),
        span_len, 0,
    )
    near_asked = exchange(near_out)
    far_carried = lax.ppermute(
        queries[-1:], "dp", [(i - 1, (i + half) % peer_count) for i in range(1, peer_count)]
    )
    requests = owners.shape[0]
    far_table = to_partner(
        jnp.pad(jnp.concatenate([owners, slot_rows]), (0, LANES - 2 * requests))[None, :]
    )
    far_first, far_carried, far_table, second, weight, _ = pinned(
        far_first, far_carried, far_table, queries[:, width:], out_weight, near_out
    )
    far_owners = far_table[0, :requests]
    far_picked = pick_requests(
        far_owners, far_table[0, requests : 2 * requests], near_peers, per_block
    )

    def answer(asked, tags, chunk, part, size, place, places, shared=None):
        return attend(
            asked, tags, neighbour_keys, neighbour_values, width, chunk, part, size,
            place, places, shared,
        )

    wide = width + LANES
    far_second = to_partner(second)
    near_index, near_use = within(owners, base, half)
    far_index, far_use = within(far_owners, base, half)
    far_out = spread([far_first], far_carried, *far_picked, span_len, 0)
    far_asked = exchange(far_out)
    near_asked, _ = pinned(near_asked, far_out)
    near_first = answer(near_asked, near_asked, 0, 0, width, 0, 2)
    near_second = answer(near_asked, near_asked, 1, 1, width, 1, 2)
    (
        far_asked, far_second, near_first, near_second, near_index, near_use, far_index,
        far_use, weight, *weight_halves,
    ) = pinned(
        far_asked, far_second, near_first, near_second, near_index, near_use, far_index,
        far_use, weight, weight[:middle], weight[middle:],
    )

    mixed = spread([far_second], far_carried, *far_picked, span_len, 1, near_first)
    next_asked = exchange(mixed)
    far_weight = [to_partner(weight_halves[0])] if by_plane else []
    tags, near_second, _ = pinned(far_asked, near_second, mixed)
    mixed = answer(tags, tags, 0, 0, wide, 0, 2, near_second)
    mixed, next_asked, weight_half, *far_weight = pinned(
        mixed, next_asked, weight_halves[1], *far_weight
    )

    far_back = exchange(mixed)
    if by_plane:
        far_weight.append(to_partner(weight_half))
    far_parts = answer(next_asked, tags, 1, 1, wide, 0, 1)
    far_back, far_parts, *far_weight = pinned(far_back, far_parts, *far_weight)
    near_back, next_back = next_asked, far_back

    far_merged = merge_far(far_back, 0, wide, far_index, far_use, blocks)
    far_home = to_partner(far_merged)
    far_back = exchange(far_parts)
    joined = jnp.concatenate([weight_halves[0], *far_weight[:1]], axis=0)
    far_home, far_back, joined, far_weight = pinned(far_home, far_back, joined, far_weight)

    def to_plane(moved):
        return [moved] + [swap(moved, by) for by in range(1, PLANE)] if by_plane else [moved]

    far_merged = merge_far(far_back, 0, wide, far_index, far_use, blocks)
    far_home, near_back, far_merged, joined, far_weight = pinned(
        far_home, near_back, far_merged, joined, far_weight
    )
    next_home = to_partner(far_merged)
    moved, first = merge_all(near_back, 0, wide, near_index, near_use, blocks, far_home)
    sources = to_plane(moved)
    swaps = [swap(joined, PLANE)] if by_plane else []
    count = len(sources)
    (next_home,) = pinned(next_home)
    next_home, next_back, weight_half, far_weight, *held = pinned(
        next_home, next_back, weight_halves[1], far_weight, *sources, *swaps
    )
    sources, held = held[:count], held[count:]
    moved, first = merge_all(
        next_back, 1, wide, near_index, near_use, blocks, next_home, first
    )
    if by_plane:
        place = lax.rem(here, PLANE).reshape(1)
        stay = lax.axis_index("tensor").astype(jnp.int32).reshape(1)
        moved, first, weight_half, far_half = pinned(moved, first, weight_half, far_weight[1])
        next_sources = to_plane(moved)
        near_next, far_next = swap(weight_half, PLANE), swap(far_half, PLANE)
        belows = [
            lax.ppermute(
                first, "dp", [(i + PLANE, i + at) for i in range(0, peer_count - PLANE, PLANE)]
            )
            for at in range(PLANE)
        ]
        first_weights = [(weight, 0), (held[0], 0), (far_weight[0], 0), (held[0], middle)]
        next_weights = [(weight, middle), (near_next, 0), (far_half, 0), (far_next, 0)]
        done = project(sources, [], first_weights, place, stay, [], jnp.float32)
        keep, send = project(
            next_sources, belows, next_weights + first_weights, place, stay, done, moved.dtype
        )
        line = jnp.stack(
            [here // PLANE, (here ^ PLANE) // PLANE, partner // PLANE, (partner ^ PLANE) // PLANE]
        )
        summed = add_cores(keep, lax.ppermute(send, "tensor", [(0, 1), (1, 0)]), place)
        branches = [summed[0]] + [swap(summed[by], by) for by in range(1, PLANE)]
    else:
        whole_weight = lax.all_gather(out_weight, "dp", axis=1, tiled=True)
        moved = jnp.concatenate([sources[0], moved], axis=1)
        below = shifted(first[:1], "dp", -1)
        cross_rows = jnp.concatenate([moved[: rows - 1], below], axis=0)
        branch = jnp.dot(cross_rows, whole_weight, preferred_element_type=jnp.float32)
        branches = [
            lax.psum_scatter(
                branch.astype(jnp.bfloat16), "tensor", scatter_dimension=0, tiled=True
            )
        ]
        place = line = jnp.zeros((1,), jnp.int32)
    return tuple(
        add_norm(
            place, line, branches, out_weight.shape[1], residual, drop_mask, norm_gain, norm_bias
        )
    )


def solution(mesh):
    placed = (
        P("dp", "tensor"),
        P("dp", None, "tensor"),
        P("dp", None, "tensor"),
        P(("dp", "tensor"), None),
        P("tensor", "dp"),
        P(("dp", "tensor"), None),
        P(),
        P(),
        P("dp", None),
        P("dp", None),
    )
    return jax.shard_map(
        local,
        mesh=mesh,
        in_specs=placed,
        out_specs=(P(("dp", "tensor"), None), P(("dp", "tensor"), None)),
        check_vma=False,
    )
```
